32 devices in a mesh: section: 4 (over y, x), frame: 4 (over z), chan: 2 (over core).
Axes of the slice: x: 2, y: 2, z: 4, core: 2. Of those that a mesh axis runs over, the one named last changes fastest.
Arguments:
- upstream: bfloat16 [512, 8, 4, 128], P('chan', None, 'frame'), may hold values from -6 to 6
- acts: bfloat16 [4, 512, 8, 4, 128], P('section', None, None, 'frame'), may hold values from -6 to 6
- weights: bfloat16 [4, 27, 512, 512], P('section', None, 'chan'), may hold values from -0.0625 to 0.0625
Outputs:
- grads: bfloat16 [4, 512, 8, 4, 128], P('section', 'chan', None, 'frame')
- weight_grads: bfloat16 [4, 27, 512, 512], P('section', None, 'chan')
The draws below stay inside these ranges and needn't reach their ends.
All inputs are finite; a program needn't handle non-finite values.
Results may differ from the reference program's by a relative error of at most 0.03.
Values may be sent and summed in bfloat16 or wider, within the bound.
No kernel may reach another device: no remote copies, remote signals or barrier semaphores. Data moves between devices by JAX's collectives and lax.ppermute only.
A program may use at most 128 MiB of HBM per device.

```python
import jax
import jax.numpy as jnp

C = 512
WIDTH = 128
LAYERS = 4
FRAMES = 8
ROWS = 4
N_SECTION = 4


def strengthened(entries, key, source, target, blocks, factor):
    def block_of(dim):
        return (jnp.arange(entries.shape[dim]) // (entries.shape[dim] // blocks)).reshape((-1,) + (1,) * (entries.ndim - 1 - dim))

    first = jax.random.permutation(key, blocks)[block_of(target)]
    second = (block_of(target) + blocks // 2) % blocks
    return jnp.where((block_of(source) == first) | (block_of(source) == second), factor * entries, entries)


def steps_of(stream_key, shape, cuts, low, top_value):
    def one(position, blocks):
        draws = jax.random.uniform(jax.random.fold_in(jax.random.fold_in(stream_key, 6), position), (blocks,), jnp.float32, low / len(cuts), top_value / len(cuts))
        return jnp.repeat(jnp.exp(draws), shape[position] // blocks).reshape((-1,) + (1,) * (len(shape) - position - 1))

    loudness = one(*cuts[0])
    for cut in cuts[1:]:
        loudness = loudness * one(*cut)
    return loudness


def gaussian(stream_key, dims, scale, reach, split=(), held_as=jnp.bfloat16):
    entries = scale * jax.random.normal(stream_key, dims, jnp.float32)
    if split:
        entries = entries * steps_of(stream_key, dims, split, -0.22, 0.18)
    return jnp.clip(entries, -reach, reach).astype(held_as)


def noise_with(key, dims, scale, bound, cuts, heavy, held_as=jnp.bfloat16):
    entries = scale * jax.random.normal(key, dims, jnp.float32)
    if cuts:
        entries = entries * steps_of(key, dims, cuts, -0.22, 0.18)
    return jnp.clip(strengthened(entries, jax.random.fold_in(key, 3), *heavy), -bound, bound).astype(held_as)


def setup_inputs(seed: int = 0) -> dict:
    key_of = jax.random.split(jax.random.key(seed), 4)
    return {
        "upstream": gaussian(key_of[0], (C, FRAMES, ROWS, WIDTH), 1.0, 6.0, ((0, 2), (2, 4))),
        "acts": gaussian(key_of[1], (LAYERS, C, FRAMES, ROWS, WIDTH), 1.0, 6.0, ((0, 4), (3, 4))),
        "weights": noise_with(key_of[2], (LAYERS, 27, C, C), (27 * C) ** -0.5, 0.0625, ((0, 4), (2, 2)), (2, 3, 2, 2.0)),
    }


def shifted_list(gradient):
    frames_n, rows_n, width_n = gradient.shape[1], gradient.shape[2], gradient.shape[3]
    padded = jnp.pad(gradient, ((0, 0), (0, 2), (1, 1), (1, 1)))
    pieces = []
    for t_lag in range(3):
        for r_off in (-1, 0, 1):
            for w_off in (-1, 0, 1):
                pieces.append(padded[:, t_lag:t_lag + frames_n, 1 - r_off:1 - r_off + rows_n, 1 - w_off:1 - w_off + width_n])
    return pieces


def reference(upstream, acts, weights):
    gradient = upstream
    results = []
    kernels = []
    for layer_index in range(N_SECTION):
        stored = acts[layer_index].astype(jnp.float32)
        logistic = jax.nn.sigmoid(stored)
        slopes = logistic * (1.0 + stored * (1.0 - logistic))
        features = (stored * logistic).astype(jnp.bfloat16).reshape(C, -1)
        transposed = jnp.zeros((C, features.shape[1]), jnp.float32)
        tap_grads = []
        for tap_index, shifted in enumerate(shifted_list(gradient)):
            flat = shifted.reshape(C, -1)
            transposed = transposed + jnp.dot(weights[layer_index, tap_index].T, flat, preferred_element_type=jnp.float32)
            tap_grads.append(jnp.dot(flat, features.T, preferred_element_type=jnp.float32))
        gradient = (gradient.astype(jnp.float32) + slopes * transposed.reshape(gradient.shape)).astype(jnp.bfloat16)
        results.append(gradient)
        kernels.append(jnp.stack(tap_grads).astype(jnp.bfloat16))
    return jnp.stack(results), jnp.stack(kernels)
```

```python
import jax
import jax.numpy as jnp
from jax import lax
from jax.experimental import pallas as pl
from jax.experimental.pallas import tpu as pltpu
from jax.sharding import PartitionSpec as P

BLOCK_FRAMES = 2
F32 = jnp.float32
BF16 = jnp.bfloat16


def back_kernel(cur_ref, later_ref, w_ref, out_ref, spread, acc):
    step = pl.program_id(0)
    frames_n, rows_n, width_n, group = cur_ref.shape

    @pl.when(step == 0)
    def _():
        acc[...] = jnp.zeros_like(acc)
        empty = jnp.zeros((width_n, 3 * group), F32)
        for frame in range(2 * frames_n):
            spread[frame, 0] = empty
            spread[frame, rows_n + 1] = empty
            for row in range(rows_n):
                source = cur_ref[frame, row] if frame < frames_n else later_ref[frame - frames_n, row]
                cells = source.astype(F32)
                spread[frame, row + 1, :, 0:group] = pltpu.roll(cells, width_n - 1, 0)
                spread[frame, row + 1, :, group : 2 * group] = cells
                spread[frame, row + 1, :, 2 * group : 3 * group] = pltpu.roll(cells, 1, 0)

    lag = step // 3
    offset = 2 - step % 3
    taken = spread[pl.ds(lag, frames_n), pl.ds(offset, rows_n)]
    taken = taken.reshape(frames_n * rows_n * width_n, 3 * group).astype(BF16)
    acc[...] += jnp.dot(taken, w_ref[...].reshape(3 * group, -1), preferred_element_type=F32)

    @pl.when(step == pl.num_programs(0) - 1)
    def _():
        out_ref[...] = acc[...].astype(BF16)


def back_block(current, later, kernels):
    frames_n, rows_n, width_n, group = current.shape
    channels = kernels.shape[2]
    cells = frames_n * rows_n * width_n
    whole = pl.BlockSpec(current.shape, lambda step: (0, 0, 0, 0))
    return pl.pallas_call(
        back_kernel,
        grid=(9,),
        in_specs=[whole, whole, pl.BlockSpec((3, group, channels), lambda step: (step, 0, 0))],
        out_specs=pl.BlockSpec((cells, channels), lambda step: (0, 0)),
        out_shape=jax.ShapeDtypeStruct((cells, channels), BF16),
        scratch_shapes=[
            pltpu.VMEM((2 * frames_n, rows_n + 2, width_n, 3 * group), F32),
            pltpu.VMEM((cells, channels), F32),
        ],
        compiler_params=pltpu.CompilerParams(vmem_limit_bytes=30 * 2**20),
        cost_estimate=pl.CostEstimate(
            flops=54 * group * channels * cells, bytes_accessed=54 * group * channels, transcendentals=0
        ),
    )(current, later, kernels)


def tap_kernel(grad_ref, parts_ref, out_ref, feature_ref, arrived):
    tap = pl.program_id(0)
    rings, chans, rows_l, _, width_c = parts_ref.shape

    @pl.when(tap == 0)
    def _():
        copies = []
        for ring in range(rings):
            for chan in range(chans):
                copies.append(
                    pltpu.make_async_copy(
                        parts_ref.at[ring, chan],
                        feature_ref.at[pl.ds(ring * rows_l, rows_l), :, pl.ds(chan * width_c, width_c)],
                        arrived.at[ring * chans + chan],
                    )
                )
        for copy in copies:
            copy.start()
        for copy in copies:
            copy.wait()

    lag = tap // 9
    offset = 2 - (tap // 3) % 3
    side = tap % 3
    rows_n, span = feature_ref.shape[0], feature_ref.shape[1]
    padded = span + 2 * 128
    total = jnp.zeros(out_ref.shape[1:], F32)
    for row in range(rows_n):
        start = pl.multiple_of((row + offset) * padded + lag * 128, 128)
        total += jnp.dot(grad_ref[side, :, pl.ds(start, span)], feature_ref[row], preferred_element_type=F32)
    out_ref[0] = total.astype(BF16)


def kernel_gradient(grads, parts):
    group = grads.shape[1]
    rings, chans, rows_l, span, width_c = parts.shape
    channels = chans * width_c
    return pl.pallas_call(
        tap_kernel,
        grid=(27,),
        in_specs=[
            pl.BlockSpec(grads.shape, lambda tap: (0, 0, 0), pipeline_mode=pl.Buffered(1)),
            pl.BlockSpec(memory_space=pl.ANY),
        ],
        out_specs=pl.BlockSpec((1, group, channels), lambda tap: (tap, 0, 0)),
        out_shape=jax.ShapeDtypeStruct((27, group, channels), BF16),
        scratch_shapes=[
            pltpu.VMEM((rings * rows_l, span, channels), BF16),
            pltpu.SemaphoreType.DMA((rings * chans,)),
        ],
        compiler_params=pltpu.CompilerParams(vmem_limit_bytes=48 * 2**20),
        cost_estimate=pl.CostEstimate(
            flops=54 * group * parts.size,
            bytes_accessed=2 * (grads.size + parts.size + 27 * group * channels),
            transcendentals=0,
        ),
    )(grads, parts)


def body(upstream, acts, weights):
    group, frames_all, rows_l, width_n = upstream.shape
    channels = acts.shape[1]
    sections, rings, chans = lax.axis_size("section"), lax.axis_size("frame"), lax.axis_size("chan")
    section_pos, ring_pos, chan_pos = lax.axis_index("section"), lax.axis_index("frame"), lax.axis_index("chan")
    rows_n = rows_l * rings
    own = width_n // rings
    halo = sections
    window = own + 2 * halo
    blocks_n = frames_all // BLOCK_FRAMES
    ticks = blocks_n + sections - 1
    kernels = weights[0]

    mine = lax.dynamic_slice_in_dim(acts[0], chan_pos * group, group, 0)
    shared = group % 128 == 0
    values = (mine if shared else acts[0]).astype(F32)
    feature_part = (values * jax.nn.sigmoid(values)).astype(BF16).transpose(2, 1, 3, 0)
    feature_part = feature_part.reshape(rows_l, frames_all * width_n, -1)
    feature_all = lax.all_gather(feature_part, ("frame", "chan") if shared else "frame")
    feature_all = feature_all.reshape(rings, chans if shared else 1, *feature_part.shape)

    both = jnp.stack([upstream, mine]).transpose(2, 0, 3, 4, 1)
    both = jnp.pad(both, ((0, 0), (0, 0), (0, 0), (halo, halo), (0, 0)))
    windows = jnp.stack([both[:, :, :, own * i : own * i + window] for i in range(rings)])
    fresh, stored = [], []
    for order in range(blocks_n):
        first = (blocks_n - 1 - order) * BLOCK_FRAMES
        piece = lax.all_to_all(windows[:, first : first + BLOCK_FRAMES], "frame", 0, 0)
        piece = piece.transpose(2, 1, 0, 3, 4, 5).reshape(2, BLOCK_FRAMES, rows_n, window, group)
        fresh.append(piece[0])
        stored.append(piece[1])

    column = ring_pos * own - halo + jnp.arange(window)
    inside = jnp.logical_and(column >= 0, column < width_n)[None, None, :, None]
    later = jnp.zeros((BLOCK_FRAMES, rows_n, window, group), BF16)
    inbound = later
    gathered, results = [], []
    for tick in range(ticks):
        if tick < blocks_n:
            current = jnp.where(section_pos == 0, fresh[tick], inbound)
        else:
            current = inbound
        gathered.append(lax.all_gather(current[:, :, halo : halo + own], "frame"))
        partial = back_block(current, later, kernels)
        summed = lax.dynamic_slice_in_dim(partial, chan_pos * group, group, 1).astype(F32)
        for step in range(1, chans):
            there = lax.rem(chan_pos + step, chans)
            piece = lax.dynamic_slice_in_dim(partial, there * group, group, 1)
            arrived = lax.ppermute(piece, "chan", [(i, (i + step) % chans) for i in range(chans)])
            summed = summed + arrived.astype(F32)
        known = jnp.stack(stored[: tick + 1])
        place = jnp.clip(tick - section_pos, 0, known.shape[0] - 1)
        slot = lax.dynamic_index_in_dim(known, place, 0, keepdims=False).astype(F32)
        logistic = jax.nn.sigmoid(slot)
        slope = logistic * (1.0 + slot * (1.0 - logistic))
        updated = current.astype(F32) + slope * summed.reshape(current.shape)
        updated = jnp.where(inside, updated, 0.0).astype(BF16)
        results.append(updated[:, :, halo : halo + own])
        later = current
        if tick + 1 < ticks:
            inbound = lax.ppermute(updated, "section", [(i, i + 1) for i in range(sections - 1)])

    taken = lax.dynamic_slice_in_dim(jnp.stack(gathered), section_pos, blocks_n, 0)[::-1]
    whole = taken.transpose(5, 3, 0, 2, 1, 4).reshape(group, rows_n, frames_all, width_n)
    padded = jnp.pad(whole, ((0, 0), (1, 1), (0, 2), (1, 1)))
    sides = jnp.stack([padded[..., 2 - j : 2 - j + width_n] for j in range(3)])
    sides = sides.reshape(3, group, -1)
    kernel_total = kernel_gradient(sides, feature_all)

    outs = lax.dynamic_slice_in_dim(jnp.stack(results), section_pos, blocks_n, 0)[::-1]
    outs = outs.reshape(frames_all, rings, rows_l, own, group).transpose(1, 0, 2, 3, 4)
    outs = lax.all_to_all(outs, "frame", 0, 0)
    outs = outs.transpose(4, 1, 2, 0, 3).reshape(group, frames_all, rows_l, width_n)
    return (outs[None], kernel_total[None])


def solution(mesh):
    placed = (
        P("chan", None, "frame", None),
        P("section", None, None, "frame", None),
        P("section", None, "chan", None),
    )
    return jax.shard_map(
        body,
        mesh=mesh,
        in_specs=placed,
        out_specs=(P("section", "chan", None, "frame", None), P("section", None, "chan", None)),
        check_vma=False,
    )
```

```python
import jax
import jax.numpy as jnp
from jax import lax
from jax.experimental import pallas as pl
from jax.experimental.pallas import tpu as pltpu
from jax.sharding import PartitionSpec as P

BLOCK_FRAMES = 2
F32 = jnp.float32
BF16 = jnp.bfloat16


def back_kernel(cur_ref, later_ref, w_ref, out_ref, spread, acc):
    frames_n, rows_n, width_n, group = cur_ref.shape
    empty = jnp.zeros((width_n, 3 * group), F32)
    for frame in range(2 * frames_n):
        spread[frame, 0] = empty
        spread[frame, rows_n + 1] = empty
        for row in range(rows_n):
            source = cur_ref[frame, row] if frame < frames_n else later_ref[frame - frames_n, row]
            cells = source.astype(F32)
            spread[frame, row + 1, :, 0:group] = pltpu.roll(cells, width_n - 1, 0)
            spread[frame, row + 1, :, group : 2 * group] = cells
            spread[frame, row + 1, :, 2 * group : 3 * group] = pltpu.roll(cells, 1, 0)
    for step in range(9):
        lag, offset = step // 3, 2 - step % 3
        taken = spread[lag : lag + frames_n, offset : offset + rows_n]
        taken = taken.reshape(frames_n * rows_n * width_n, 3 * group).astype(BF16)
        part = jnp.dot(
            taken, w_ref[3 * step : 3 * step + 3].reshape(3 * group, -1), preferred_element_type=F32
        )
        if step == 0:
            acc[...] = part
        elif step < 8:
            acc[...] += part
        else:
            out_ref[...] = (acc[...] + part).astype(BF16)


def back_block(current, later, kernels):
    frames_n, rows_n, width_n, group = current.shape
    channels = kernels.shape[2]
    cells = frames_n * rows_n * width_n
    held = pl.BlockSpec(memory_space=pltpu.VMEM)
    return pl.pallas_call(
        back_kernel,
        in_specs=[held, held, held],
        out_specs=held,
        out_shape=jax.ShapeDtypeStruct((cells, channels), BF16),
        scratch_shapes=[
            pltpu.VMEM((2 * frames_n, rows_n + 2, width_n, 3 * group), F32),
            pltpu.VMEM((cells, channels), F32),
        ],
        compiler_params=pltpu.CompilerParams(vmem_limit_bytes=24 * 2**20),
        cost_estimate=pl.CostEstimate(
            flops=54 * group * channels * cells, bytes_accessed=54 * group * channels, transcendentals=0
        ),
    )(current, later, kernels)


def tap_kernel(first, has_next, has_sum, *refs):
    grad_ref, next_ref, parts_ref, sum_ref, out_ref, sides, feature_ref, arrived = refs
    step = pl.program_id(0)
    rings, chans, rows_l, _, width_c = parts_ref.shape
    _, frames_n, rows_n, own, group = grad_ref.shape
    width_n = rings * own
    span = frames_n * width_n

    @pl.when(step == 0)
    def _():
        copies = []
        for ring in range(rings):
            for chan in range(chans):
                copies.append(
                    pltpu.make_async_copy(
                        parts_ref.at[ring, chan, :, pl.ds(first * width_n, span)],
                        feature_ref.at[pl.ds(ring * rows_l, rows_l), :, pl.ds(chan * width_c, width_c)],
                        arrived.at[ring * chans + chan],
                    )
                )
        for copy in copies:
            copy.start()
        column = lax.broadcasted_iota(jnp.int32, (group, width_n), 1)
        empty = jnp.zeros((3 * group, width_n), BF16)
        for row in range(rows_n + 2):
            for frame in range(frames_n + 2):
                start = (row * (frames_n + 2) + frame) * width_n
                if row in (0, rows_n + 1) or (frame >= frames_n and not has_next):
                    sides[:, start : start + width_n] = empty
                    continue
                ref, place = (grad_ref, frame) if frame < frames_n else (next_ref, frame - frames_n)
                cells = jnp.concatenate([ref[ring, place, row - 1] for ring in range(rings)], axis=0)
                cells = cells.astype(F32).T
                left = jnp.where(column == width_n - 1, 0.0, pltpu.roll(cells, width_n - 1, 1))
                right = jnp.where(column == 0, 0.0, pltpu.roll(cells, 1, 1))
                sides[0:group, start : start + width_n] = left.astype(BF16)
                sides[group : 2 * group, start : start + width_n] = cells.astype(BF16)
                sides[2 * group : 3 * group, start : start + width_n] = right.astype(BF16)
        for copy in copies:
            copy.wait()

    lag = step // 3
    offset = 2 - step % 3
    pieces = []
    for row in range(rows_n):
        start = ((row + offset) * (frames_n + 2) + lag) * width_n
        pieces.append(sides[:, pl.ds(pl.multiple_of(start, 128), span)])
    total = jnp.dot(
        jnp.concatenate(pieces, axis=1),
        feature_ref[...].reshape(rows_n * span, -1),
        preferred_element_type=F32,
    ).reshape(out_ref.shape)
    if has_sum:
        total = total + sum_ref[...]
    out_ref[...] = total.astype(out_ref.dtype)


def kernel_gradient(first, grads, later, parts, known):
    _, frames_n, rows_n, own, group = grads.shape
    rings, chans, rows_l, _, width_c = parts.shape
    channels = chans * width_c
    width_n = rings * own
    held = pl.BlockSpec(grads.shape, lambda step: (0,) * 5, pipeline_mode=pl.Buffered(1))
    out_spec = pl.BlockSpec((3, group, channels), lambda step: (step, 0, 0))
    has_next, has_sum = later is not None, known is not None
    operands = [grads] + ([later] if has_next else []) + [parts] + ([known] if has_sum else [])
    specs = [held] * (2 if has_next else 1) + [pl.BlockSpec(memory_space=pl.ANY)] + [out_spec] * has_sum

    def kernel(*refs):
        refs = list(refs)
        if not has_next:
            refs.insert(1, None)
        if not has_sum:
            refs.insert(3, None)
        tap_kernel(first, has_next, has_sum, *refs)

    return pl.pallas_call(
        kernel,
        grid=(9,),
        in_specs=specs,
        out_specs=out_spec,
        out_shape=jax.ShapeDtypeStruct((27, group, channels), BF16 if has_sum else F32),
        scratch_shapes=[
            pltpu.VMEM((3 * group, (rows_n + 2) * (frames_n + 2) * width_n), BF16),
            pltpu.VMEM((rows_n, frames_n * width_n, channels), BF16),
            pltpu.SemaphoreType.DMA((rings * chans,)),
        ],
        compiler_params=pltpu.CompilerParams(vmem_limit_bytes=40 * 2**20),
        cost_estimate=pl.CostEstimate(
            flops=54 * group * channels * rows_n * frames_n * width_n,
            bytes_accessed=(12 if has_sum else 8) * 27 * group * channels,
            transcendentals=0,
        ),
    )(*operands)


def body(upstream, acts, weights):
    group, frames_all, rows_l, width_n = upstream.shape
    channels = acts.shape[1]
    sections, rings, chans = lax.axis_size("section"), lax.axis_size("frame"), lax.axis_size("chan")
    section_pos, ring_pos, chan_pos = lax.axis_index("section"), lax.axis_index("frame"), lax.axis_index("chan")
    rows_n = rows_l * rings
    own = width_n // rings
    halo = sections
    window = own + 2 * halo
    blocks_n = frames_all // BLOCK_FRAMES
    ticks = blocks_n + sections - 1
    kernels = weights[0]

    mine = lax.dynamic_slice_in_dim(acts[0], chan_pos * group, group, 0)
    both = jnp.stack([upstream, mine]).transpose(2, 0, 3, 4, 1)
    both = jnp.pad(both, ((0, 0), (0, 0), (0, 0), (halo, halo), (0, 0)))
    windows = jnp.stack([both[:, :, :, own * i : own * i + window] for i in range(rings)])
    fresh, stored = [], []
    half = frames_all // 2
    for first in (half, 0):
        piece = lax.all_to_all(windows[:, first : first + half], "frame", 0, 0)
        piece = piece.transpose(2, 1, 0, 3, 4, 5).reshape(2, half, rows_n, window, group)
        for order in range(half // BLOCK_FRAMES):
            start = half - (order + 1) * BLOCK_FRAMES
            fresh.append(piece[0, start : start + BLOCK_FRAMES])
            stored.append(piece[1, start : start + BLOCK_FRAMES])

    shared = group % 128 == 0
    mine, acts, _ = lax.optimization_barrier((mine, acts, piece))
    values = (mine if shared else acts[0]).astype(F32)
    feature_part = (values * jax.nn.sigmoid(values)).astype(BF16).transpose(2, 1, 3, 0)
    feature_part = feature_part.reshape(rows_l, frames_all * width_n, -1)
    feature_all = lax.all_gather(feature_part, ("frame", "chan") if shared else "frame")
    feature_all = feature_all.reshape(rings, chans if shared else 1, *feature_part.shape)

    column = ring_pos * own - halo + jnp.arange(window)
    inside = jnp.logical_and(column >= 0, column < width_n)[None, None, :, None]
    later = jnp.zeros((BLOCK_FRAMES, rows_n, window, group), BF16)
    inbound = later
    held, gathered, results = [], [], []
    per_half = blocks_n // 2
    for tick in range(ticks):
        if tick < blocks_n:
            current = jnp.where(section_pos == 0, fresh[tick], inbound)
        else:
            current = inbound
        held.append(current[:, :, halo : halo + own])
        if tick in (ticks - 1 - per_half, ticks - 1):
            begin = len(gathered) * per_half
            taken = jnp.stack(held[begin : begin + per_half + sections - 1])
            taken = lax.dynamic_slice_in_dim(taken, section_pos, per_half, 0)[::-1]
            gathered.append(lax.all_gather(taken.reshape(half, rows_n, own, group), "frame"))
        partial = back_block(current, later, kernels)
        summed = lax.dynamic_slice_in_dim(partial, chan_pos * group, group, 1).astype(F32)
        for step in range(1, chans):
            there = lax.rem(chan_pos + step, chans)
            piece = lax.dynamic_slice_in_dim(partial, there * group, group, 1)
            arrived = lax.ppermute(piece, "chan", [(i, (i + step) % chans) for i in range(chans)])
            summed = summed + arrived.astype(F32)
        known = jnp.stack(stored[: tick + 1])
        place = jnp.clip(tick - section_pos, 0, known.shape[0] - 1)
        slot = lax.dynamic_index_in_dim(known, place, 0, keepdims=False).astype(F32)
        logistic = jax.nn.sigmoid(slot)
        slope = logistic * (1.0 + slot * (1.0 - logistic))
        updated = current.astype(F32) + slope * summed.reshape(current.shape)
        updated = jnp.where(inside, updated, 0.0).astype(BF16)
        results.append(updated[:, :, halo : halo + own])
        later = current
        if tick + 1 < ticks:
            inbound = lax.ppermute(updated, "section", [(i, i + 1) for i in range(sections - 1)])

    kernel_sum = kernel_gradient(half, gathered[0], None, feature_all, None)
    kernel_total = kernel_gradient(0, gathered[1], gathered[0], feature_all, kernel_sum)

    outs = lax.dynamic_slice_in_dim(jnp.stack(results), section_pos, blocks_n, 0)[::-1]
    outs = outs.reshape(frames_all, rings, rows_l, own, group).transpose(1, 0, 2, 3, 4)
    outs = lax.all_to_all(outs, "frame", 0, 0)
    outs = outs.transpose(4, 1, 2, 0, 3).reshape(group, frames_all, rows_l, width_n)
    return (outs[None], kernel_total[None])


def solution(mesh):
    placed = (
        P("chan", None, "frame", None),
        P("section", None, None, "frame", None),
        P("section", None, "chan", None),
    )
    return jax.shard_map(
        body,
        mesh=mesh,
        in_specs=placed,
        out_specs=(P("section", "chan", None, "frame", None), P("section", None, "chan", None)),
        check_vma=False,
    )
```

```python
import jax
import jax.numpy as jnp
from jax import lax
from jax.experimental import pallas as pl
from jax.experimental.pallas import tpu as pltpu
from jax.sharding import PartitionSpec as P

BLOCK_FRAMES = 2
F32 = jnp.float32
BF16 = jnp.bfloat16


def back_kernel(cur_ref, later_ref, w_ref, out_ref, spread, acc):
    frames_n, rows_n, width_n, group = cur_ref.shape
    empty = jnp.zeros((width_n, 3 * group), F32)
    for frame in range(2 * frames_n):
        spread[frame, 0] = empty
        spread[frame, rows_n + 1] = empty
        for row in range(rows_n):
            source = cur_ref[frame, row] if frame < frames_n else later_ref[frame - frames_n, row]
            cells = source.astype(F32)
            spread[frame, row + 1, :, 0:group] = pltpu.roll(cells, width_n - 1, 0)
            spread[frame, row + 1, :, group : 2 * group] = cells
            spread[frame, row + 1, :, 2 * group : 3 * group] = pltpu.roll(cells, 1, 0)
    for step in range(9):
        lag, offset = step // 3, 2 - step % 3
        taken = spread[lag : lag + frames_n, offset : offset + rows_n]
        taken = taken.reshape(frames_n * rows_n * width_n, 3 * group).astype(BF16)
        part = jnp.dot(
            taken, w_ref[3 * step : 3 * step + 3].reshape(3 * group, -1), preferred_element_type=F32
        )
        if step == 0:
            acc[...] = part
        elif step < 8:
            acc[...] += part
        else:
            out_ref[...] = (acc[...] + part).astype(BF16)


def back_block(current, later, kernels):
    frames_n, rows_n, width_n, group = current.shape
    channels = kernels.shape[2]
    cells = frames_n * rows_n * width_n
    held = pl.BlockSpec(memory_space=pltpu.VMEM)
    return pl.pallas_call(
        back_kernel,
        in_specs=[held, held, held],
        out_specs=held,
        out_shape=jax.ShapeDtypeStruct((cells, channels), BF16),
        scratch_shapes=[
            pltpu.VMEM((2 * frames_n, rows_n + 2, width_n, 3 * group), F32),
            pltpu.VMEM((cells, channels), F32),
        ],
        compiler_params=pltpu.CompilerParams(vmem_limit_bytes=24 * 2**20),
        cost_estimate=pl.CostEstimate(
            flops=54 * group * channels * cells, bytes_accessed=54 * group * channels, transcendentals=0
        ),
    )(current, later, kernels)


def tap_kernel(first, has_next, has_sum, *refs):
    grad_ref, next_ref, parts_ref, sum_ref, out_ref, sides, feature_ref, arrived = refs
    step = pl.program_id(0)
    rings, chans, rows_l, _, width_c = parts_ref.shape
    _, frames_n, rows_n, own, group = grad_ref.shape
    width_n = rings * own
    span = frames_n * width_n

    @pl.when(step == 0)
    def _():
        copies = []
        for ring in range(rings):
            for chan in range(chans):
                copies.append(
                    pltpu.make_async_copy(
                        parts_ref.at[ring, chan, :, pl.ds(first * width_n, span)],
                        feature_ref.at[pl.ds(ring * rows_l, rows_l), :, pl.ds(chan * width_c, width_c)],
                        arrived.at[ring * chans + chan],
                    )
                )
        for copy in copies:
            copy.start()
        column = lax.broadcasted_iota(jnp.int32, (group, width_n), 1)
        empty = jnp.zeros((3 * group, width_n), BF16)
        for row in range(rows_n + 2):
            for frame in range(frames_n + 2):
                start = (row * (frames_n + 2) + frame) * width_n
                if row in (0, rows_n + 1) or (frame >= frames_n and not has_next):
                    sides[:, start : start + width_n] = empty
                    continue
                ref, place = (grad_ref, frame) if frame < frames_n else (next_ref, frame - frames_n)
                cells = jnp.concatenate([ref[ring, place, row - 1] for ring in range(rings)], axis=0)
                cells = cells.astype(F32).T
                left = jnp.where(column == width_n - 1, 0.0, pltpu.roll(cells, width_n - 1, 1))
                right = jnp.where(column == 0, 0.0, pltpu.roll(cells, 1, 1))
                sides[0:group, start : start + width_n] = left.astype(BF16)
                sides[group : 2 * group, start : start + width_n] = cells.astype(BF16)
                sides[2 * group : 3 * group, start : start + width_n] = right.astype(BF16)
        for copy in copies:
            copy.wait()

    lag = step // 3
    offset = 2 - step % 3
    pieces = []
    for row in range(rows_n):
        start = ((row + offset) * (frames_n + 2) + lag) * width_n
        pieces.append(sides[:, pl.ds(pl.multiple_of(start, 128), span)])
    total = jnp.dot(
        jnp.concatenate(pieces, axis=1),
        feature_ref[...].reshape(rows_n * span, -1),
        preferred_element_type=F32,
    ).reshape(out_ref.shape)
    if has_sum:
        total = total + sum_ref[...]
    out_ref[...] = total.astype(out_ref.dtype)


def kernel_gradient(first, grads, later, parts, known):
    _, frames_n, rows_n, own, group = grads.shape
    rings, chans, rows_l, _, width_c = parts.shape
    channels = chans * width_c
    width_n = rings * own
    held = pl.BlockSpec(grads.shape, lambda step: (0,) * 5, pipeline_mode=pl.Buffered(1))
    out_spec = pl.BlockSpec((3, group, channels), lambda step: (step, 0, 0))
    has_next, has_sum = later is not None, known is not None
    operands = [grads] + ([later] if has_next else []) + [parts] + ([known] if has_sum else [])
    specs = [held] * (2 if has_next else 1) + [pl.BlockSpec(memory_space=pl.ANY)] + [out_spec] * has_sum

    def kernel(*refs):
        refs = list(refs)
        if not has_next:
            refs.insert(1, None)
        if not has_sum:
            refs.insert(3, None)
        tap_kernel(first, has_next, has_sum, *refs)

    return pl.pallas_call(
        kernel,
        grid=(9,),
        in_specs=specs,
        out_specs=out_spec,
        out_shape=jax.ShapeDtypeStruct((27, group, channels), BF16 if has_sum else F32),
        scratch_shapes=[
            pltpu.VMEM((3 * group, (rows_n + 2) * (frames_n + 2) * width_n), BF16),
            pltpu.VMEM((rows_n, frames_n * width_n, channels), BF16),
            pltpu.SemaphoreType.DMA((rings * chans,)),
        ],
        compiler_params=pltpu.CompilerParams(vmem_limit_bytes=40 * 2**20),
        cost_estimate=pl.CostEstimate(
            flops=54 * group * channels * rows_n * frames_n * width_n,
            bytes_accessed=(12 if has_sum else 8) * 27 * group * channels,
            transcendentals=0,
        ),
    )(*operands)


def body(upstream, acts, weights):
    group, frames_all, rows_l, width_n = upstream.shape
    channels = acts.shape[1]
    sections, rings, chans = lax.axis_size("section"), lax.axis_size("frame"), lax.axis_size("chan")
    section_pos, ring_pos, chan_pos = lax.axis_index("section"), lax.axis_index("frame"), lax.axis_index("chan")
    rows_n = rows_l * rings
    own = width_n // rings
    halo = sections
    window = own + 2 * halo
    blocks_n = frames_all // BLOCK_FRAMES
    ticks = blocks_n + sections - 1
    kernels = weights[0]

    mine = lax.dynamic_slice_in_dim(acts[0], chan_pos * group, group, 0)
    both = jnp.stack([upstream, mine]).transpose(2, 0, 3, 4, 1)
    both = jnp.pad(both, ((0, 0), (0, 0), (0, 0), (halo, halo), (0, 0)))
    windows = jnp.stack([both[:, :, :, own * i : own * i + window] for i in range(rings)])
    fresh, stored = [], []
    half = frames_all // 2
    for top, low in ((frames_all, frames_all - BLOCK_FRAMES), (frames_all - BLOCK_FRAMES, half), (half, 0)):
        piece = lax.all_to_all(windows[:, low:top], "frame", 0, 0)
        piece = piece.transpose(2, 1, 0, 3, 4, 5).reshape(2, top - low, rows_n, window, group)
        for start in range(top - low - BLOCK_FRAMES, -1, -BLOCK_FRAMES):
            fresh.append(piece[0, start : start + BLOCK_FRAMES])
            stored.append(piece[1, start : start + BLOCK_FRAMES])

    shared = group % 128 == 0
    mine, acts, _ = lax.optimization_barrier((mine, acts, stored[0]))
    values = (mine if shared else acts[0]).astype(F32)
    feature_part = (values * jax.nn.sigmoid(values)).astype(BF16).transpose(2, 1, 3, 0)
    feature_part = feature_part.reshape(rows_l, frames_all * width_n, -1)
    feature_all = lax.all_gather(feature_part, ("frame", "chan") if shared else "frame")
    feature_all = feature_all.reshape(rings, chans if shared else 1, *feature_part.shape)

    column = ring_pos * own - halo + jnp.arange(window)
    inside = jnp.logical_and(column >= 0, column < width_n)[None, None, :, None]
    later = jnp.zeros((BLOCK_FRAMES, rows_n, window, group), BF16)
    inbound = later
    held, gathered, results = [], [], []
    per_half = blocks_n // 2
    for tick in range(ticks):
        if tick < blocks_n:
            current = jnp.where(section_pos == 0, fresh[tick], inbound)
        else:
            current = inbound
        if tick == ticks - 2:
            current, feature_all = lax.optimization_barrier((current, feature_all))
        held.append(current[:, :, halo : halo + own])
        if tick in (ticks - 1 - per_half, ticks - 1):
            begin = len(gathered) * per_half
            taken = jnp.stack(held[begin : begin + per_half + sections - 1])
            taken = lax.dynamic_slice_in_dim(taken, section_pos, per_half, 0)[::-1]
            if not gathered:
                taken, feature_all = lax.optimization_barrier((taken, feature_all))
            gathered.append(lax.all_gather(taken.reshape(half, rows_n, own, group), "frame"))
        partial = back_block(current, later, kernels)
        summed = lax.dynamic_slice_in_dim(partial, chan_pos * group, group, 1).astype(F32)
        for step in range(1, chans):
            there = lax.rem(chan_pos + step, chans)
            piece = lax.dynamic_slice_in_dim(partial, there * group, group, 1)
            arrived = lax.ppermute(piece, "chan", [(i, (i + step) % chans) for i in range(chans)])
            summed = summed + arrived.astype(F32)
        known = jnp.stack(stored[: tick + 1])
        place = jnp.clip(tick - section_pos, 0, known.shape[0] - 1)
        slot = lax.dynamic_index_in_dim(known, place, 0, keepdims=False).astype(F32)
        logistic = jax.nn.sigmoid(slot)
        slope = logistic * (1.0 + slot * (1.0 - logistic))
        updated = current.astype(F32) + slope * summed.reshape(current.shape)
        updated = jnp.where(inside, updated, 0.0).astype(BF16)
        results.append(updated[:, :, halo : halo + own])
        later = current
        if tick + 1 < ticks:
            inbound = lax.ppermute(updated, "section", [(i, i + 1) for i in range(sections - 1)])

    kernel_sum = kernel_gradient(half, gathered[0], None, feature_all, None)
    kernel_total = kernel_gradient(0, gathered[1], gathered[0], feature_all, kernel_sum)

    outs = lax.dynamic_slice_in_dim(jnp.stack(results), section_pos, blocks_n, 0)[::-1]
    outs = outs.reshape(frames_all, rings, rows_l, own, group).transpose(1, 0, 2, 3, 4)
    outs, _ = lax.optimization_barrier((outs, gathered[1]))
    outs = lax.all_to_all(outs, "frame", 0, 0)
    outs, kernel_total = lax.optimization_barrier((outs, kernel_total))
    outs = outs.transpose(4, 1, 2, 0, 3).reshape(group, frames_all, rows_l, width_n)
    return (outs[None], kernel_total[None])


def solution(mesh):
    placed = (
        P("chan", None, "frame", None),
        P("section", None, None, "frame", None),
        P("section", None, "chan", None),
    )
    return jax.shard_map(
        body,
        mesh=mesh,
        in_specs=placed,
        out_specs=(P("section", "chan", None, "frame", None), P("section", None, "chan", None)),
        check_vma=False,
    )
```

```python
import jax
import jax.numpy as jnp
from jax import lax
from jax.experimental import pallas as pl
from jax.experimental.pallas import tpu as pltpu
from jax.sharding import PartitionSpec as P

BLOCK_FRAMES = 2
F32 = jnp.float32
BF16 = jnp.bfloat16


def back_kernel(cur_ref, later_ref, kernels_ref, out_ref, spread, acc, w_ref, arrived):
    frames_n, rows_n, width_n, group = cur_ref.shape
    copies = []
    for step in range(9):
        taps = pl.ds(3 * step, 3)
        copies.append(pltpu.make_async_copy(kernels_ref.at[taps], w_ref.at[taps], arrived.at[step]))
    for copy in copies:
        copy.start()
    empty = jnp.zeros((width_n, 3 * group), F32)
    for frame in range(2 * frames_n):
        spread[frame, 0] = empty
        spread[frame, rows_n + 1] = empty
        for row in range(rows_n):
            source = cur_ref[frame, row] if frame < frames_n else later_ref[frame - frames_n, row]
            cells = source.astype(F32)
            spread[frame, row + 1, :, 0:group] = pltpu.roll(cells, width_n - 1, 0)
            spread[frame, row + 1, :, group : 2 * group] = cells
            spread[frame, row + 1, :, 2 * group : 3 * group] = pltpu.roll(cells, 1, 0)
    for step in range(9):
        lag, offset = step // 3, 2 - step % 3
        taken = spread[lag : lag + frames_n, offset : offset + rows_n]
        taken = taken.reshape(frames_n * rows_n * width_n, 3 * group).astype(BF16)
        copies[step].wait()
        part = jnp.dot(
            taken, w_ref[3 * step : 3 * step + 3].reshape(3 * group, -1), preferred_element_type=F32
        )
        if step == 0:
            acc[...] = part
        elif step < 8:
            acc[...] += part
        else:
            out_ref[...] = (acc[...] + part).astype(BF16)


def back_block(current, later, kernels):
    frames_n, rows_n, width_n, group = current.shape
    channels = kernels.shape[2]
    cells = frames_n * rows_n * width_n
    held = pl.BlockSpec(memory_space=pltpu.VMEM)
    return pl.pallas_call(
        back_kernel,
        in_specs=[held, held, pl.BlockSpec(memory_space=pltpu.HBM)],
        out_specs=held,
        out_shape=jax.ShapeDtypeStruct((cells, channels), BF16),
        scratch_shapes=[
            pltpu.VMEM((2 * frames_n, rows_n + 2, width_n, 3 * group), F32),
            pltpu.VMEM((cells, channels), F32),
            pltpu.VMEM(kernels.shape, BF16),
            pltpu.SemaphoreType.DMA((9,)),
        ],
        compiler_params=pltpu.CompilerParams(vmem_limit_bytes=24 * 2**20),
        cost_estimate=pl.CostEstimate(
            flops=54 * group * channels * cells, bytes_accessed=54 * group * channels, transcendentals=0
        ),
    )(current, later, kernels)


def tap_kernel(first, blocks_n, has_next, grad_refs, parts_ref, sum_ref, out_ref, cells_ref, sides, feature_ref, g_here, f_here):
    step = pl.program_id(0)
    rings, chans, rows_l, _, width_c = parts_ref.shape
    pieces_n, block, rows_n, own, group = grad_refs[0].shape
    width_n = pieces_n * own
    frames_n = blocks_n * block
    span = frames_n * width_n

    @pl.when(step == 0)
    def _():
        g_copies, f_copies = [], []
        for index, ref in enumerate(grad_refs):
            for piece in range(pieces_n):
                g_copies.append(
                    pltpu.make_async_copy(
                        ref.at[piece],
                        cells_ref.at[pl.ds(index * block, block), :, pl.ds(piece * own, own)],
                        g_here.at[index * pieces_n + piece],
                    )
                )
        for ring in range(rings):
            for chan in range(chans):
                f_copies.append(
                    pltpu.make_async_copy(
                        parts_ref.at[ring, chan, :, pl.ds(first * width_n, span)],
                        feature_ref.at[pl.ds(ring * rows_l, rows_l), :, pl.ds(chan * width_c, width_c)],
                        f_here.at[ring * chans + chan],
                    )
                )
        for copy in g_copies + f_copies:
            copy.start()
        column = lax.broadcasted_iota(jnp.int32, (group, width_n), 1)
        empty = jnp.zeros((3 * group, width_n), BF16)
        for frame in range(frames_n + 2):
            filled = frame < frames_n or has_next
            if filled and frame % block == 0:
                for piece in range(pieces_n):
                    g_copies[frame // block * pieces_n + piece].wait()
            for row in range(rows_n + 2):
                start = (row * (frames_n + 2) + frame) * width_n
                if row in (0, rows_n + 1) or not filled:
                    sides[:, start : start + width_n] = empty
                    continue
                cells = cells_ref[frame, row - 1].astype(F32).T
                left = jnp.where(column == width_n - 1, 0.0, pltpu.roll(cells, width_n - 1, 1))
                right = jnp.where(column == 0, 0.0, pltpu.roll(cells, 1, 1))
                sides[0:group, start : start + width_n] = left.astype(BF16)
                sides[group : 2 * group, start : start + width_n] = cells.astype(BF16)
                sides[2 * group : 3 * group, start : start + width_n] = right.astype(BF16)
        for copy in f_copies:
            copy.wait()

    lag = step // 3
    offset = 2 - step % 3
    pieces = []
    for row in range(rows_n):
        start = ((row + offset) * (frames_n + 2) + lag) * width_n
        pieces.append(sides[:, pl.ds(pl.multiple_of(start, 128), span)])
    total = jnp.dot(
        jnp.concatenate(pieces, axis=1),
        feature_ref[...].reshape(rows_n * span, -1),
        preferred_element_type=F32,
    ).reshape(out_ref.shape)
    if sum_ref is not None:
        total = total + sum_ref[...]
    out_ref[...] = total.astype(out_ref.dtype)


def kernel_gradient(first, blocks, later, parts, known, out_type):
    pieces_n, block, rows_n, own, group = blocks[0].shape
    rings, chans, rows_l, _, width_c = parts.shape
    channels = chans * width_c
    width_n = pieces_n * own
    frames_n = len(blocks) * block
    far = pl.BlockSpec(memory_space=pltpu.HBM)
    out_spec = pl.BlockSpec((3, group, channels), lambda step: (step, 0, 0))
    grads = list(blocks) + ([] if later is None else [later])
    operands = grads + [parts] + ([] if known is None else [known])

    def kernel(*refs):
        inputs, rest = refs[: len(operands)], refs[len(operands) :]
        sum_ref = None if known is None else inputs[-1]
        tap_kernel(
            first, len(blocks), later is not None, inputs[: len(grads)], inputs[len(grads)], sum_ref, *rest
        )

    return pl.pallas_call(
        kernel,
        grid=(9,),
        in_specs=[far] * (len(grads) + 1) + ([] if known is None else [out_spec]),
        out_specs=out_spec,
        out_shape=jax.ShapeDtypeStruct((27, group, channels), out_type),
        scratch_shapes=[
            pltpu.VMEM((len(grads) * block, rows_n, width_n, group), BF16),
            pltpu.VMEM((3 * group, (rows_n + 2) * (frames_n + 2) * width_n), BF16),
            pltpu.VMEM((rows_n, frames_n * width_n, channels), BF16),
            pltpu.SemaphoreType.DMA((len(grads) * pieces_n,)),
            pltpu.SemaphoreType.DMA((rings * chans,)),
        ],
        compiler_params=pltpu.CompilerParams(vmem_limit_bytes=40 * 2**20),
        cost_estimate=pl.CostEstimate(
            flops=54 * group * channels * rows_n * frames_n * width_n,
            bytes_accessed=8 * 27 * group * channels,
            transcendentals=0,
        ),
    )(*operands)


def body(upstream, acts, weights):
    group, frames_all, rows_l, width_n = upstream.shape
    channels = acts.shape[1]
    sections, rings, chans = lax.axis_size("section"), lax.axis_size("frame"), lax.axis_size("chan")
    section_pos, ring_pos, chan_pos = lax.axis_index("section"), lax.axis_index("frame"), lax.axis_index("chan")
    rows_n = rows_l * rings
    own = width_n // rings
    halo = sections
    window = own + 2 * halo
    blocks_n = frames_all // BLOCK_FRAMES
    ticks = blocks_n + sections - 1
    kernels = weights[0]

    mine = lax.dynamic_slice_in_dim(acts[0], chan_pos * group, group, 0)
    both = jnp.stack([upstream, mine]).transpose(2, 0, 3, 4, 1)
    both = jnp.pad(both, ((0, 0), (0, 0), (0, 0), (halo, halo), (0, 0)))
    windows = jnp.stack([both[:, :, :, own * i : own * i + window] for i in range(rings)])
    fresh, stored = [], []
    half = frames_all // 2
    for top, low in ((frames_all, frames_all - BLOCK_FRAMES), (frames_all - BLOCK_FRAMES, half), (half, 0)):
        piece = lax.all_to_all(windows[:, low:top], "frame", 0, 0)
        piece = piece.transpose(2, 1, 0, 3, 4, 5).reshape(2, top - low, rows_n, window, group)
        for start in range(top - low - BLOCK_FRAMES, -1, -BLOCK_FRAMES):
            fresh.append(piece[0, start : start + BLOCK_FRAMES])
            stored.append(piece[1, start : start + BLOCK_FRAMES])

    shared = group % 128 == 0
    mine, acts, _ = lax.optimization_barrier((mine, acts, stored[-1]))
    values = (mine if shared else acts[0]).astype(F32)
    feature_part = (values * jax.nn.sigmoid(values)).astype(BF16).transpose(2, 1, 3, 0)
    feature_part = feature_part.reshape(rows_l, frames_all * width_n, -1)
    feature_all = lax.all_gather(feature_part, ("frame", "chan") if shared else "frame")
    feature_all = feature_all.reshape(rings, chans if shared else 1, *feature_part.shape)

    column = ring_pos * own - halo + jnp.arange(window)
    inside = jnp.logical_and(column >= 0, column < width_n)[None, None, :, None]
    later = jnp.zeros((BLOCK_FRAMES, rows_n, window, group), BF16)
    inbound = later
    held, gathered, results = [], [], []
    for tick in range(ticks):
        if tick < blocks_n:
            current = jnp.where(section_pos == 0, fresh[tick], inbound)
        else:
            current = inbound
        if tick == ticks - 2:
            current, feature_all = lax.optimization_barrier((current, feature_all))
        if tick == ticks - 1:
            current, gathered[0] = lax.optimization_barrier((current, gathered[0]))
        held.append(current[:, :, halo : halo + own])
        if tick >= sections - 1:
            order = tick - sections + 1
            taken = lax.dynamic_index_in_dim(jnp.stack(held[order:]), section_pos, 0, keepdims=False)
            if order == 0:
                taken, feature_all = lax.optimization_barrier((taken, feature_all))
            else:
                taken, gathered[-1] = lax.optimization_barrier((taken, gathered[-1]))
            gathered.append(lax.all_gather(taken, "frame"))
        partial = back_block(current, later, kernels)
        summed = lax.dynamic_slice_in_dim(partial, chan_pos * group, group, 1).astype(F32)
        for step in range(1, chans):
            there = lax.rem(chan_pos + step, chans)
            piece = lax.dynamic_slice_in_dim(partial, there * group, group, 1)
            arrived = lax.ppermute(piece, "chan", [(i, (i + step) % chans) for i in range(chans)])
            summed = summed + arrived.astype(F32)
        known = jnp.stack(stored[: tick + 1])
        place = jnp.clip(tick - section_pos, 0, known.shape[0] - 1)
        slot = lax.dynamic_index_in_dim(known, place, 0, keepdims=False).astype(F32)
        logistic = jax.nn.sigmoid(slot)
        slope = logistic * (1.0 + slot * (1.0 - logistic))
        updated = current.astype(F32) + slope * summed.reshape(current.shape)
        updated = jnp.where(inside, updated, 0.0).astype(BF16)
        results.append(updated[:, :, halo : halo + own])
        later = current
        if tick + 1 < ticks:
            inbound = lax.ppermute(updated, "section", [(i, i + 1) for i in range(sections - 1)])

    if own % 16:
        gathered = [
            block.transpose(1, 2, 0, 3, 4).reshape(1, BLOCK_FRAMES, rows_n, width_n, group) for block in gathered
        ]
    kernel_total = kernel_gradient(half, gathered[blocks_n // 2 - 1 :: -1], None, feature_all, None, F32)
    for order in range(blocks_n // 2, blocks_n):
        first = (blocks_n - 1 - order) * BLOCK_FRAMES
        out_type = BF16 if order == blocks_n - 1 else F32
        kernel_total = kernel_gradient(first, [gathered[order]], gathered[order - 1], feature_all, kernel_total, out_type)

    outs = lax.dynamic_slice_in_dim(jnp.stack(results), section_pos, blocks_n, 0)[::-1]
    outs = outs.reshape(frames_all, rings, rows_l, own, group).transpose(1, 0, 2, 3, 4)
    outs, _ = lax.optimization_barrier((outs, gathered[-1]))
    outs = lax.all_to_all(outs, "frame", 0, 0)
    outs, kernel_total = lax.optimization_barrier((outs, kernel_total))
    outs = outs.transpose(4, 1, 2, 0, 3).reshape(group, frames_all, rows_l, width_n)
    return (outs[None], kernel_total[None])


def solution(mesh):
    placed = (
        P("chan", None, "frame", None),
        P("section", None, None, "frame", None),
        P("section", None, "chan", None),
    )
    return jax.shard_map(
        body,
        mesh=mesh,
        in_specs=placed,
        out_specs=(P("section", "chan", None, "frame", None), P("section", None, "chan", None)),
        check_vma=False,
    )
```

```python
import jax
import jax.numpy as jnp
from jax import lax
from jax.experimental import pallas as pl
from jax.experimental.pallas import tpu as pltpu
from jax.sharding import PartitionSpec as P

BLOCK_FRAMES = 2
F32 = jnp.float32
BF16 = jnp.bfloat16


def back_kernel(cur_ref, later_ref, kernels_ref, out_ref, spread, acc, w_ref, arrived):
    frames_n, rows_n, width_n, group = cur_ref.shape
    copies = []
    for step in range(9):
        taps = pl.ds(3 * step, 3)
        copies.append(pltpu.make_async_copy(kernels_ref.at[taps], w_ref.at[taps], arrived.at[step]))
    for copy in copies:
        copy.start()
    empty = jnp.zeros((width_n, 3 * group), F32)
    for frame in range(2 * frames_n):
        spread[frame, 0] = empty
        spread[frame, rows_n + 1] = empty
        for row in range(rows_n):
            source = cur_ref[frame, row] if frame < frames_n else later_ref[frame - frames_n, row]
            cells = source.astype(F32)
            spread[frame, row + 1, :, 0:group] = pltpu.roll(cells, width_n - 1, 0)
            spread[frame, row + 1, :, group : 2 * group] = cells
            spread[frame, row + 1, :, 2 * group : 3 * group] = pltpu.roll(cells, 1, 0)
    for step in range(9):
        lag, offset = step // 3, 2 - step % 3
        taken = spread[lag : lag + frames_n, offset : offset + rows_n]
        taken = taken.reshape(frames_n * rows_n * width_n, 3 * group).astype(BF16)
        copies[step].wait()
        part = jnp.dot(
            taken, w_ref[3 * step : 3 * step + 3].reshape(3 * group, -1), preferred_element_type=F32
        )
        if step == 0:
            acc[...] = part
        elif step < 8:
            acc[...] += part
        else:
            out_ref[...] = (acc[...] + part).astype(BF16)


def back_block(current, later, kernels):
    frames_n, rows_n, width_n, group = current.shape
    channels = kernels.shape[2]
    cells = frames_n * rows_n * width_n
    held = pl.BlockSpec(memory_space=pltpu.VMEM)
    return pl.pallas_call(
        back_kernel,
        in_specs=[held, held, pl.BlockSpec(memory_space=pltpu.HBM)],
        out_specs=held,
        out_shape=jax.ShapeDtypeStruct((cells, channels), BF16),
        scratch_shapes=[
            pltpu.VMEM((2 * frames_n, rows_n + 2, width_n, 3 * group), F32),
            pltpu.VMEM((cells, channels), F32),
            pltpu.VMEM(kernels.shape, BF16),
            pltpu.SemaphoreType.DMA((9,)),
        ],
        compiler_params=pltpu.CompilerParams(vmem_limit_bytes=56 * 2**20),
        cost_estimate=pl.CostEstimate(
            flops=54 * group * channels * cells, bytes_accessed=54 * group * channels, transcendentals=0
        ),
    )(current, later, kernels)


def tap_kernel(first, grad_refs, parts_ref, sum_ref, out_ref, cells_ref, sides, feature_ref, g_here, f_here):
    step = pl.program_id(0)
    rings, chans, rows_l, _, width_c = parts_ref.shape
    pieces_n, block, rows_n, own, group = grad_refs[0].shape
    width_n = pieces_n * own
    frames_n = block
    span = frames_n * width_n

    @pl.when(step == 0)
    def _():
        g_copies, f_copies = [], []
        for index, ref in enumerate(grad_refs):
            for piece in range(pieces_n):
                g_copies.append(
                    pltpu.make_async_copy(
                        ref.at[piece],
                        cells_ref.at[pl.ds(index * block, block), :, pl.ds(piece * own, own)],
                        g_here.at[index * pieces_n + piece],
                    )
                )
        for ring in range(rings):
            for chan in range(chans):
                f_copies.append(
                    pltpu.make_async_copy(
                        parts_ref.at[ring, chan, :, pl.ds(first * width_n, span)],
                        feature_ref.at[pl.ds(ring * rows_l, rows_l), :, pl.ds(chan * width_c, width_c)],
                        f_here.at[ring * chans + chan],
                    )
                )
        for copy in g_copies + f_copies:
            copy.start()
        column = lax.broadcasted_iota(jnp.int32, (group, width_n), 1)
        empty = jnp.zeros((3 * group, width_n), BF16)
        for frame in range(frames_n + 2):
            filled = frame < len(grad_refs) * block
            if filled and frame % block == 0:
                for piece in range(pieces_n):
                    g_copies[frame // block * pieces_n + piece].wait()
            for row in range(rows_n + 2):
                start = (row * (frames_n + 2) + frame) * width_n
                if row in (0, rows_n + 1) or not filled:
                    sides[:, start : start + width_n] = empty
                    continue
                cells = cells_ref[frame, row - 1].astype(F32).T
                left = jnp.where(column == width_n - 1, 0.0, pltpu.roll(cells, width_n - 1, 1))
                right = jnp.where(column == 0, 0.0, pltpu.roll(cells, 1, 1))
                sides[0:group, start : start + width_n] = left.astype(BF16)
                sides[group : 2 * group, start : start + width_n] = cells.astype(BF16)
                sides[2 * group : 3 * group, start : start + width_n] = right.astype(BF16)
        for copy in f_copies:
            copy.wait()

    lag = step // 3
    offset = 2 - step % 3
    pieces = []
    for row in range(rows_n):
        start = ((row + offset) * (frames_n + 2) + lag) * width_n
        pieces.append(sides[:, pl.ds(pl.multiple_of(start, 128), span)])
    total = jnp.dot(
        jnp.concatenate(pieces, axis=1),
        feature_ref[...].reshape(rows_n * span, -1),
        preferred_element_type=F32,
    ).reshape(out_ref.shape)
    if sum_ref is not None:
        total = total + sum_ref[...]
    out_ref[...] = total.astype(out_ref.dtype)


def gather_columns(block, rings):
    frames_n, rows_n, own, group = block.shape
    copies = jnp.broadcast_to(block[None], (rings,) + block.shape)
    pieces = lax.all_to_all(copies, "frame", 0, 0)
    if own % 16:
        pieces = pieces.transpose(1, 2, 0, 3, 4).reshape(1, frames_n, rows_n, rings * own, group)
    return pieces


def kernel_gradient(first, grads, later, parts, known, out_type):
    pieces_n, block, rows_n, own, group = grads.shape
    rings, chans, rows_l, _, width_c = parts.shape
    channels = chans * width_c
    width_n = pieces_n * own
    frames_n = block
    far = pl.BlockSpec(memory_space=pltpu.HBM)
    out_spec = pl.BlockSpec((3, group, channels), lambda step: (step, 0, 0))
    grads = [grads] + ([] if later is None else [later])
    operands = grads + [parts] + ([] if known is None else [known])

    def kernel(*refs):
        inputs, rest = refs[: len(operands)], refs[len(operands) :]
        sum_ref = None if known is None else inputs[-1]
        tap_kernel(first, inputs[: len(grads)], inputs[len(grads)], sum_ref, *rest)

    return pl.pallas_call(
        kernel,
        grid=(9,),
        in_specs=[far] * (len(grads) + 1) + ([] if known is None else [out_spec]),
        out_specs=out_spec,
        out_shape=jax.ShapeDtypeStruct((27, group, channels), out_type),
        scratch_shapes=[
            pltpu.VMEM((len(grads) * block, rows_n, width_n, group), BF16),
            pltpu.VMEM((3 * group, (rows_n + 2) * (frames_n + 2) * width_n), BF16),
            pltpu.VMEM((rows_n, frames_n * width_n, channels), BF16),
            pltpu.SemaphoreType.DMA((len(grads) * pieces_n,)),
            pltpu.SemaphoreType.DMA((rings * chans,)),
        ],
        compiler_params=pltpu.CompilerParams(vmem_limit_bytes=58 * 2**20),
        cost_estimate=pl.CostEstimate(
            flops=54 * group * channels * rows_n * frames_n * width_n,
            bytes_accessed=8 * 27 * group * channels,
            transcendentals=0,
        ),
    )(*operands)


def body(upstream, acts, weights):
    group, frames_all, rows_l, width_n = upstream.shape
    channels = acts.shape[1]
    sections, rings, chans = lax.axis_size("section"), lax.axis_size("frame"), lax.axis_size("chan")
    section_pos, ring_pos, chan_pos = lax.axis_index("section"), lax.axis_index("frame"), lax.axis_index("chan")
    rows_n = rows_l * rings
    own = width_n // rings
    halo = sections
    window = own + 2 * halo
    blocks_n = frames_all // BLOCK_FRAMES
    ticks = blocks_n + sections - 1
    kernels = weights[0]

    mine = lax.dynamic_slice_in_dim(acts[0], chan_pos * group, group, 0)
    both = jnp.stack([upstream, mine]).transpose(2, 0, 3, 4, 1)
    both = jnp.pad(both, ((0, 0), (0, 0), (0, 0), (halo, halo), (0, 0)))
    windows = jnp.stack([both[:, :, :, own * i : own * i + window] for i in range(rings)])
    fresh, stored = [], []
    half = frames_all // 2
    for top, low in ((frames_all, frames_all - BLOCK_FRAMES), (frames_all - BLOCK_FRAMES, half), (half, 0)):
        piece = lax.all_to_all(windows[:, low:top], "frame", 0, 0)
        piece = piece.transpose(2, 1, 0, 3, 4, 5).reshape(2, top - low, rows_n, window, group)
        for start in range(top - low - BLOCK_FRAMES, -1, -BLOCK_FRAMES):
            fresh.append(piece[0, start : start + BLOCK_FRAMES])
            stored.append(piece[1, start : start + BLOCK_FRAMES])

    shared = group % 128 == 0
    mine, acts, stored[-1] = lax.optimization_barrier((mine, acts, stored[-1]))
    values = (mine if shared else acts[0]).astype(F32)
    feature_part = (values * jax.nn.sigmoid(values)).astype(BF16).transpose(2, 1, 3, 0)
    feature_part = feature_part.reshape(rows_l, frames_all * width_n, -1)
    feature_all = lax.all_gather(feature_part, ("frame", "chan") if shared else "frame")
    feature_all = feature_all.reshape(rings, chans if shared else 1, *feature_part.shape)

    column = ring_pos * own - halo + jnp.arange(window)
    inside = jnp.logical_and(column >= 0, column < width_n)[None, None, :, None]
    later = jnp.zeros((BLOCK_FRAMES, rows_n, window, group), BF16)
    inbound = later
    held, gathered, results = [], [], []
    for tick in range(ticks):
        if tick < blocks_n:
            current = jnp.where(section_pos == 0, fresh[tick], inbound)
        else:
            current = inbound
        if tick == ticks - 2:
            current, feature_all = lax.optimization_barrier((current, feature_all))
        held.append(current[:, :, halo : halo + own])
        partial = back_block(current, later, kernels)
        summed = lax.dynamic_slice_in_dim(partial, chan_pos * group, group, 1).astype(F32)
        for step in range(1, chans):
            there = lax.rem(chan_pos + step, chans)
            piece = lax.dynamic_slice_in_dim(partial, there * group, group, 1)
            arrived = lax.ppermute(piece, "chan", [(i, (i + step) % chans) for i in range(chans)])
            summed = summed + arrived.astype(F32)
        known = jnp.stack(stored[: tick + 1])
        place = jnp.clip(tick - section_pos, 0, known.shape[0] - 1)
        slot = lax.dynamic_index_in_dim(known, place, 0, keepdims=False).astype(F32)
        logistic = jax.nn.sigmoid(slot)
        slope = logistic * (1.0 + slot * (1.0 - logistic))
        updated = current.astype(F32) + slope * summed.reshape(current.shape)
        updated = jnp.where(inside, updated, 0.0).astype(BF16)
        results.append(updated[:, :, halo : halo + own])
        later = current
        if tick >= sections - 1:
            order = tick - sections + 1
            taken = lax.dynamic_index_in_dim(jnp.stack(held[order:]), section_pos, 0, keepdims=False)
            if tick + 1 < ticks:
                taken, updated = lax.optimization_barrier((taken, updated))
            gathered.append(gather_columns(taken, rings))
        if tick == ticks - 2:
            gathered[0], updated = lax.optimization_barrier((gathered[0], updated))
        if tick + 1 < ticks:
            pairs = [(i, i + 1) for i in range(sections - 1) if i <= tick < i + blocks_n]
            inbound = lax.ppermute(updated, "section", pairs)
        if tick == ticks - 2:
            first = frames_all - BLOCK_FRAMES
            kernel_sum = kernel_gradient(first, gathered[0], None, feature_all, None, F32)
            inbound, kernel_sum = lax.optimization_barrier((inbound, kernel_sum))

    outs = lax.dynamic_slice_in_dim(jnp.stack(results), section_pos, blocks_n, 0)[::-1]
    outs = outs.reshape(frames_all, rings, rows_l, own, group).transpose(1, 0, 2, 3, 4)
    outs, gathered[-1] = lax.optimization_barrier((outs, gathered[-1]))
    outs = lax.all_to_all(outs, "frame", 0, 0)

    for order in range(1, blocks_n):
        first = (blocks_n - 1 - order) * BLOCK_FRAMES
        out_type = BF16 if order == blocks_n - 1 else F32
        kernel_sum = kernel_gradient(first, gathered[order], gathered[order - 1], feature_all, kernel_sum, out_type)

    outs, kernel_total = lax.optimization_barrier((outs, kernel_sum))
    outs = outs.transpose(4, 1, 2, 0, 3).reshape(group, frames_all, rows_l, width_n)
    return (outs[None], kernel_total[None])


def solution(mesh):
    placed = (
        P("chan", None, "frame", None),
        P("section", None, None, "frame", None),
        P("section", None, "chan", None),
    )
    return jax.shard_map(
        body,
        mesh=mesh,
        in_specs=placed,
        out_specs=(P("section", "chan", None, "frame", None), P("section", None, "chan", None)),
        check_vma=False,
    )
```

```python
import jax
import jax.numpy as jnp
from jax import lax
from jax.experimental import pallas as pl
from jax.experimental.pallas import tpu as pltpu
from jax.sharding import PartitionSpec as P

BLOCK_FRAMES = 2
F32 = jnp.float32
BF16 = jnp.bfloat16


def back_kernel(cur_ref, later_ref, w_ref, out_ref, spread, acc):
    frames_n, rows_n, width_n, group = cur_ref.shape
    empty = jnp.zeros((width_n, 3 * group), F32)
    for frame in range(2 * frames_n):
        spread[frame, 0] = empty
        spread[frame, rows_n + 1] = empty
        for row in range(rows_n):
            source = cur_ref[frame, row] if frame < frames_n else later_ref[frame - frames_n, row]
            cells = source.astype(F32)
            spread[frame, row + 1, :, 0:group] = pltpu.roll(cells, width_n - 1, 0)
            spread[frame, row + 1, :, group : 2 * group] = cells
            spread[frame, row + 1, :, 2 * group : 3 * group] = pltpu.roll(cells, 1, 0)
    for step in range(9):
        lag, offset = step // 3, 2 - step % 3
        taken = spread[lag : lag + frames_n, offset : offset + rows_n]
        taken = taken.reshape(frames_n * rows_n * width_n, 3 * group).astype(BF16)
        part = jnp.dot(
            taken, w_ref[3 * step : 3 * step + 3].reshape(3 * group, -1), preferred_element_type=F32
        )
        if step == 0:
            acc[...] = part
        elif step < 8:
            acc[...] += part
        else:
            out_ref[...] = (acc[...] + part).astype(BF16)


def back_block(current, later, kernels):
    frames_n, rows_n, width_n, group = current.shape
    channels = kernels.shape[2]
    cells = frames_n * rows_n * width_n
    held = pl.BlockSpec(memory_space=pltpu.VMEM)
    return pl.pallas_call(
        back_kernel,
        in_specs=[held, held, held],
        out_specs=held,
        out_shape=jax.ShapeDtypeStruct((cells, channels), BF16),
        scratch_shapes=[
            pltpu.VMEM((2 * frames_n, rows_n + 2, width_n, 3 * group), F32),
            pltpu.VMEM((cells, channels), F32),
        ],
        compiler_params=pltpu.CompilerParams(vmem_limit_bytes=24 * 2**20),
        cost_estimate=pl.CostEstimate(
            flops=54 * group * channels * cells, bytes_accessed=54 * group * channels, transcendentals=0
        ),
    )(current, later, kernels)


def tap_kernel(first, grad_refs, parts_ref, sum_ref, out_ref, cells_ref, sides, feature_ref, g_here, f_here):
    step = pl.program_id(0)
    rings, chans, rows_l, _, width_c = parts_ref.shape
    pieces_n, block, rows_n, own, group = grad_refs[0].shape
    width_n = pieces_n * own
    frames_n = block
    span = frames_n * width_n

    @pl.when(step == 0)
    def _():
        g_copies, f_copies = [], []
        for index, ref in enumerate(grad_refs):
            for piece in range(pieces_n):
                g_copies.append(
                    pltpu.make_async_copy(
                        ref.at[piece],
                        cells_ref.at[pl.ds(index * block, block), :, pl.ds(piece * own, own)],
                        g_here.at[index * pieces_n + piece],
                    )
                )
        for ring in range(rings):
            for chan in range(chans):
                f_copies.append(
                    pltpu.make_async_copy(
                        parts_ref.at[ring, chan, :, pl.ds(first * width_n, span)],
                        feature_ref.at[pl.ds(ring * rows_l, rows_l), :, pl.ds(chan * width_c, width_c)],
                        f_here.at[ring * chans + chan],
                    )
                )
        for copy in g_copies + f_copies:
            copy.start()
        column = lax.broadcasted_iota(jnp.int32, (group, width_n), 1)
        empty = jnp.zeros((3 * group, width_n), BF16)
        for frame in range(frames_n + 2):
            filled = frame < len(grad_refs) * block
            if filled and frame % block == 0:
                for piece in range(pieces_n):
                    g_copies[frame // block * pieces_n + piece].wait()
            for row in range(rows_n + 2):
                start = (row * (frames_n + 2) + frame) * width_n
                if row in (0, rows_n + 1) or not filled:
                    sides[:, start : start + width_n] = empty
                    continue
                cells = cells_ref[frame, row - 1].astype(F32).T
                left = jnp.where(column == width_n - 1, 0.0, pltpu.roll(cells, width_n - 1, 1))
                right = jnp.where(column == 0, 0.0, pltpu.roll(cells, 1, 1))
                sides[0:group, start : start + width_n] = left.astype(BF16)
                sides[group : 2 * group, start : start + width_n] = cells.astype(BF16)
                sides[2 * group : 3 * group, start : start + width_n] = right.astype(BF16)
        for copy in f_copies:
            copy.wait()

    lag = step // 3
    offset = 2 - step % 3
    pieces = []
    for row in range(rows_n):
        start = ((row + offset) * (frames_n + 2) + lag) * width_n
        pieces.append(sides[:, pl.ds(pl.multiple_of(start, 128), span)])
    total = jnp.dot(
        jnp.concatenate(pieces, axis=1),
        feature_ref[...].reshape(rows_n * span, -1),
        preferred_element_type=F32,
    ).reshape(out_ref.shape)
    if sum_ref is not None:
        total = total + sum_ref[...].astype(F32)
    out_ref[...] = total.astype(out_ref.dtype)


def kernel_gradient(first, grads, later, parts, known):
    pieces_n, block, rows_n, own, group = grads.shape
    rings, chans, rows_l, _, width_c = parts.shape
    channels = chans * width_c
    width_n = pieces_n * own
    frames_n = block
    far = pl.BlockSpec(memory_space=pltpu.HBM)
    out_spec = pl.BlockSpec((3, group, channels), lambda step: (step, 0, 0))
    grads = [grads] + ([] if later is None else [later])
    operands = grads + [parts] + ([] if known is None else [known])

    def kernel(*refs):
        inputs, rest = refs[: len(operands)], refs[len(operands) :]
        sum_ref = None if known is None else inputs[-1]
        tap_kernel(first, inputs[: len(grads)], inputs[len(grads)], sum_ref, *rest)

    return pl.pallas_call(
        kernel,
        grid=(9,),
        in_specs=[far] * (len(grads) + 1) + ([] if known is None else [out_spec]),
        out_specs=out_spec,
        out_shape=jax.ShapeDtypeStruct((27, group, channels), BF16),
        scratch_shapes=[
            pltpu.VMEM((len(grads) * block, rows_n, width_n, group), BF16),
            pltpu.VMEM((3 * group, (rows_n + 2) * (frames_n + 2) * width_n), BF16),
            pltpu.VMEM((rows_n, frames_n * width_n, channels), BF16),
            pltpu.SemaphoreType.DMA((len(grads) * pieces_n,)),
            pltpu.SemaphoreType.DMA((rings * chans,)),
        ],
        compiler_params=pltpu.CompilerParams(vmem_limit_bytes=58 * 2**20),
        cost_estimate=pl.CostEstimate(
            flops=54 * group * channels * rows_n * frames_n * width_n,
            bytes_accessed=6 * 27 * group * channels,
            transcendentals=0,
        ),
    )(*operands)


def body(upstream, acts, weights):
    group, frames_all, rows_l, width_n = upstream.shape
    sections, rings, chans = lax.axis_size("section"), lax.axis_size("frame"), lax.axis_size("chan")
    section_pos, ring_pos, chan_pos = lax.axis_index("section"), lax.axis_index("frame"), lax.axis_index("chan")
    rows_n = rows_l * rings
    own = width_n // rings
    halo = sections
    window = own + 2 * halo
    blocks_n = frames_all // BLOCK_FRAMES
    assert blocks_n == sections
    half = frames_all // 2
    ticks = blocks_n + sections - 1
    kernels = weights[0]

    def to_columns(cells):
        wide = jnp.pad(cells, [(0, 0)] * (cells.ndim - 2) + [(halo, halo), (0, 0)])
        pieces = jnp.stack([wide[..., own * i : own * i + window, :] for i in range(rings)])
        pieces = lax.all_to_all(pieces, "frame", 0, 0)
        pieces = jnp.moveaxis(pieces, 0, -4)
        return pieces.reshape(cells.shape[:-3] + (rows_n, window, group))

    mine = lax.dynamic_slice_in_dim(acts[0], chan_pos * group, group, 0)
    top = frames_all - BLOCK_FRAMES
    relayed = lax.dynamic_slice_in_dim(upstream, (blocks_n - 1 - section_pos) * BLOCK_FRAMES, BLOCK_FRAMES, 1)
    pair = to_columns(jnp.stack([relayed, mine[:, top:]]).transpose(0, 2, 3, 4, 1))
    relayed = pair[0]
    rest = to_columns(mine[:, :top].transpose(1, 2, 3, 0))
    stored = [pair[1]]
    for order in range(1, blocks_n):
        first = top - order * BLOCK_FRAMES
        stored.append(rest[first : first + BLOCK_FRAMES])

    shared = group % 128 == 0
    mine, acts, stored[-1] = lax.optimization_barrier((mine, acts, stored[-1]))
    values = (mine if shared else acts[0]).astype(F32)
    feature_part = (values * jax.nn.sigmoid(values)).astype(BF16).transpose(2, 1, 3, 0)
    feature_part = feature_part.reshape(rows_l, frames_all * width_n, -1)
    feature_all = lax.all_gather(feature_part, ("frame", "chan") if shared else "frame")
    feature_all = feature_all.reshape(rings, chans if shared else 1, *feature_part.shape)

    column = ring_pos * own - halo + jnp.arange(window)
    inside = jnp.logical_and(column >= 0, column < width_n)[None, None, :, None]
    later = jnp.zeros((BLOCK_FRAMES, rows_n, window, group), BF16)
    current = jnp.where(section_pos == 0, relayed, later)
    held, gathered, results = [], [], []
    for tick in range(ticks):
        if tick == ticks - 2:
            current, feature_all = lax.optimization_barrier((current, feature_all))
        held.append(current[:, :, halo : halo + own])
        if tick in (ticks - 1 - blocks_n // 2, ticks - 1):
            begin = len(gathered) * (blocks_n // 2)
            taken = jnp.stack(held[begin:])
            taken = lax.dynamic_slice_in_dim(taken, section_pos, blocks_n // 2, 0)[::-1]
            if not gathered:
                taken, feature_all = lax.optimization_barrier((taken, feature_all))
            gathered.append(lax.all_gather(taken.reshape(half, rows_n, own, group), "frame"))
        partial = back_block(current, later, kernels)
        summed = lax.dynamic_slice_in_dim(partial, chan_pos * group, group, 1).astype(F32)
        for step in range(1, chans):
            there = lax.rem(chan_pos + step, chans)
            piece = lax.dynamic_slice_in_dim(partial, there * group, group, 1)
            arrived = lax.ppermute(piece, "chan", [(i, (i + step) % chans) for i in range(chans)])
            summed = summed + arrived.astype(F32)
        known = jnp.stack(stored[: tick + 1])
        place = jnp.clip(tick - section_pos, 0, known.shape[0] - 1)
        slot = lax.dynamic_index_in_dim(known, place, 0, keepdims=False).astype(F32)
        logistic = jax.nn.sigmoid(slot)
        slope = logistic * (1.0 + slot * (1.0 - logistic))
        updated = current.astype(F32) + slope * summed.reshape(current.shape)
        updated = jnp.where(inside, updated, 0.0).astype(BF16)
        results.append(updated[:, :, halo : halo + own])
        later = current
        if tick + 1 < ticks:
            pairs = [(i, i + 1) for i in range(sections - 1) if i <= tick < i + blocks_n]
            if tick + 1 < sections:
                updated = jnp.where(section_pos == tick + 1, relayed, updated)
                pairs.append((tick + 1, 0))
            current = lax.ppermute(updated, "section", pairs)

    if own % 16:
        gathered = [
            block.transpose(1, 2, 0, 3, 4).reshape(1, half, rows_n, width_n, group) for block in gathered
        ]
    kernel_sum = kernel_gradient(half, gathered[0], None, feature_all, None)

    outs = lax.dynamic_slice_in_dim(jnp.stack(results), section_pos, blocks_n, 0)[::-1]
    outs = outs.reshape(frames_all, rings, rows_l, own, group).transpose(1, 0, 2, 3, 4)
    outs, kernel_sum = lax.optimization_barrier((outs, kernel_sum))
    outs = lax.all_to_all(outs, "frame", 0, 0)
    kernel_total = kernel_gradient(0, gathered[1], gathered[0], feature_all, kernel_sum)
    outs, kernel_total = lax.optimization_barrier((outs, kernel_total))
    outs = outs.transpose(4, 1, 2, 0, 3).reshape(group, frames_all, rows_l, width_n)
    return (outs[None], kernel_total[None])


def solution(mesh):
    placed = (
        P("chan", None, "frame", None),
        P("section", None, None, "frame", None),
        P("section", None, "chan", None),
    )
    return jax.shard_map(
        body,
        mesh=mesh,
        in_specs=placed,
        out_specs=(P("section", "chan", None, "frame", None), P("section", None, "chan", None)),
        check_vma=False,
    )
```

```python
import jax
import jax.numpy as jnp
from jax import lax
from jax.experimental import pallas as pl
from jax.experimental.pallas import tpu as pltpu
from jax.sharding import PartitionSpec as P

BLOCK_FRAMES = 2
F32 = jnp.float32
BF16 = jnp.bfloat16


def back_kernel(cur_ref, later_ref, w_ref, out_ref, spread, acc):
    frames_n, rows_n, width_n, group = cur_ref.shape
    empty = jnp.zeros((width_n, 3 * group), F32)
    for frame in range(2 * frames_n):
        spread[frame, 0] = empty
        spread[frame, rows_n + 1] = empty
        for row in range(rows_n):
            source = cur_ref[frame, row] if frame < frames_n else later_ref[frame - frames_n, row]
            cells = source.astype(F32)
            spread[frame, row + 1, :, 0:group] = pltpu.roll(cells, width_n - 1, 0)
            spread[frame, row + 1, :, group : 2 * group] = cells
            spread[frame, row + 1, :, 2 * group : 3 * group] = pltpu.roll(cells, 1, 0)
    for step in range(9):
        lag, offset = step // 3, 2 - step % 3
        taken = spread[lag : lag + frames_n, offset : offset + rows_n]
        taken = taken.reshape(frames_n * rows_n * width_n, 3 * group).astype(BF16)
        part = jnp.dot(
            taken, w_ref[3 * step : 3 * step + 3].reshape(3 * group, -1), preferred_element_type=F32
        )
        if step == 0:
            acc[...] = part
        elif step < 8:
            acc[...] += part
        else:
            out_ref[...] = (acc[...] + part).astype(BF16)


def back_block(current, later, kernels):
    frames_n, rows_n, width_n, group = current.shape
    channels = kernels.shape[2]
    cells = frames_n * rows_n * width_n
    held = pl.BlockSpec(memory_space=pltpu.VMEM)
    return pl.pallas_call(
        back_kernel,
        in_specs=[held, held, held],
        out_specs=held,
        out_shape=jax.ShapeDtypeStruct((cells, channels), BF16),
        scratch_shapes=[
            pltpu.VMEM((2 * frames_n, rows_n + 2, width_n, 3 * group), F32),
            pltpu.VMEM((cells, channels), F32),
        ],
        compiler_params=pltpu.CompilerParams(vmem_limit_bytes=24 * 2**20),
        cost_estimate=pl.CostEstimate(
            flops=54 * group * channels * cells, bytes_accessed=54 * group * channels, transcendentals=0
        ),
    )(current, later, kernels)


def tap_kernel(first, grad_refs, parts_ref, sum_ref, out_ref, cells_ref, sides, feature_ref, g_here, f_here):
    step = pl.program_id(0)
    rings, chans, rows_l, _, width_c = parts_ref.shape
    pieces_n, block, rows_n, own, group = grad_refs[0].shape
    width_n = pieces_n * own
    frames_n = block
    span = frames_n * width_n

    @pl.when(step == 0)
    def _():
        g_copies, f_copies = [], []
        for index, ref in enumerate(grad_refs):
            for piece in range(pieces_n):
                g_copies.append(
                    pltpu.make_async_copy(
                        ref.at[piece],
                        cells_ref.at[pl.ds(index * block, block), :, pl.ds(piece * own, own)],
                        g_here.at[index * pieces_n + piece],
                    )
                )
        for ring in range(rings):
            for chan in range(chans):
                f_copies.append(
                    pltpu.make_async_copy(
                        parts_ref.at[ring, chan, :, pl.ds(first * width_n, span)],
                        feature_ref.at[pl.ds(ring * rows_l, rows_l), :, pl.ds(chan * width_c, width_c)],
                        f_here.at[ring * chans + chan],
                    )
                )
        for copy in g_copies + f_copies:
            copy.start()
        column = lax.broadcasted_iota(jnp.int32, (group, width_n), 1)
        empty = jnp.zeros((3 * group, width_n), BF16)
        for frame in range(frames_n + 2):
            filled = frame < len(grad_refs) * block
            if filled and frame % block == 0:
                for piece in range(pieces_n):
                    g_copies[frame // block * pieces_n + piece].wait()
            for row in range(rows_n + 2):
                start = (row * (frames_n + 2) + frame) * width_n
                if row in (0, rows_n + 1) or not filled:
                    sides[:, start : start + width_n] = empty
                    continue
                cells = cells_ref[frame, row - 1].astype(F32).T
                left = jnp.where(column == width_n - 1, 0.0, pltpu.roll(cells, width_n - 1, 1))
                right = jnp.where(column == 0, 0.0, pltpu.roll(cells, 1, 1))
                sides[0:group, start : start + width_n] = left.astype(BF16)
                sides[group : 2 * group, start : start + width_n] = cells.astype(BF16)
                sides[2 * group : 3 * group, start : start + width_n] = right.astype(BF16)
        for copy in f_copies:
            copy.wait()

    lag = step // 3
    offset = 2 - step % 3
    pieces = []
    for row in range(rows_n):
        start = ((row + offset) * (frames_n + 2) + lag) * width_n
        pieces.append(sides[:, pl.ds(pl.multiple_of(start, 128), span)])
    total = jnp.dot(
        jnp.concatenate(pieces, axis=1),
        feature_ref[...].reshape(rows_n * span, -1),
        preferred_element_type=F32,
    ).reshape(out_ref.shape)
    if sum_ref is not None:
        total = total + sum_ref[...].astype(F32)
    out_ref[...] = total.astype(out_ref.dtype)


def kernel_gradient(first, grads, later, parts, known):
    pieces_n, block, rows_n, own, group = grads.shape
    rings, chans, rows_l, _, width_c = parts.shape
    channels = chans * width_c
    width_n = pieces_n * own
    frames_n = block
    far = pl.BlockSpec(memory_space=pltpu.HBM)
    out_spec = pl.BlockSpec((3, group, channels), lambda step: (step, 0, 0))
    grads = [grads] + ([] if later is None else [later])
    operands = grads + [parts] + ([] if known is None else [known])

    def kernel(*refs):
        inputs, rest = refs[: len(operands)], refs[len(operands) :]
        sum_ref = None if known is None else inputs[-1]
        tap_kernel(first, inputs[: len(grads)], inputs[len(grads)], sum_ref, *rest)

    return pl.pallas_call(
        kernel,
        grid=(9,),
        in_specs=[far] * (len(grads) + 1) + ([] if known is None else [out_spec]),
        out_specs=out_spec,
        out_shape=jax.ShapeDtypeStruct((27, group, channels), BF16),
        scratch_shapes=[
            pltpu.VMEM((len(grads) * block, rows_n, width_n, group), BF16),
            pltpu.VMEM((3 * group, (rows_n + 2) * (frames_n + 2) * width_n), BF16),
            pltpu.VMEM((rows_n, frames_n * width_n, channels), BF16),
            pltpu.SemaphoreType.DMA((len(grads) * pieces_n,)),
            pltpu.SemaphoreType.DMA((rings * chans,)),
        ],
        compiler_params=pltpu.CompilerParams(vmem_limit_bytes=58 * 2**20),
        cost_estimate=pl.CostEstimate(
            flops=54 * group * channels * rows_n * frames_n * width_n,
            bytes_accessed=6 * 27 * group * channels,
            transcendentals=0,
        ),
    )(*operands)


def body(upstream, acts, weights):
    group, frames_all, rows_l, width_n = upstream.shape
    sections, rings, chans = lax.axis_size("section"), lax.axis_size("frame"), lax.axis_size("chan")
    section_pos, ring_pos, chan_pos = lax.axis_index("section"), lax.axis_index("frame"), lax.axis_index("chan")
    rows_n = rows_l * rings
    own = width_n // rings
    halo = sections
    window = own + 2 * halo
    blocks_n = frames_all // BLOCK_FRAMES
    assert blocks_n == sections
    half = frames_all // 2
    ticks = blocks_n + sections - 1
    kernels = weights[0]

    def to_columns(cells):
        wide = jnp.pad(cells, [(0, 0)] * (cells.ndim - 2) + [(halo, halo), (0, 0)])
        pieces = jnp.stack([wide[..., own * i : own * i + window, :] for i in range(rings)])
        pieces = lax.all_to_all(pieces, "frame", 0, 0)
        pieces = jnp.moveaxis(pieces, 0, -4)
        return pieces.reshape(cells.shape[:-3] + (rows_n, window, group))

    mine = lax.dynamic_slice_in_dim(acts[0], chan_pos * group, group, 0)
    top = frames_all - BLOCK_FRAMES
    relayed = lax.dynamic_slice_in_dim(upstream, (blocks_n - 1 - section_pos) * BLOCK_FRAMES, BLOCK_FRAMES, 1)
    pair = to_columns(jnp.stack([relayed, mine[:, top:]]).transpose(0, 2, 3, 4, 1))
    relayed = pair[0]
    rest = to_columns(mine[:, :top].transpose(1, 2, 3, 0))
    stored = [pair[1]]
    for order in range(1, blocks_n):
        first = top - order * BLOCK_FRAMES
        stored.append(rest[first : first + BLOCK_FRAMES])

    shared = group % 128 == 0
    mine, acts, stored[0] = lax.optimization_barrier((mine, acts, stored[0]))
    values = (mine if shared else acts[0]).astype(F32)
    feature_part = (values * jax.nn.sigmoid(values)).astype(BF16).transpose(2, 1, 3, 0)
    feature_part = feature_part.reshape(rows_l, frames_all * width_n, -1)
    feature_all = lax.all_gather(feature_part, ("frame", "chan") if shared else "frame")
    feature_all = feature_all.reshape(rings, chans if shared else 1, *feature_part.shape)

    column = ring_pos * own - halo + jnp.arange(window)
    inside = jnp.logical_and(column >= 0, column < width_n)[None, None, :, None]
    later = jnp.zeros((BLOCK_FRAMES, rows_n, window, group), BF16)
    current = jnp.where(section_pos == 0, relayed, later)
    held, gathered, results = [], [], []
    for tick in range(ticks):
        if tick == ticks - 1 - blocks_n // 2:
            current, feature_all = lax.optimization_barrier((current, feature_all))
        held.append(current[:, :, halo : halo + own])
        if tick in (ticks - 1 - blocks_n // 2, ticks - 1):
            begin = len(gathered) * (blocks_n // 2)
            taken = jnp.stack(held[begin:])
            taken = lax.dynamic_slice_in_dim(taken, section_pos, blocks_n // 2, 0)[::-1]
            taken, current = lax.optimization_barrier((taken, current))
            gathered.append(lax.all_gather(taken.reshape(half, rows_n, own, group), "frame"))
        partial = back_block(current, later, kernels)
        summed = lax.dynamic_slice_in_dim(partial, chan_pos * group, group, 1).astype(F32)
        for step in range(1, chans):
            there = lax.rem(chan_pos + step, chans)
            piece = lax.dynamic_slice_in_dim(partial, there * group, group, 1)
            arrived = lax.ppermute(piece, "chan", [(i, (i + step) % chans) for i in range(chans)])
            summed = summed + arrived.astype(F32)
        known = jnp.stack(stored[: tick + 1])
        place = jnp.clip(tick - section_pos, 0, known.shape[0] - 1)
        slot = lax.dynamic_index_in_dim(known, place, 0, keepdims=False).astype(F32)
        logistic = jax.nn.sigmoid(slot)
        slope = logistic * (1.0 + slot * (1.0 - logistic))
        updated = current.astype(F32) + slope * summed.reshape(current.shape)
        updated = jnp.where(inside, updated, 0.0).astype(BF16)
        results.append(updated[:, :, halo : halo + own])
        later = current
        if tick + 1 < ticks:
            pairs = [(i, i + 1) for i in range(sections - 1) if i <= tick < i + blocks_n]
            if tick + 1 < sections:
                updated = jnp.where(section_pos == tick + 1, relayed, updated)
                pairs.append((tick + 1, 0))
            current = lax.ppermute(updated, "section", pairs)

    if own % 16:
        gathered = [
            block.transpose(1, 2, 0, 3, 4).reshape(1, half, rows_n, width_n, group) for block in gathered
        ]
    kernel_sum = kernel_gradient(half, gathered[0], None, feature_all, None)

    outs = lax.dynamic_slice_in_dim(jnp.stack(results), section_pos, blocks_n, 0)[::-1]
    outs = outs.reshape(frames_all, rings, rows_l, own, group).transpose(1, 0, 2, 3, 4)
    outs, kernel_sum = lax.optimization_barrier((outs, kernel_sum))
    outs = lax.all_to_all(outs, "frame", 0, 0)
    kernel_total = kernel_gradient(0, gathered[1], gathered[0], feature_all, kernel_sum)
    outs, kernel_total = lax.optimization_barrier((outs, kernel_total))
    outs = outs.transpose(4, 1, 2, 0, 3).reshape(group, frames_all, rows_l, width_n)
    return (outs[None], kernel_total[None])


def solution(mesh):
    placed = (
        P("chan", None, "frame", None),
        P("section", None, None, "frame", None),
        P("section", None, "chan", None),
    )
    return jax.shard_map(
        body,
        mesh=mesh,
        in_specs=placed,
        out_specs=(P("section", "chan", None, "frame", None), P("section", None, "chan", None)),
        check_vma=False,
    )
```

```python
import jax
import jax.numpy as jnp
from jax import lax
from jax.experimental import pallas as pl
from jax.experimental.pallas import tpu as pltpu
from jax.sharding import PartitionSpec as P

BLOCK_FRAMES = 2
F32 = jnp.float32
BF16 = jnp.bfloat16


def back_kernel(cur_ref, later_ref, w_ref, out_ref, spread, acc):
    frames_n, rows_n, width_n, group = cur_ref.shape
    empty = jnp.zeros((width_n, 3 * group), F32)
    for frame in range(2 * frames_n):
        spread[frame, 0] = empty
        spread[frame, rows_n + 1] = empty
        for row in range(rows_n):
            source = cur_ref[frame, row] if frame < frames_n else later_ref[frame - frames_n, row]
            cells = source.astype(F32)
            spread[frame, row + 1, :, 0:group] = pltpu.roll(cells, width_n - 1, 0)
            spread[frame, row + 1, :, group : 2 * group] = cells
            spread[frame, row + 1, :, 2 * group : 3 * group] = pltpu.roll(cells, 1, 0)
    for step in range(9):
        lag, offset = step // 3, 2 - step % 3
        taken = spread[lag : lag + frames_n, offset : offset + rows_n]
        taken = taken.reshape(frames_n * rows_n * width_n, 3 * group).astype(BF16)
        part = jnp.dot(
            taken, w_ref[3 * step : 3 * step + 3].reshape(3 * group, -1), preferred_element_type=F32
        )
        if step == 0:
            acc[...] = part
        elif step < 8:
            acc[...] += part
        else:
            out_ref[...] = (acc[...] + part).astype(BF16)


def back_block(current, later, kernels):
    frames_n, rows_n, width_n, group = current.shape
    channels = kernels.shape[2]
    cells = frames_n * rows_n * width_n
    held = pl.BlockSpec(memory_space=pltpu.VMEM)
    return pl.pallas_call(
        back_kernel,
        in_specs=[held, held, held],
        out_specs=held,
        out_shape=jax.ShapeDtypeStruct((cells, channels), BF16),
        scratch_shapes=[
            pltpu.VMEM((2 * frames_n, rows_n + 2, width_n, 3 * group), F32),
            pltpu.VMEM((cells, channels), F32),
        ],
        compiler_params=pltpu.CompilerParams(vmem_limit_bytes=24 * 2**20),
        cost_estimate=pl.CostEstimate(
            flops=54 * group * channels * cells, bytes_accessed=54 * group * channels, transcendentals=0
        ),
    )(current, later, kernels)


def tap_kernel(first, grad_refs, parts_ref, sum_ref, out_ref, cells_ref, sides, feature_ref, g_here, f_here):
    step = pl.program_id(0)
    rings, chans, rows_l, _, width_c = parts_ref.shape
    pieces_n, block, rows_n, own, group = grad_refs[0].shape
    width_n = pieces_n * own
    frames_n = block
    span = frames_n * width_n

    @pl.when(step == 0)
    def _():
        g_copies, f_copies = [], []
        for index, ref in enumerate(grad_refs):
            count = block if index == 0 else 2
            for piece in range(pieces_n):
                g_copies.append(
                    pltpu.make_async_copy(
                        ref.at[piece, pl.ds(0, count)],
                        cells_ref.at[pl.ds(index * block, count), :, pl.ds(piece * own, own)],
                        g_here.at[index * pieces_n + piece],
                    )
                )
        for ring in range(rings):
            for chan in range(chans):
                f_copies.append(
                    pltpu.make_async_copy(
                        parts_ref.at[ring, chan, :, pl.ds(first * width_n, span)],
                        feature_ref.at[pl.ds(ring * rows_l, rows_l), :, pl.ds(chan * width_c, width_c)],
                        f_here.at[ring * chans + chan],
                    )
                )
        for copy in g_copies + f_copies:
            copy.start()
        same = lax.broadcasted_iota(jnp.int32, (group, group), 0) == lax.broadcasted_iota(jnp.int32, (group, group), 1)
        identity = jnp.where(same, 1.0, 0.0).astype(BF16)
        source = lax.broadcasted_iota(jnp.int32, (width_n, 2 * width_n), 0)
        target = lax.broadcasted_iota(jnp.int32, (width_n, 2 * width_n), 1)
        moved = (source == target + 1) & (target < width_n) | (source == target - width_n - 1)
        shifts = jnp.where(moved, 1.0, 0.0).astype(BF16)
        empty = jnp.zeros((3 * group, width_n), BF16)
        for frame in range(frames_n + 2):
            filled = frame < len(grad_refs) * block
            if filled and frame in (0, frames_n):
                for piece in range(pieces_n):
                    g_copies[frame // block * pieces_n + piece].wait()
            if filled:
                turned = lax.dot_general(
                    identity,
                    cells_ref[frame].reshape(rows_n * width_n, group),
                    (((1,), (1,)), ((), ())),
                    preferred_element_type=F32,
                ).astype(BF16)
            for row in range(rows_n + 2):
                start = (row * (frames_n + 2) + frame) * width_n
                if row in (0, rows_n + 1) or not filled:
                    sides[:, start : start + width_n] = empty
                    continue
                cells = turned[:, (row - 1) * width_n : row * width_n]
                both = jnp.dot(cells, shifts, preferred_element_type=F32).astype(BF16)
                sides[0:group, start : start + width_n] = both[:, :width_n]
                sides[group : 2 * group, start : start + width_n] = cells
                sides[2 * group : 3 * group, start : start + width_n] = both[:, width_n:]
        for copy in f_copies:
            copy.wait()

    lag = step // 3
    offset = 2 - step % 3
    pieces = []
    for row in range(rows_n):
        start = ((row + offset) * (frames_n + 2) + lag) * width_n
        pieces.append(sides[:, pl.ds(pl.multiple_of(start, 128), span)])
    total = jnp.dot(
        jnp.concatenate(pieces, axis=1),
        feature_ref[...].reshape(rows_n * span, -1),
        preferred_element_type=F32,
    ).reshape(out_ref.shape)
    if sum_ref is not None:
        total = total + sum_ref[...].astype(F32)
    out_ref[...] = total.astype(out_ref.dtype)


def kernel_gradient(first, grads, later, parts, known):
    pieces_n, block, rows_n, own, group = grads.shape
    rings, chans, rows_l, _, width_c = parts.shape
    channels = chans * width_c
    width_n = pieces_n * own
    frames_n = block
    far = pl.BlockSpec(memory_space=pltpu.HBM)
    out_spec = pl.BlockSpec((3, group, channels), lambda step: (step, 0, 0))
    grads = [grads] + ([] if later is None else [later])
    operands = grads + [parts] + ([] if known is None else [known])

    def kernel(*refs):
        inputs, rest = refs[: len(operands)], refs[len(operands) :]
        sum_ref = None if known is None else inputs[-1]
        tap_kernel(first, inputs[: len(grads)], inputs[len(grads)], sum_ref, *rest)

    return pl.pallas_call(
        kernel,
        grid=(9,),
        in_specs=[far] * (len(grads) + 1) + ([] if known is None else [out_spec]),
        out_specs=out_spec,
        out_shape=jax.ShapeDtypeStruct((27, group, channels), BF16),
        scratch_shapes=[
            pltpu.VMEM((frames_n + 2, rows_n, width_n, group), BF16),
            pltpu.VMEM((3 * group, (rows_n + 2) * (frames_n + 2) * width_n), BF16),
            pltpu.VMEM((rows_n, frames_n * width_n, channels), BF16),
            pltpu.SemaphoreType.DMA((len(grads) * pieces_n,)),
            pltpu.SemaphoreType.DMA((rings * chans,)),
        ],
        compiler_params=pltpu.CompilerParams(vmem_limit_bytes=58 * 2**20),
        cost_estimate=pl.CostEstimate(
            flops=54 * group * channels * rows_n * frames_n * width_n,
            bytes_accessed=6 * 27 * group * channels,
            transcendentals=0,
        ),
    )(*operands)


def body(upstream, acts, weights):
    group, frames_all, rows_l, width_n = upstream.shape
    sections, rings, chans = lax.axis_size("section"), lax.axis_size("frame"), lax.axis_size("chan")
    section_pos, ring_pos, chan_pos = lax.axis_index("section"), lax.axis_index("frame"), lax.axis_index("chan")
    rows_n = rows_l * rings
    own = width_n // rings
    halo = sections
    window = own + 2 * halo
    blocks_n = frames_all // BLOCK_FRAMES
    assert blocks_n == sections
    half = frames_all // 2
    ticks = blocks_n + sections - 1
    kernels = weights[0]

    def to_columns(cells):
        wide = jnp.pad(cells, [(0, 0)] * (cells.ndim - 2) + [(halo, halo), (0, 0)])
        pieces = jnp.stack([wide[..., own * i : own * i + window, :] for i in range(rings)])
        pieces = lax.all_to_all(pieces, "frame", 0, 0)
        pieces = jnp.moveaxis(pieces, 0, -4)
        return pieces.reshape(cells.shape[:-3] + (rows_n, window, group))

    mine = lax.dynamic_slice_in_dim(acts[0], chan_pos * group, group, 0)
    top = frames_all - BLOCK_FRAMES
    relayed = lax.dynamic_slice_in_dim(upstream, (blocks_n - 1 - section_pos) * BLOCK_FRAMES, BLOCK_FRAMES, 1)
    pair = to_columns(jnp.stack([relayed, mine[:, top:]]).transpose(0, 2, 3, 4, 1))
    relayed = pair[0]
    rest = to_columns(mine[:, :top].transpose(1, 2, 3, 0))
    stored = [pair[1]]
    for order in range(1, blocks_n):
        first = top - order * BLOCK_FRAMES
        stored.append(rest[first : first + BLOCK_FRAMES])

    shared = group % 128 == 0
    values = (mine if shared else acts[0]).astype(F32)
    feature_part = (values * jax.nn.sigmoid(values)).astype(BF16).transpose(2, 1, 3, 0)
    feature_part = feature_part.reshape(rows_l, frames_all * width_n, -1)

    column = ring_pos * own - halo + jnp.arange(window)
    inside = jnp.logical_and(column >= 0, column < width_n)[None, None, :, None]
    later = jnp.zeros((BLOCK_FRAMES, rows_n, window, group), BF16)
    current = jnp.where(section_pos == 0, relayed, later)
    held, gathered, results = [], [], []
    for tick in range(ticks):
        if tick == 1:
            feature_part, current, stored[-1] = lax.optimization_barrier((feature_part, current, stored[-1]))
            feature_all = lax.all_gather(feature_part, ("frame", "chan") if shared else "frame")
            feature_all = feature_all.reshape(rings, chans if shared else 1, *feature_part.shape)
        if tick == ticks - 2:
            current, feature_all = lax.optimization_barrier((current, feature_all))
        held.append(current[:, :, halo : halo + own])
        if tick in (ticks - 1 - blocks_n // 2, ticks - 1):
            begin = len(gathered) * (blocks_n // 2)
            taken = jnp.stack(held[begin:])
            taken = lax.dynamic_slice_in_dim(taken, section_pos, blocks_n // 2, 0)[::-1]
            taken, current = lax.optimization_barrier((taken, current))
            gathered.append(lax.all_gather(taken.reshape(half, rows_n, own, group), "frame"))
        partial = back_block(current, later, kernels)
        if tick == ticks - 1:
            partial, gathered[0] = lax.optimization_barrier((partial, gathered[0]))
        summed = lax.dynamic_slice_in_dim(partial, chan_pos * group, group, 1).astype(F32)
        for step in range(1, chans):
            there = lax.rem(chan_pos + step, chans)
            piece = lax.dynamic_slice_in_dim(partial, there * group, group, 1)
            arrived = lax.ppermute(piece, "chan", [(i, (i + step) % chans) for i in range(chans)])
            summed = summed + arrived.astype(F32)
        known = jnp.stack(stored[: tick + 1])
        place = jnp.clip(tick - section_pos, 0, known.shape[0] - 1)
        slot = lax.dynamic_index_in_dim(known, place, 0, keepdims=False).astype(F32)
        logistic = jax.nn.sigmoid(slot)
        slope = logistic * (1.0 + slot * (1.0 - logistic))
        updated = current.astype(F32) + slope * summed.reshape(current.shape)
        updated = jnp.where(inside, updated, 0.0).astype(BF16)
        results.append(updated[:, :, halo : halo + own])
        later = current
        if tick + 1 < ticks:
            pairs = [(i, i + 1) for i in range(sections - 1) if i <= tick < i + blocks_n]
            if tick + 1 < sections:
                updated = jnp.where(section_pos == tick + 1, relayed, updated)
                pairs.append((tick + 1, 0))
            current = lax.ppermute(updated, "section", pairs)

    if own % 16:
        gathered = [
            block.transpose(1, 2, 0, 3, 4).reshape(1, half, rows_n, width_n, group) for block in gathered
        ]
    kernel_sum = kernel_gradient(half, gathered[0], None, feature_all, None)

    outs = lax.dynamic_slice_in_dim(jnp.stack(results), section_pos, blocks_n, 0)[::-1]
    outs = outs.reshape(frames_all, rings, rows_l, own, group).transpose(1, 0, 2, 3, 4)
    outs, kernel_sum = lax.optimization_barrier((outs, kernel_sum))
    outs = lax.all_to_all(outs, "frame", 0, 0)
    kernel_total = kernel_gradient(0, gathered[1], gathered[0], feature_all, kernel_sum)
    outs, kernel_total = lax.optimization_barrier((outs, kernel_total))
    outs = outs.transpose(4, 1, 2, 0, 3).reshape(group, frames_all, rows_l, width_n)
    return (outs[None], kernel_total[None])


def solution(mesh):
    placed = (
        P("chan", None, "frame", None),
        P("section", None, None, "frame", None),
        P("section", None, "chan", None),
    )
    return jax.shard_map(
        body,
        mesh=mesh,
        in_specs=placed,
        out_specs=(P("section", "chan", None, "frame", None), P("section", None, "chan", None)),
        check_vma=False,
    )
```

```python
import functools

import jax
import jax.numpy as jnp
from jax import lax
from jax.experimental import pallas as pl
from jax.experimental.pallas import tpu as pltpu
from jax.sharding import PartitionSpec as P

BLOCK_FRAMES = 2
F32 = jnp.float32
BF16 = jnp.bfloat16


def back_kernel(cur_ref, later_ref, w_ref, out_ref, spread, acc):
    frames_n, rows_n, width_n, group = cur_ref.shape
    empty = jnp.zeros((width_n, 3 * group), F32)
    for frame in range(2 * frames_n):
        spread[frame, 0] = empty
        spread[frame, rows_n + 1] = empty
        for row in range(rows_n):
            source = cur_ref[frame, row] if frame < frames_n else later_ref[frame - frames_n, row]
            cells = source.astype(F32)
            spread[frame, row + 1, :, 0:group] = pltpu.roll(cells, width_n - 1, 0)
            spread[frame, row + 1, :, group : 2 * group] = cells
            spread[frame, row + 1, :, 2 * group : 3 * group] = pltpu.roll(cells, 1, 0)
    for step in range(9):
        lag, offset = step // 3, 2 - step % 3
        taken = spread[lag : lag + frames_n, offset : offset + rows_n]
        taken = taken.reshape(frames_n * rows_n * width_n, 3 * group).astype(BF16)
        part = jnp.dot(
            taken, w_ref[3 * step : 3 * step + 3].reshape(3 * group, -1), preferred_element_type=F32
        )
        if step == 0:
            acc[...] = part
        elif step < 8:
            acc[...] += part
        else:
            out_ref[...] = (acc[...] + part).astype(BF16)


def back_block(current, later, kernels):
    frames_n, rows_n, width_n, group = current.shape
    channels = kernels.shape[2]
    cells = frames_n * rows_n * width_n
    held = pl.BlockSpec(memory_space=pltpu.VMEM)
    return pl.pallas_call(
        back_kernel,
        in_specs=[held, held, held],
        out_specs=held,
        out_shape=jax.ShapeDtypeStruct((cells, channels), BF16),
        scratch_shapes=[
            pltpu.VMEM((2 * frames_n, rows_n + 2, width_n, 3 * group), F32),
            pltpu.VMEM((cells, channels), F32),
        ],
        compiler_params=pltpu.CompilerParams(vmem_limit_bytes=24 * 2**20),
        cost_estimate=pl.CostEstimate(
            flops=54 * group * channels * cells, bytes_accessed=54 * group * channels, transcendentals=0
        ),
    )(current, later, kernels)


def tap_kernel(first, f_first, has_sum, *refs):
    ring_ref, parts_ref, *refs = refs
    sum_ref = refs.pop(0) if has_sum else None
    out_ref, cells_ref, sides, feature_ref, g_here, f_here = refs[-6:]
    grad_refs = refs[:-6]
    step = pl.program_id(0)
    frames_n, rows_n, width_n, group = cells_ref.shape
    pieces_n, block, _, own, _ = grad_refs[0].shape
    arrays_n = width_n // (pieces_n * own)
    rings, chans, rows_l, _, width_c = parts_ref.shape
    held_n = feature_ref.shape[1] // width_n

    @pl.when(step == 0)
    def _():
        g_copies, f_copies = [], []
        for index, ref in enumerate(grad_refs):
            frames = pl.ds(index // arrays_n * block, block)
            for piece in range(pieces_n):
                place = piece * own
                if arrays_n > 1:
                    place = lax.rem(ring_ref[0] + arrays_n - index % arrays_n, arrays_n) * own
                    place = pl.multiple_of(place, own)
                g_copies.append(
                    pltpu.make_async_copy(
                        ref.at[piece],
                        cells_ref.at[frames, :, pl.ds(place, own)],
                        g_here.at[index * pieces_n + piece],
                    )
                )
        for ring in range(rings):
            for chan in range(chans):
                f_copies.append(
                    pltpu.make_async_copy(
                        parts_ref.at[ring, chan, :, pl.ds(f_first * width_n, held_n * width_n)],
                        feature_ref.at[pl.ds(ring * rows_l, rows_l), :, pl.ds(chan * width_c, width_c)],
                        f_here.at[ring * chans + chan],
                    )
                )
        for copy in g_copies + f_copies:
            copy.start()
        same = lax.broadcasted_iota(jnp.int32, (group, group), 0) == lax.broadcasted_iota(jnp.int32, (group, group), 1)
        identity = jnp.where(same, 1.0, 0.0).astype(BF16)
        source = lax.broadcasted_iota(jnp.int32, (width_n, 2 * width_n), 0)
        target = lax.broadcasted_iota(jnp.int32, (width_n, 2 * width_n), 1)
        moved = (source == target + 1) & (target < width_n) | (source == target - width_n - 1)
        shifts = jnp.where(moved, 1.0, 0.0).astype(BF16)
        edge = jnp.zeros((3 * group, frames_n * width_n), BF16)
        sides[:, 0 : frames_n * width_n] = edge
        sides[:, (rows_n + 1) * frames_n * width_n :] = edge
        for copy in g_copies:
            copy.wait()
        for frame in range(frames_n):
            turned = lax.dot_general(
                identity,
                cells_ref[frame].reshape(rows_n * width_n, group),
                (((1,), (1,)), ((), ())),
                preferred_element_type=F32,
            ).astype(BF16)
            for row in range(rows_n):
                start = ((row + 1) * frames_n + frame) * width_n
                cells = turned[:, row * width_n : (row + 1) * width_n]
                both = jnp.dot(cells, shifts, preferred_element_type=F32).astype(BF16)
                sides[0:group, start : start + width_n] = both[:, :width_n]
                sides[group : 2 * group, start : start + width_n] = cells
                sides[2 * group : 3 * group, start : start + width_n] = both[:, width_n:]
        for copy in f_copies:
            copy.wait()

    offset = 2 - step % 3
    for lag in range(3):

        @pl.when(step // 3 == lag)
        def _():
            skipped = max(0, lag - first)
            span = (frames_n - skipped) * width_n
            low = (first + skipped - lag - f_first) * width_n
            lefts, rights = [], []
            for row in range(rows_n):
                start = ((row + offset) * frames_n + skipped) * width_n
                lefts.append(sides[:, pl.ds(pl.multiple_of(start, 128), span)])
                rights.append(feature_ref[row, low : low + span])
            total = jnp.dot(
                jnp.concatenate(lefts, axis=1), jnp.concatenate(rights, axis=0), preferred_element_type=F32
            ).reshape(out_ref.shape)
            if has_sum:
                total = total + sum_ref[...].astype(F32)
            out_ref[...] = total.astype(out_ref.dtype)


def gather_columns(block, rings):
    frames_n, rows_n, own, group = block.shape
    if rings > 4 or own % 16:
        whole = lax.all_gather(block, "frame")
        if own % 16:
            whole = whole.transpose(1, 2, 0, 3, 4).reshape(1, frames_n, rows_n, rings * own, group)
        return [whole]
    sent = [lax.ppermute(block, "frame", [(i, (i + step) % rings) for i in range(rings)]) for step in range(1, rings)]
    return [piece[None] for piece in [block] + sent]


def kernel_gradient(first, blocks, parts, ring_pos, known):
    pieces_n, block, rows_n, own, group = blocks[0][0].shape
    rings, chans, rows_l, _, width_c = parts.shape
    channels = chans * width_c
    width_n = len(blocks[0]) * pieces_n * own
    frames_n = len(blocks) * block
    grads = [array for arrays in blocks for array in arrays]
    f_first = max(0, first - 2)
    held_n = first + frames_n - f_first
    far = pl.BlockSpec(memory_space=pltpu.HBM)
    out_spec = pl.BlockSpec((3, group, channels), lambda step: (step, 0, 0))
    has_sum = known is not None
    return pl.pallas_call(
        functools.partial(tap_kernel, first, f_first, has_sum),
        grid=(9,),
        in_specs=[pl.BlockSpec(memory_space=pltpu.SMEM), far] + [out_spec] * has_sum + [far] * len(grads),
        out_specs=out_spec,
        out_shape=jax.ShapeDtypeStruct((27, group, channels), BF16),
        scratch_shapes=[
            pltpu.VMEM((frames_n, rows_n, width_n, group), BF16),
            pltpu.VMEM((3 * group, (rows_n + 2) * frames_n * width_n), BF16),
            pltpu.VMEM((rows_n, held_n * width_n, channels), BF16),
            pltpu.SemaphoreType.DMA((len(grads) * pieces_n,)),
            pltpu.SemaphoreType.DMA((rings * chans,)),
        ],
        compiler_params=pltpu.CompilerParams(vmem_limit_bytes=58 * 2**20),
        cost_estimate=pl.CostEstimate(
            flops=54 * group * channels * rows_n * frames_n * width_n,
            bytes_accessed=6 * 27 * group * channels,
            transcendentals=0,
        ),
    )(*([ring_pos.reshape(1), parts] + [known] * has_sum + grads))


def body(upstream, acts, weights):
    group, frames_all, rows_l, width_n = upstream.shape
    sections, rings, chans = lax.axis_size("section"), lax.axis_size("frame"), lax.axis_size("chan")
    section_pos, ring_pos, chan_pos = lax.axis_index("section"), lax.axis_index("frame"), lax.axis_index("chan")
    rows_n = rows_l * rings
    own = width_n // rings
    halo = sections
    window = own + 2 * halo
    blocks_n = frames_all // BLOCK_FRAMES
    assert blocks_n == sections
    half = frames_all // 2
    ticks = blocks_n + sections - 1
    kernels = weights[0]

    def to_columns(cells):
        wide = jnp.pad(cells, [(0, 0)] * (cells.ndim - 2) + [(halo, halo), (0, 0)])
        pieces = jnp.stack([wide[..., own * i : own * i + window, :] for i in range(rings)])
        pieces = lax.all_to_all(pieces, "frame", 0, 0)
        pieces = jnp.moveaxis(pieces, 0, -4)
        return pieces.reshape(cells.shape[:-3] + (rows_n, window, group))

    mine = lax.dynamic_slice_in_dim(acts[0], chan_pos * group, group, 0)
    top = frames_all - BLOCK_FRAMES
    relayed = lax.dynamic_slice_in_dim(upstream, (blocks_n - 1 - section_pos) * BLOCK_FRAMES, BLOCK_FRAMES, 1)
    pair = to_columns(jnp.stack([relayed, mine[:, top:]]).transpose(0, 2, 3, 4, 1))
    relayed = pair[0]
    rest = to_columns(mine[:, :top].transpose(1, 2, 3, 0))
    stored = [pair[1]]
    for order in range(1, blocks_n):
        first = top - order * BLOCK_FRAMES
        stored.append(rest[first : first + BLOCK_FRAMES])

    shared = group % 128 == 0
    values = (mine if shared else acts[0]).astype(F32)
    feature_part = (values * jax.nn.sigmoid(values)).astype(BF16).transpose(2, 1, 3, 0)
    feature_part = feature_part.reshape(rows_l, frames_all * width_n, -1)

    column = ring_pos * own - halo + jnp.arange(window)
    inside = jnp.logical_and(column >= 0, column < width_n)[None, None, :, None]
    later = jnp.zeros((BLOCK_FRAMES, rows_n, window, group), BF16)
    current = jnp.where(section_pos == 0, relayed, later)
    held, gathered, results = [], [], []
    for tick in range(ticks):
        if tick == 1:
            feature_part, current, stored[-1] = lax.optimization_barrier((feature_part, current, stored[-1]))
            feature_all = lax.all_gather(feature_part, ("frame", "chan") if shared else "frame")
            feature_all = feature_all.reshape(rings, chans if shared else 1, *feature_part.shape)
        if tick == ticks - 3:
            current, feature_all = lax.optimization_barrier((current, feature_all))
        held.append(current[:, :, halo : halo + own])
        partial = back_block(current, later, kernels)
        if tick == ticks - 1:
            partial, gathered[0], gathered[2] = lax.optimization_barrier((partial, gathered[0], gathered[2]))
        summed = lax.dynamic_slice_in_dim(partial, chan_pos * group, group, 1).astype(F32)
        for step in range(1, chans):
            there = lax.rem(chan_pos + step, chans)
            piece = lax.dynamic_slice_in_dim(partial, there * group, group, 1)
            arrived = lax.ppermute(piece, "chan", [(i, (i + step) % chans) for i in range(chans)])
            summed = summed + arrived.astype(F32)
        known = jnp.stack(stored[: tick + 1])
        place = jnp.clip(tick - section_pos, 0, known.shape[0] - 1)
        slot = lax.dynamic_index_in_dim(known, place, 0, keepdims=False).astype(F32)
        logistic = jax.nn.sigmoid(slot)
        slope = logistic * (1.0 + slot * (1.0 - logistic))
        updated = current.astype(F32) + slope * summed.reshape(current.shape)
        updated = jnp.where(inside, updated, 0.0).astype(BF16)
        if tick >= sections - 1:
            order = tick - sections + 1
            if order in (1, 2):
                updated, gathered[order - 1] = lax.optimization_barrier((updated, gathered[order - 1]))
            taken = lax.dynamic_index_in_dim(jnp.stack(held[order:]), section_pos, 0, keepdims=False)
            if tick + 1 < ticks:
                taken, updated = lax.optimization_barrier((taken, updated))
            gathered.append(gather_columns(taken, rings))
        results.append(updated[:, :, halo : halo + own])
        later = current
        if tick + 1 < ticks:
            pairs = [(i, i + 1) for i in range(sections - 1) if i <= tick < i + blocks_n]
            if tick + 1 < sections:
                updated = jnp.where(section_pos == tick + 1, relayed, updated)
                pairs.append((tick + 1, 0))
            current = lax.ppermute(updated, "section", pairs)

    kernel_sum = kernel_gradient(half, [gathered[1], gathered[0]], feature_all, ring_pos, None)

    outs = lax.dynamic_slice_in_dim(jnp.stack(results[::-1]), ticks - blocks_n - section_pos, blocks_n, 0)
    outs = outs.reshape(frames_all, rings, rows_l, own, group).transpose(1, 0, 2, 3, 4)
    outs, gathered[-1], kernel_sum = lax.optimization_barrier((outs, gathered[-1], kernel_sum))
    outs = lax.all_to_all(outs, "frame", 0, 0)
    kernel_total = kernel_gradient(0, [gathered[3], gathered[2]], feature_all, ring_pos, kernel_sum)
    outs, kernel_total = lax.optimization_barrier((outs, kernel_total))
    outs = outs.transpose(4, 1, 2, 0, 3).reshape(group, frames_all, rows_l, width_n)
    return (outs[None], kernel_total[None])


def solution(mesh):
    placed = (
        P("chan", None, "frame", None),
        P("section", None, None, "frame", None),
        P("section", None, "chan", None),
    )
    return jax.shard_map(
        body,
        mesh=mesh,
        in_specs=placed,
        out_specs=(P("section", "chan", None, "frame", None), P("section", None, "chan", None)),
        check_vma=False,
    )
```

```python
import functools

import jax
import jax.numpy as jnp
from jax import lax
from jax.experimental import pallas as pl
from jax.experimental.pallas import tpu as pltpu
from jax.sharding import PartitionSpec as P

BLOCK_FRAMES = 2
F32 = jnp.float32
BF16 = jnp.bfloat16


def back_kernel(cur_ref, later_ref, w_ref, out_ref, spread, acc):
    frames_n, rows_n, width_n, group = cur_ref.shape
    empty = jnp.zeros((width_n, 3 * group), F32)
    for frame in range(2 * frames_n):
        spread[frame, 0] = empty
        spread[frame, rows_n + 1] = empty
        for row in range(rows_n):
            source = cur_ref[frame, row] if frame < frames_n else later_ref[frame - frames_n, row]
            cells = source.astype(F32)
            spread[frame, row + 1, :, 0:group] = pltpu.roll(cells, width_n - 1, 0)
            spread[frame, row + 1, :, group : 2 * group] = cells
            spread[frame, row + 1, :, 2 * group : 3 * group] = pltpu.roll(cells, 1, 0)
    for step in range(9):
        lag, offset = step // 3, 2 - step % 3
        taken = spread[lag : lag + frames_n, offset : offset + rows_n]
        taken = taken.reshape(frames_n * rows_n * width_n, 3 * group).astype(BF16)
        part = jnp.dot(
            taken, w_ref[3 * step : 3 * step + 3].reshape(3 * group, -1), preferred_element_type=F32
        )
        if step == 0:
            acc[...] = part
        elif step < 8:
            acc[...] += part
        else:
            out_ref[...] = (acc[...] + part).astype(BF16)


def back_block(current, later, kernels):
    frames_n, rows_n, width_n, group = current.shape
    channels = kernels.shape[2]
    cells = frames_n * rows_n * width_n
    held = pl.BlockSpec(memory_space=pltpu.VMEM)
    return pl.pallas_call(
        back_kernel,
        in_specs=[held, held, held],
        out_specs=held,
        out_shape=jax.ShapeDtypeStruct((cells, channels), BF16),
        scratch_shapes=[
            pltpu.VMEM((2 * frames_n, rows_n + 2, width_n, 3 * group), F32),
            pltpu.VMEM((cells, channels), F32),
        ],
        compiler_params=pltpu.CompilerParams(vmem_limit_bytes=24 * 2**20),
        cost_estimate=pl.CostEstimate(
            flops=54 * group * channels * cells, bytes_accessed=54 * group * channels, transcendentals=0
        ),
    )(current, later, kernels)


def tap_kernel(first, f_first, has_sum, grad_moves, feature_moves, place_ref, *refs):
    out_ref, cells_ref, sides, feature_ref, arrived = refs[-5:]
    step = pl.program_id(0)
    frames_n, rows_n, width_n, group = cells_ref.shape

    def placed(position, relative, size, which):
        if not relative:
            return position
        return lax.rem(place_ref[which] + size - position, size)

    @pl.when(step == 0)
    def _():
        copies = []
        for operand, index, frame, ring, ring_back, _, _ in grad_moves:
            source = refs[operand] if index is None else refs[operand].at[index]
            count, own = source.shape[0], source.shape[2]
            ring = placed(ring, ring_back, width_n // own, 0)
            columns = pl.ds(ring * own if isinstance(ring, int) else pl.multiple_of(ring * own, own), own)
            target = cells_ref.at[pl.ds(frame - first, count), :, columns]
            copies.append(pltpu.make_async_copy(source, target, arrived.at[len(copies)]))
        for operand, index, frame, ring, ring_back, chan, chan_back in feature_moves:
            source = refs[operand] if index is None else refs[operand].at[index]
            rows_l, cells, width_c = source.shape
            ring = placed(ring, ring_back, rows_n // rows_l, 0)
            chan = placed(chan, chan_back, feature_ref.shape[2] // width_c, 1)
            lanes = pl.ds(chan * width_c if isinstance(chan, int) else pl.multiple_of(chan * width_c, 128), width_c)
            target = feature_ref.at[pl.ds(ring * rows_l, rows_l), pl.ds((frame - f_first) * width_n, cells), lanes]
            copies.append(pltpu.make_async_copy(source, target, arrived.at[len(copies)]))
        for copy in copies:
            copy.start()
        same = lax.broadcasted_iota(jnp.int32, (group, group), 0) == lax.broadcasted_iota(jnp.int32, (group, group), 1)
        identity = jnp.where(same, 1.0, 0.0).astype(BF16)
        source = lax.broadcasted_iota(jnp.int32, (width_n, 2 * width_n), 0)
        target = lax.broadcasted_iota(jnp.int32, (width_n, 2 * width_n), 1)
        moved = (source == target + 1) & (target < width_n) | (source == target - width_n - 1)
        shifts = jnp.where(moved, 1.0, 0.0).astype(BF16)
        edge = jnp.zeros((3 * group, frames_n * width_n), BF16)
        sides[:, 0 : frames_n * width_n] = edge
        sides[:, (rows_n + 1) * frames_n * width_n :] = edge
        for copy in copies[: len(grad_moves)]:
            copy.wait()

        for frame in range(frames_n):
            turned = lax.dot_general(
                identity,
                cells_ref[frame].reshape(rows_n * width_n, group),
                (((1,), (1,)), ((), ())),
                preferred_element_type=F32,
            ).astype(BF16)
            for row in range(rows_n):
                start = ((row + 1) * frames_n + frame) * width_n
                cells = turned[:, row * width_n : (row + 1) * width_n]
                both = jnp.dot(cells, shifts, preferred_element_type=F32).astype(BF16)
                sides[0:group, start : start + width_n] = both[:, :width_n]
                sides[group : 2 * group, start : start + width_n] = cells
                sides[2 * group : 3 * group, start : start + width_n] = both[:, width_n:]

        for copy in copies[len(grad_moves) :]:
            copy.wait()

    offset = 2 - step % 3
    for lag in range(3):

        @pl.when(step // 3 == lag)
        def _():
            skipped = max(0, lag - first)
            span = (frames_n - skipped) * width_n
            low = (first + skipped - lag - f_first) * width_n
            lefts, rights = [], []
            for row in range(rows_n):
                start = ((row + offset) * frames_n + skipped) * width_n
                lefts.append(sides[:, pl.ds(pl.multiple_of(start, 128), span)])
                rights.append(feature_ref[row, low : low + span])
            total = jnp.dot(
                jnp.concatenate(lefts, axis=1), jnp.concatenate(rights, axis=0), preferred_element_type=F32
            ).reshape(out_ref.shape)
            if has_sum:
                total = total + refs[0][...].astype(F32)
            out_ref[...] = total.astype(out_ref.dtype)


def gather_ring(block, rings):
    if rings > 4:
        return [lax.all_gather(block, "frame")]
    return [block] + [
        lax.ppermute(block, "frame", [(i, (i + step) % rings) for i in range(rings)]) for step in range(1, rings)
    ]


def swap_chan(pieces, chans):
    whole = jnp.stack(pieces) if len(pieces) > 1 else pieces[0]
    return [whole] + [
        lax.ppermute(whole, "chan", [(i, (i + step) % chans) for i in range(chans)]) for step in range(1, chans)
    ]


def kernel_gradient(grads, features, places, shape, known):
    frames_n, held_n, rows_n, width_n, group, channels = shape
    has_sum = known is not None
    operands, grad_moves, feature_moves = [places] + [known] * has_sum, [], []
    for frame, pieces in grads.items():
        for ring, piece in enumerate(pieces):
            operand = len(operands) - 1
            if len(pieces) > 1:
                grad_moves.append((operand, None, frame, ring, True, 0, False))
            else:
                grad_moves += [(operand, i, frame, i, False, 0, False) for i in range(piece.shape[0])]
            operands.append(piece)
    for frame, (arrays, ordered) in features.items():
        for chan, array in enumerate(arrays):
            operand = len(operands) - 1
            for ring in range(array.shape[0]):
                feature_moves.append((operand, ring, frame, ring, not ordered, chan, len(arrays) > 1))
            operands.append(array)
    far = pl.BlockSpec(memory_space=pltpu.HBM)
    out_spec = pl.BlockSpec((3, group, channels), lambda step: (step, 0, 0))
    return pl.pallas_call(
        functools.partial(tap_kernel, min(grads), min(features), has_sum, grad_moves, feature_moves),
        grid=(9,),
        in_specs=[pl.BlockSpec(memory_space=pltpu.SMEM)]
        + [out_spec] * has_sum
        + [far] * (len(operands) - 1 - has_sum),
        out_specs=out_spec,
        out_shape=jax.ShapeDtypeStruct((27, group, channels), BF16),
        scratch_shapes=[
            pltpu.VMEM((frames_n, rows_n, width_n, group), BF16),
            pltpu.VMEM((3 * group, (rows_n + 2) * frames_n * width_n), BF16),
            pltpu.VMEM((rows_n, held_n * width_n, channels), BF16),
            pltpu.SemaphoreType.DMA((len(grad_moves) + len(feature_moves),)),
        ],
        compiler_params=pltpu.CompilerParams(vmem_limit_bytes=58 * 2**20),
        cost_estimate=pl.CostEstimate(
            flops=54 * group * channels * rows_n * frames_n * width_n,
            bytes_accessed=4 * 27 * group * channels,
            transcendentals=0,
        ),
    )(*operands)


def body(upstream, acts, weights):
    group, frames_all, rows_l, width_n = upstream.shape
    sections, rings, chans = lax.axis_size("section"), lax.axis_size("frame"), lax.axis_size("chan")
    section_pos, ring_pos, chan_pos = lax.axis_index("section"), lax.axis_index("frame"), lax.axis_index("chan")
    rows_n = rows_l * rings
    own = width_n // rings
    halo = sections
    window = own + 2 * halo
    blocks_n = frames_all // BLOCK_FRAMES
    assert blocks_n == sections
    half = frames_all // 2
    ticks = blocks_n + sections - 1
    kernels = weights[0]

    def to_columns(cells):
        wide = jnp.pad(cells, [(0, 0)] * (cells.ndim - 2) + [(halo, halo), (0, 0)])
        pieces = jnp.stack([wide[..., own * i : own * i + window, :] for i in range(rings)])
        pieces = lax.all_to_all(pieces, "frame", 0, 0)
        pieces = jnp.moveaxis(pieces, 0, -4)
        return pieces.reshape(cells.shape[:-3] + (rows_n, window, group))

    mine = lax.dynamic_slice_in_dim(acts[0], chan_pos * group, group, 0)
    top = frames_all - BLOCK_FRAMES
    relayed = lax.dynamic_slice_in_dim(upstream, (blocks_n - 1 - section_pos) * BLOCK_FRAMES, BLOCK_FRAMES, 1)
    pair = to_columns(jnp.stack([relayed, mine[:, top:]]).transpose(0, 2, 3, 4, 1))
    relayed = pair[0]
    rest = to_columns(mine[:, :top].transpose(1, 2, 3, 0))
    stored = [pair[1]]
    for order in range(1, blocks_n):
        first = top - order * BLOCK_FRAMES
        stored.append(rest[first : first + BLOCK_FRAMES])

    shared = group % 128 == 0
    values = (mine if shared else acts[0]).astype(F32)
    feature_part = (values * jax.nn.sigmoid(values)).astype(BF16).transpose(2, 1, 3, 0)

    def feature_block(order):
        first = top - order * BLOCK_FRAMES
        return feature_part[:, first : first + BLOCK_FRAMES].reshape(rows_l, BLOCK_FRAMES * width_n, -1)

    column = ring_pos * own - halo + jnp.arange(window)
    inside = jnp.logical_and(column >= 0, column < width_n)[None, None, :, None]
    later = jnp.zeros((BLOCK_FRAMES, rows_n, window, group), BF16)
    current = jnp.where(section_pos == 0, relayed, later)
    held, received, features, results = [], [], [], []
    for tick in range(ticks):
        held.append(current[:, :, halo : halo + own])
        partial = back_block(current, later, kernels)
        if tick in (1, 2):
            partial, received[tick - 1] = lax.optimization_barrier((partial, received[tick - 1]))
        if tick == ticks - 1:
            partial, received = lax.optimization_barrier((partial, received))
        summed = lax.dynamic_slice_in_dim(partial, chan_pos * group, group, 1).astype(F32)
        for step in range(1, chans):
            there = lax.rem(chan_pos + step, chans)
            piece = lax.dynamic_slice_in_dim(partial, there * group, group, 1)
            arrived = lax.ppermute(piece, "chan", [(i, (i + step) % chans) for i in range(chans)])
            summed = summed + arrived.astype(F32)
        known = jnp.stack(stored[: tick + 1])
        place = jnp.clip(tick - section_pos, 0, known.shape[0] - 1)
        slot = lax.dynamic_index_in_dim(known, place, 0, keepdims=False).astype(F32)
        logistic = jax.nn.sigmoid(slot)
        slope = logistic * (1.0 + slot * (1.0 - logistic))
        updated = current.astype(F32) + slope * summed.reshape(current.shape)
        updated = jnp.where(inside, updated, 0.0).astype(BF16)
        if 2 < tick < ticks - 1:
            updated, received[tick - 1] = lax.optimization_barrier((updated, received[tick - 1]))
        if 1 < tick < blocks_n + 1:
            updated, features[tick - 2] = lax.optimization_barrier((updated, features[tick - 2]))
        if tick < blocks_n - 1:
            block = feature_block(tick)
        else:
            order = tick - sections + 1
            block = lax.dynamic_index_in_dim(jnp.stack(held[order:]), section_pos, 0, keepdims=False)
        if tick + 1 < ticks:
            block, updated = lax.optimization_barrier((block, updated))
            received.append(gather_ring(block, rings))
        elif shared and rings <= 4:
            both = jnp.concatenate([block.reshape(1, -1, group), feature_block(blocks_n - 1).reshape(1, -1, group)])
            pieces = gather_ring(both, rings)
            received.append([piece[0].reshape(block.shape) for piece in pieces])
            received.append([piece[1].reshape(rows_l, -1, group) for piece in pieces])
        else:
            received.append(gather_ring(block, rings))
            received.append(gather_ring(feature_block(blocks_n - 1), rings))
        if 0 < tick < blocks_n:
            features.append(swap_chan(received[tick - 1], chans if shared else 1))
        results.append(updated[:, :, halo : halo + own])
        later = current
        if tick + 1 < ticks:
            pairs = [(i, i + 1) for i in range(sections - 1) if i <= tick < i + blocks_n]
            if tick + 1 < sections:
                updated = jnp.where(section_pos == tick + 1, relayed, updated)
                pairs.append((tick + 1, 0))
            current = lax.ppermute(updated, "section", pairs)

    features.append(swap_chan(received[-1], chans if shared else 1))
    features = [(arrays, rings > 4) for arrays in features]
    gathered = received[blocks_n - 1 : -1]
    if own % 16:
        gathered = [
            [jnp.moveaxis(pieces[0], 0, 2).reshape(1, BLOCK_FRAMES, rows_n, width_n, group)] for pieces in gathered
        ]
    places = jnp.stack([ring_pos, chan_pos]).astype(jnp.int32)
    first = {order: top - order * BLOCK_FRAMES for order in range(blocks_n)}
    channels = acts.shape[1]
    kernel_sum = kernel_gradient(
        {first[order]: gathered[order] for order in (0, 1)},
        {first[order]: features[order] for order in (0, 1, 2)},
        places,
        (2 * BLOCK_FRAMES, 3 * BLOCK_FRAMES, rows_n, width_n, group, channels),
        None,
    )

    outs = lax.dynamic_slice_in_dim(jnp.stack(results[::-1]), ticks - blocks_n - section_pos, blocks_n, 0)
    outs = outs.reshape(frames_all, rings, rows_l, own, group).transpose(1, 0, 2, 3, 4)
    outs, gathered[-1], kernel_sum = lax.optimization_barrier((outs, gathered[-1], kernel_sum))
    outs = lax.all_to_all(outs, "frame", 0, 0)
    kernel_total = kernel_gradient(
        {first[order]: gathered[order] for order in (2, 3)},
        {first[order]: features[order] for order in (2, 3)},
        places,
        (2 * BLOCK_FRAMES, 2 * BLOCK_FRAMES, rows_n, width_n, group, channels),
        kernel_sum,
    )
    outs, kernel_total = lax.optimization_barrier((outs, kernel_total))
    outs = outs.transpose(4, 1, 2, 0, 3).reshape(group, frames_all, rows_l, width_n)
    return (outs[None], kernel_total[None])


def solution(mesh):
    placed = (
        P("chan", None, "frame", None),
        P("section", None, None, "frame", None),
        P("section", None, "chan", None),
    )
    return jax.shard_map(
        body,
        mesh=mesh,
        in_specs=placed,
        out_specs=(P("section", "chan", None, "frame", None), P("section", None, "chan", None)),
        check_vma=False,
    )
```

```python
import functools

import jax
import jax.numpy as jnp
from jax import lax
from jax.experimental import pallas as pl
from jax.experimental.pallas import tpu as pltpu
from jax.sharding import PartitionSpec as P

BLOCK_FRAMES = 2
F32 = jnp.float32
BF16 = jnp.bfloat16


def back_kernel(cur_ref, later_ref, w_ref, out_ref, spread, acc):
    frames_n, rows_n, width_n, group = cur_ref.shape
    empty = jnp.zeros((width_n, 3 * group), F32)
    for frame in range(2 * frames_n):
        spread[frame, 0] = empty
        spread[frame, rows_n + 1] = empty
        for row in range(rows_n):
            source = cur_ref[frame, row] if frame < frames_n else later_ref[frame - frames_n, row]
            cells = source.astype(F32)
            spread[frame, row + 1, :, 0:group] = pltpu.roll(cells, width_n - 1, 0)
            spread[frame, row + 1, :, group : 2 * group] = cells
            spread[frame, row + 1, :, 2 * group : 3 * group] = pltpu.roll(cells, 1, 0)
    for step in range(9):
        lag, offset = step // 3, 2 - step % 3
        taken = spread[lag : lag + frames_n, offset : offset + rows_n]
        taken = taken.reshape(frames_n * rows_n * width_n, 3 * group).astype(BF16)
        part = jnp.dot(
            taken, w_ref[3 * step : 3 * step + 3].reshape(3 * group, -1), preferred_element_type=F32
        )
        if step == 0:
            acc[...] = part
        elif step < 8:
            acc[...] += part
        else:
            out_ref[...] = (acc[...] + part).astype(BF16)


def back_block(current, later, kernels):
    frames_n, rows_n, width_n, group = current.shape
    channels = kernels.shape[2]
    cells = frames_n * rows_n * width_n
    held = pl.BlockSpec(memory_space=pltpu.VMEM)
    return pl.pallas_call(
        back_kernel,
        in_specs=[held, held, held],
        out_specs=held,
        out_shape=jax.ShapeDtypeStruct((cells, channels), BF16),
        scratch_shapes=[
            pltpu.VMEM((2 * frames_n, rows_n + 2, width_n, 3 * group), F32),
            pltpu.VMEM((cells, channels), F32),
        ],
        compiler_params=pltpu.CompilerParams(vmem_limit_bytes=24 * 2**20),
        cost_estimate=pl.CostEstimate(
            flops=54 * group * channels * cells, bytes_accessed=54 * group * channels, transcendentals=0
        ),
    )(current, later, kernels)


def tap_kernel(first, f_first, has_sum, *refs):
    grad_ref, parts_ref, *refs = refs
    sum_ref = refs.pop(0) if has_sum else None
    out_ref, cells_ref, sides, feature_ref, total, g_here, f_here = refs
    step = pl.program_id(0)
    pieces_n, frames_n, rows_n, own, group = grad_ref.shape
    rings, chans, rows_l, _, width_c = parts_ref.shape
    width_n = pieces_n * own
    held_n = feature_ref.shape[1] // width_n

    @pl.when(step == 0)
    def _():
        g_copies, f_copies = [], []
        for piece in range(pieces_n):
            columns = pl.ds(piece * own, own)
            g_copies.append(pltpu.make_async_copy(grad_ref.at[piece], cells_ref.at[:, :, columns], g_here.at[piece]))
        for ring in range(rings):
            for chan in range(chans):
                f_copies.append(
                    pltpu.make_async_copy(
                        parts_ref.at[ring, chan, :, pl.ds(f_first * width_n, held_n * width_n)],
                        feature_ref.at[pl.ds(ring * rows_l, rows_l), :, pl.ds(chan * width_c, width_c)],
                        f_here.at[ring * chans + chan],
                    )
                )
        for copy in g_copies + f_copies:
            copy.start()
        same = lax.broadcasted_iota(jnp.int32, (group, group), 0) == lax.broadcasted_iota(jnp.int32, (group, group), 1)
        identity = jnp.where(same, 1.0, 0.0).astype(BF16)
        source = lax.broadcasted_iota(jnp.int32, (width_n, 2 * width_n), 0)
        target = lax.broadcasted_iota(jnp.int32, (width_n, 2 * width_n), 1)
        moved = (source == target + 1) & (target < width_n) | (source == target - width_n - 1)
        shifts = jnp.where(moved, 1.0, 0.0).astype(BF16)
        edge = jnp.zeros((3 * group, frames_n * width_n), BF16)
        sides[:, 0 : frames_n * width_n] = edge
        sides[:, (rows_n + 1) * frames_n * width_n :] = edge
        for copy in g_copies:
            copy.wait()
        for frame in range(frames_n):
            turned = lax.dot_general(
                identity,
                cells_ref[frame].reshape(rows_n * width_n, group),
                (((1,), (1,)), ((), ())),
                preferred_element_type=F32,
            ).astype(BF16)
            for row in range(rows_n):
                start = ((row + 1) * frames_n + frame) * width_n
                cells = turned[:, row * width_n : (row + 1) * width_n]
                both = jnp.dot(cells, shifts, preferred_element_type=F32).astype(BF16)
                sides[0:group, start : start + width_n] = both[:, :width_n]
                sides[group : 2 * group, start : start + width_n] = cells
                sides[2 * group : 3 * group, start : start + width_n] = both[:, width_n:]
        for copy in f_copies:
            copy.wait()

    offset = 2 - step % 3
    for lag in range(3):

        @pl.when(step // 3 == lag)
        def _():
            skipped = max(0, lag - first)
            span = (frames_n - skipped) * width_n
            low = (first + skipped - lag - f_first) * width_n
            for row in range(rows_n):
                start = ((row + offset) * frames_n + skipped) * width_n
                part = jnp.dot(
                    sides[:, pl.ds(pl.multiple_of(start, 128), span)],
                    feature_ref[row, low : low + span],
                    preferred_element_type=F32,
                )
                if row == 0:
                    total[...] = part
                elif row < rows_n - 1:
                    total[...] += part
                else:
                    whole = (total[...] + part).reshape(out_ref.shape)
                    if has_sum:
                        whole = whole + sum_ref[...].astype(F32)
                    out_ref[...] = whole.astype(out_ref.dtype)


def kernel_gradient(first, grads, parts, known):
    pieces_n, frames_n, rows_n, own, group = grads.shape
    rings, chans, rows_l, _, width_c = parts.shape
    channels = chans * width_c
    width_n = pieces_n * own
    f_first = max(0, first - 2)
    held_n = first + frames_n - f_first
    far = pl.BlockSpec(memory_space=pltpu.HBM)
    out_spec = pl.BlockSpec((3, group, channels), lambda step: (step, 0, 0))
    has_sum = known is not None
    return pl.pallas_call(
        functools.partial(tap_kernel, first, f_first, has_sum),
        grid=(9,),
        in_specs=[far, far] + [out_spec] * has_sum,
        out_specs=out_spec,
        out_shape=jax.ShapeDtypeStruct((27, group, channels), BF16),
        scratch_shapes=[
            pltpu.VMEM((frames_n, rows_n, width_n, group), BF16),
            pltpu.VMEM((3 * group, (rows_n + 2) * frames_n * width_n), BF16),
            pltpu.VMEM((rows_n, held_n * width_n, channels), BF16),
            pltpu.VMEM((3 * group, channels), F32),
            pltpu.SemaphoreType.DMA((pieces_n,)),
            pltpu.SemaphoreType.DMA((rings * chans,)),
        ],
        compiler_params=pltpu.CompilerParams(vmem_limit_bytes=58 * 2**20),
        cost_estimate=pl.CostEstimate(
            flops=54 * group * channels * rows_n * frames_n * width_n,
            bytes_accessed=6 * 27 * group * channels,
            transcendentals=0,
        ),
    )(*([grads, parts] + [known] * has_sum))


def body(upstream, acts, weights):
    group, frames_all, rows_l, width_n = upstream.shape
    sections, rings, chans = lax.axis_size("section"), lax.axis_size("frame"), lax.axis_size("chan")
    section_pos, ring_pos, chan_pos = lax.axis_index("section"), lax.axis_index("frame"), lax.axis_index("chan")
    rows_n = rows_l * rings
    own = width_n // rings
    halo = sections
    window = own + 2 * halo
    blocks_n = frames_all // BLOCK_FRAMES
    assert blocks_n == sections
    half = frames_all // 2
    ticks = blocks_n + sections - 1
    kernels = weights[0]

    def to_columns(cells):
        wide = jnp.pad(cells, [(0, 0)] * (cells.ndim - 2) + [(halo, halo), (0, 0)])
        pieces = jnp.stack([wide[..., own * i : own * i + window, :] for i in range(rings)])
        pieces = lax.all_to_all(pieces, "frame", 0, 0)
        pieces = jnp.moveaxis(pieces, 0, -4)
        return pieces.reshape(cells.shape[:-3] + (rows_n, window, group))

    mine = lax.dynamic_slice_in_dim(acts[0], chan_pos * group, group, 0)
    top = frames_all - BLOCK_FRAMES
    relayed = lax.dynamic_slice_in_dim(upstream, (blocks_n - 1 - section_pos) * BLOCK_FRAMES, BLOCK_FRAMES, 1)
    pair = to_columns(jnp.stack([relayed, mine[:, top:]]).transpose(0, 2, 3, 4, 1))
    relayed = pair[0]
    rest = to_columns(mine[:, :top].transpose(1, 2, 3, 0))
    stored = [pair[1]]
    for order in range(1, blocks_n):
        first = top - order * BLOCK_FRAMES
        stored.append(rest[first : first + BLOCK_FRAMES])

    shared = group % 128 == 0
    values = (mine if shared else acts[0]).astype(F32)
    feature_part = (values * jax.nn.sigmoid(values)).astype(BF16).transpose(2, 1, 3, 0)
    feature_part = feature_part.reshape(rows_l, frames_all * width_n, -1)

    column = ring_pos * own - halo + jnp.arange(window)
    inside = jnp.logical_and(column >= 0, column < width_n)[None, None, :, None]
    later = jnp.zeros((BLOCK_FRAMES, rows_n, window, group), BF16)
    current = jnp.where(section_pos == 0, relayed, later)
    held, gathered, results = [], [], []
    for tick in range(ticks):
        if tick == 1:
            feature_part, current, stored[-1] = lax.optimization_barrier((feature_part, current, stored[-1]))
            feature_all = lax.all_gather(feature_part, ("frame", "chan") if shared else "frame")
            feature_all = feature_all.reshape(rings, chans if shared else 1, *feature_part.shape)
        if tick == ticks - 2:
            current, feature_all = lax.optimization_barrier((current, feature_all))
        held.append(current[:, :, halo : halo + own])
        if tick in (ticks - 1 - blocks_n // 2, ticks - 1):
            begin = len(gathered) * (blocks_n // 2)
            taken = jnp.stack(held[begin:])
            taken = lax.dynamic_slice_in_dim(taken, section_pos, blocks_n // 2, 0)[::-1]
            taken, current = lax.optimization_barrier((taken, current))
            gathered.append(lax.all_gather(taken.reshape(half, rows_n, own, group), "frame"))
        partial = back_block(current, later, kernels)
        if tick == ticks - 1:
            partial, gathered[0] = lax.optimization_barrier((partial, gathered[0]))
        summed = lax.dynamic_slice_in_dim(partial, chan_pos * group, group, 1).astype(F32)
        for step in range(1, chans):
            there = lax.rem(chan_pos + step, chans)
            piece = lax.dynamic_slice_in_dim(partial, there * group, group, 1)
            arrived = lax.ppermute(piece, "chan", [(i, (i + step) % chans) for i in range(chans)])
            summed = summed + arrived.astype(F32)
        known = jnp.stack(stored[: tick + 1])
        place = jnp.clip(tick - section_pos, 0, known.shape[0] - 1)
        slot = lax.dynamic_index_in_dim(known, place, 0, keepdims=False).astype(F32)
        logistic = jax.nn.sigmoid(slot)
        slope = logistic * (1.0 + slot * (1.0 - logistic))
        updated = current.astype(F32) + slope * summed.reshape(current.shape)
        updated = jnp.where(inside, updated, 0.0).astype(BF16)
        results.append(updated[:, :, halo : halo + own])
        later = current
        if tick + 1 < ticks:
            pairs = [(i, i + 1) for i in range(sections - 1) if i <= tick < i + blocks_n]
            if tick + 1 < sections:
                updated = jnp.where(section_pos == tick + 1, relayed, updated)
                pairs.append((tick + 1, 0))
            current = lax.ppermute(updated, "section", pairs)

    if own % 16:
        gathered = [
            block.transpose(1, 2, 0, 3, 4).reshape(1, half, rows_n, width_n, group) for block in gathered
        ]
    kernel_sum = kernel_gradient(half, gathered[0], feature_all, None)

    outs = lax.dynamic_slice_in_dim(jnp.stack(results), section_pos, blocks_n, 0)[::-1]
    outs = outs.reshape(frames_all, rings, rows_l, own, group).transpose(1, 0, 2, 3, 4)
    outs, gathered[1], kernel_sum = lax.optimization_barrier((outs, gathered[1], kernel_sum))
    outs = lax.all_to_all(outs, "frame", 0, 0)
    kernel_total = kernel_gradient(0, gathered[1], feature_all, kernel_sum)
    outs, kernel_total = lax.optimization_barrier((outs, kernel_total))
    outs = outs.transpose(4, 1, 2, 0, 3).reshape(group, frames_all, rows_l, width_n)
    return (outs[None], kernel_total[None])


def solution(mesh):
    placed = (
        P("chan", None, "frame", None),
        P("section", None, None, "frame", None),
        P("section", None, "chan", None),
    )
    return jax.shard_map(
        body,
        mesh=mesh,
        in_specs=placed,
        out_specs=(P("section", "chan", None, "frame", None), P("section", None, "chan", None)),
        check_vma=False,
    )
```

```python
import functools

import jax
import jax.numpy as jnp
from jax import lax
from jax.experimental import pallas as pl
from jax.experimental.pallas import tpu as pltpu
from jax.sharding import PartitionSpec as P

BLOCK_FRAMES = 2
F32 = jnp.float32
BF16 = jnp.bfloat16


def back_kernel(cur_ref, later_ref, w_ref, out_ref, spread, acc):
    frames_n, rows_n, width_n, group = cur_ref.shape
    empty = jnp.zeros((width_n, 3 * group), F32)
    for frame in range(2 * frames_n):
        spread[frame, 0] = empty
        spread[frame, rows_n + 1] = empty
        for row in range(rows_n):
            source = cur_ref[frame, row] if frame < frames_n else later_ref[frame - frames_n, row]
            cells = source.astype(F32)
            spread[frame, row + 1, :, 0:group] = pltpu.roll(cells, width_n - 1, 0)
            spread[frame, row + 1, :, group : 2 * group] = cells
            spread[frame, row + 1, :, 2 * group : 3 * group] = pltpu.roll(cells, 1, 0)
    for step in range(9):
        lag, offset = step // 3, 2 - step % 3
        taken = spread[lag : lag + frames_n, offset : offset + rows_n]
        taken = taken.reshape(frames_n * rows_n * width_n, 3 * group).astype(BF16)
        part = jnp.dot(
            taken, w_ref[3 * step : 3 * step + 3].reshape(3 * group, -1), preferred_element_type=F32
        )
        if step == 0:
            acc[...] = part
        elif step < 8:
            acc[...] += part
        else:
            out_ref[...] = (acc[...] + part).astype(BF16)


def back_block(current, later, kernels):
    frames_n, rows_n, width_n, group = current.shape
    channels = kernels.shape[2]
    cells = frames_n * rows_n * width_n
    held = pl.BlockSpec(memory_space=pltpu.VMEM)
    return pl.pallas_call(
        back_kernel,
        in_specs=[held, held, held],
        out_specs=held,
        out_shape=jax.ShapeDtypeStruct((cells, channels), BF16),
        scratch_shapes=[
            pltpu.VMEM((2 * frames_n, rows_n + 2, width_n, 3 * group), F32),
            pltpu.VMEM((cells, channels), F32),
        ],
        compiler_params=pltpu.CompilerParams(vmem_limit_bytes=24 * 2**20),
        cost_estimate=pl.CostEstimate(
            flops=54 * group * channels * cells, bytes_accessed=54 * group * channels, transcendentals=0
        ),
    )(current, later, kernels)


def tap_kernel(first, f_first, has_sum, *refs):
    grad_ref, parts_ref, *refs = refs
    sum_ref = refs.pop(0) if has_sum else None
    out_ref, cells_ref, sides, feature_ref, total, g_here, f_here = refs
    step = pl.program_id(0)
    pieces_n, frames_n, rows_n, own, group = grad_ref.shape
    rings, chans, rows_l, _, width_c = parts_ref.shape
    width_n = pieces_n * own
    held_n = feature_ref.shape[2] // width_n

    @pl.when(step == 0)
    def _():
        g_copies, f_copies = [], []
        for piece in range(pieces_n):
            g_copies.append(pltpu.make_async_copy(grad_ref.at[piece], cells_ref.at[piece], g_here.at[piece]))
        for ring in range(rings):
            for chan in range(chans):
                f_copies.append(
                    pltpu.make_async_copy(
                        parts_ref.at[ring, chan, :, pl.ds(f_first * width_n, held_n * width_n)],
                        feature_ref.at[chan, pl.ds(ring * rows_l, rows_l)],
                        f_here.at[ring * chans + chan],
                    )
                )
        for copy in g_copies + f_copies:
            copy.start()
        same = lax.broadcasted_iota(jnp.int32, (group, group), 0) == lax.broadcasted_iota(jnp.int32, (group, group), 1)
        identity = jnp.where(same, 1.0, 0.0).astype(BF16)
        source = lax.broadcasted_iota(jnp.int32, (width_n, 2 * width_n), 0)
        target = lax.broadcasted_iota(jnp.int32, (width_n, 2 * width_n), 1)
        moved = (source == target + 1) & (target < width_n) | (source == target - width_n - 1)
        shifts = jnp.where(moved, 1.0, 0.0).astype(BF16)
        edge = jnp.zeros((3 * group, frames_n * width_n), BF16)
        sides[:, 0 : frames_n * width_n] = edge
        sides[:, (rows_n + 1) * frames_n * width_n :] = edge
        for copy in g_copies:
            copy.wait()
        for frame in range(frames_n):
            joined = [cells_ref[piece, frame, row] for row in range(rows_n) for piece in range(pieces_n)]
            turned = lax.dot_general(
                identity,
                jnp.concatenate(joined, axis=0),
                (((1,), (1,)), ((), ())),
                preferred_element_type=F32,
            ).astype(BF16)
            for row in range(rows_n):
                start = ((row + 1) * frames_n + frame) * width_n
                cells = turned[:, row * width_n : (row + 1) * width_n]
                both = jnp.dot(cells, shifts, preferred_element_type=F32).astype(BF16)
                sides[0:group, start : start + width_n] = both[:, :width_n]
                sides[group : 2 * group, start : start + width_n] = cells
                sides[2 * group : 3 * group, start : start + width_n] = both[:, width_n:]
        for copy in f_copies:
            copy.wait()

    offset = 2 - step % 3
    for lag in range(3):

        @pl.when(step // 3 == lag)
        def _():
            skipped = max(0, lag - first)
            span = (frames_n - skipped) * width_n
            low = (first + skipped - lag - f_first) * width_n
            for chan in range(chans):
                lanes = slice(chan * width_c, (chan + 1) * width_c)
                for row in range(rows_n):
                    start = ((row + offset) * frames_n + skipped) * width_n
                    part = jnp.dot(
                        sides[:, pl.ds(pl.multiple_of(start, 128), span)],
                        feature_ref[chan, row, low : low + span],
                        preferred_element_type=F32,
                    )
                    if row == 0:
                        total[...] = part
                    elif row < rows_n - 1:
                        total[...] += part
                    else:
                        whole = (total[...] + part).reshape(3, group, width_c)
                        if has_sum:
                            whole = whole + sum_ref[:, :, lanes].astype(F32)
                        out_ref[:, :, lanes] = whole.astype(out_ref.dtype)


def kernel_gradient(first, grads, parts, known):
    pieces_n, frames_n, rows_n, own, group = grads.shape
    rings, chans, rows_l, _, width_c = parts.shape
    channels = chans * width_c
    width_n = pieces_n * own
    f_first = max(0, first - 2)
    held_n = first + frames_n - f_first
    far = pl.BlockSpec(memory_space=pltpu.HBM)
    out_spec = pl.BlockSpec((3, group, channels), lambda step: (step, 0, 0))
    has_sum = known is not None
    return pl.pallas_call(
        functools.partial(tap_kernel, first, f_first, has_sum),
        grid=(9,),
        in_specs=[far, far] + [out_spec] * has_sum,
        out_specs=out_spec,
        out_shape=jax.ShapeDtypeStruct((27, group, channels), BF16),
        scratch_shapes=[
            pltpu.VMEM(grads.shape, BF16),
            pltpu.VMEM((3 * group, (rows_n + 2) * frames_n * width_n), BF16),
            pltpu.VMEM((chans, rows_n, held_n * width_n, width_c), BF16),
            pltpu.VMEM((3 * group, width_c), F32),
            pltpu.SemaphoreType.DMA((pieces_n,)),
            pltpu.SemaphoreType.DMA((rings * chans,)),
        ],
        compiler_params=pltpu.CompilerParams(vmem_limit_bytes=58 * 2**20),
        cost_estimate=pl.CostEstimate(
            flops=54 * group * channels * rows_n * frames_n * width_n,
            bytes_accessed=6 * 27 * group * channels,
            transcendentals=0,
        ),
    )(*([grads, parts] + [known] * has_sum))


def body(upstream, acts, weights):
    group, frames_all, rows_l, width_n = upstream.shape
    sections, rings, chans = lax.axis_size("section"), lax.axis_size("frame"), lax.axis_size("chan")
    section_pos, ring_pos, chan_pos = lax.axis_index("section"), lax.axis_index("frame"), lax.axis_index("chan")
    rows_n = rows_l * rings
    own = width_n // rings
    halo = sections
    window = own + 2 * halo
    blocks_n = frames_all // BLOCK_FRAMES
    assert blocks_n == sections
    half = frames_all // 2
    ticks = blocks_n + sections - 1
    kernels = weights[0]

    def to_columns(cells):
        wide = jnp.pad(cells, [(0, 0)] * (cells.ndim - 2) + [(halo, halo), (0, 0)])
        pieces = jnp.stack([wide[..., own * i : own * i + window, :] for i in range(rings)])
        pieces = lax.all_to_all(pieces, "frame", 0, 0)
        pieces = jnp.moveaxis(pieces, 0, -4)
        return pieces.reshape(cells.shape[:-3] + (rows_n, window, group))

    mine = lax.dynamic_slice_in_dim(acts[0], chan_pos * group, group, 0)
    top = frames_all - BLOCK_FRAMES
    relayed = lax.dynamic_slice_in_dim(upstream, (blocks_n - 1 - section_pos) * BLOCK_FRAMES, BLOCK_FRAMES, 1)
    pair = to_columns(jnp.stack([relayed, mine[:, top:]]).transpose(0, 2, 3, 4, 1))
    relayed = pair[0]
    rest = to_columns(mine[:, :top].transpose(1, 2, 3, 0))
    stored = [pair[1]]
    for order in range(1, blocks_n):
        first = top - order * BLOCK_FRAMES
        stored.append(rest[first : first + BLOCK_FRAMES])

    shared = group % 128 == 0
    values = (mine if shared else acts[0]).astype(F32)
    feature_part = (values * jax.nn.sigmoid(values)).astype(BF16).transpose(2, 1, 3, 0)
    feature_part = feature_part.reshape(rows_l, frames_all * width_n, -1)

    column = ring_pos * own - halo + jnp.arange(window)
    inside = jnp.logical_and(column >= 0, column < width_n)[None, None, :, None]
    later = jnp.zeros((BLOCK_FRAMES, rows_n, window, group), BF16)
    current = jnp.where(section_pos == 0, relayed, later)
    held, gathered, results = [], [], []
    for tick in range(ticks):
        if tick == 1:
            feature_all = lax.all_gather(feature_part, ("frame", "chan") if shared else "frame")
            feature_all = feature_all.reshape(rings, chans if shared else 1, *feature_part.shape)
        if tick == ticks - 2:
            current, feature_all = lax.optimization_barrier((current, feature_all))
        held.append(current[:, :, halo : halo + own])
        if tick in (ticks - 1 - blocks_n // 2, ticks - 1):
            begin = len(gathered) * (blocks_n // 2)
            taken = jnp.stack(held[begin:])
            taken = lax.dynamic_slice_in_dim(taken, section_pos, blocks_n // 2, 0)[::-1]
            taken, current = lax.optimization_barrier((taken, current))
            gathered.append(lax.all_gather(taken.reshape(half, rows_n, own, group), "frame"))
        partial = back_block(current, later, kernels)
        if tick == ticks - 1:
            partial, gathered[0] = lax.optimization_barrier((partial, gathered[0]))
        summed = lax.dynamic_slice_in_dim(partial, chan_pos * group, group, 1).astype(F32)
        for step in range(1, chans):
            there = lax.rem(chan_pos + step, chans)
            piece = lax.dynamic_slice_in_dim(partial, there * group, group, 1)
            arrived = lax.ppermute(piece, "chan", [(i, (i + step) % chans) for i in range(chans)])
            summed = summed + arrived.astype(F32)
        known = jnp.stack(stored[: tick + 1])
        place = jnp.clip(tick - section_pos, 0, known.shape[0] - 1)
        slot = lax.dynamic_index_in_dim(known, place, 0, keepdims=False).astype(F32)
        logistic = jax.nn.sigmoid(slot)
        slope = logistic * (1.0 + slot * (1.0 - logistic))
        updated = current.astype(F32) + slope * summed.reshape(current.shape)
        updated = jnp.where(inside, updated, 0.0).astype(BF16)
        if tick == 0:
            feature_part, updated = lax.optimization_barrier((feature_part, updated))
        results.append(updated[:, :, halo : halo + own])
        later = current
        if tick + 1 < ticks:
            pairs = [(i, i + 1) for i in range(sections - 1) if i <= tick < i + blocks_n]
            if tick + 1 < sections:
                updated = jnp.where(section_pos == tick + 1, relayed, updated)
                pairs.append((tick + 1, 0))
            current = lax.ppermute(updated, "section", pairs)

    if own % 16:
        gathered = [
            block.transpose(1, 2, 0, 3, 4).reshape(1, half, rows_n, width_n, group) for block in gathered
        ]
    kernel_sum = kernel_gradient(half, gathered[0], feature_all, None)

    outs = lax.dynamic_slice_in_dim(jnp.stack(results), section_pos, blocks_n, 0)[::-1]
    outs = outs.reshape(frames_all, rings, rows_l, own, group).transpose(1, 0, 2, 3, 4)
    outs, gathered[1], kernel_sum = lax.optimization_barrier((outs, gathered[1], kernel_sum))
    outs = lax.all_to_all(outs, "frame", 0, 0)
    kernel_total = kernel_gradient(0, gathered[1], feature_all, kernel_sum)
    outs, kernel_total = lax.optimization_barrier((outs, kernel_total))
    outs = outs.transpose(4, 1, 2, 0, 3).reshape(group, frames_all, rows_l, width_n)
    return (outs[None], kernel_total[None])


def solution(mesh):
    placed = (
        P("chan", None, "frame", None),
        P("section", None, None, "frame", None),
        P("section", None, "chan", None),
    )
    return jax.shard_map(
        body,
        mesh=mesh,
        in_specs=placed,
        out_specs=(P("section", "chan", None, "frame", None), P("section", None, "chan", None)),
        check_vma=False,
    )
```

```python
import functools

import jax
import jax.numpy as jnp
from jax import lax
from jax.experimental import pallas as pl
from jax.experimental.pallas import tpu as pltpu
from jax.sharding import PartitionSpec as P

BLOCK_FRAMES = 2
F32 = jnp.float32
BF16 = jnp.bfloat16


def back_kernel(cur_ref, later_ref, w_ref, out_ref, spread, acc):
    frames_n, rows_n, width_n, group = cur_ref.shape
    empty = jnp.zeros((width_n, 3 * group), F32)
    for frame in range(2 * frames_n):
        spread[frame, 0] = empty
        spread[frame, rows_n + 1] = empty
        for row in range(rows_n):
            source = cur_ref[frame, row] if frame < frames_n else later_ref[frame - frames_n, row]
            cells = source.astype(F32)
            spread[frame, row + 1, :, 0:group] = pltpu.roll(cells, width_n - 1, 0)
            spread[frame, row + 1, :, group : 2 * group] = cells
            spread[frame, row + 1, :, 2 * group : 3 * group] = pltpu.roll(cells, 1, 0)
    for step in range(9):
        lag, offset = step // 3, 2 - step % 3
        taken = spread[lag : lag + frames_n, offset : offset + rows_n]
        taken = taken.reshape(frames_n * rows_n * width_n, 3 * group).astype(BF16)
        part = jnp.dot(
            taken, w_ref[3 * step : 3 * step + 3].reshape(3 * group, -1), preferred_element_type=F32
        )
        if step == 0:
            acc[...] = part
        elif step < 8:
            acc[...] += part
        else:
            out_ref[...] = (acc[...] + part).astype(BF16)


def back_block(current, later, kernels):
    frames_n, rows_n, width_n, group = current.shape
    channels = kernels.shape[2]
    cells = frames_n * rows_n * width_n
    held = pl.BlockSpec(memory_space=pltpu.VMEM)
    return pl.pallas_call(
        back_kernel,
        in_specs=[held, held, held],
        out_specs=held,
        out_shape=jax.ShapeDtypeStruct((cells, channels), BF16),
        scratch_shapes=[
            pltpu.VMEM((2 * frames_n, rows_n + 2, width_n, 3 * group), F32),
            pltpu.VMEM((cells, channels), F32),
        ],
        compiler_params=pltpu.CompilerParams(vmem_limit_bytes=24 * 2**20),
        cost_estimate=pl.CostEstimate(
            flops=54 * group * channels * cells, bytes_accessed=54 * group * channels, transcendentals=0
        ),
    )(current, later, kernels)


def tap_kernel(first, has_sum, *refs):
    ring_ref, parts_ref, *refs = refs
    sum_ref = refs.pop(0) if has_sum else None
    out_ref, cells_ref, sides, feature_ref, g_here, f_here = refs[-6:]
    grad_refs = refs[:-6]
    step = pl.program_id(0)
    pieces_n, frames_n, rows_n, own, group = cells_ref.shape
    rings, chans, rows_l, _, width_c = parts_ref.shape
    width_n = pieces_n * own
    span = frames_n * width_n

    def feature_copies(lag):
        missing = max(0, lag - first) * width_n
        return [
            pltpu.make_async_copy(
                parts_ref.at[ring, chan, :, pl.ds((first - lag) * width_n + missing, span - missing)],
                feature_ref.at[lag, chan, pl.ds(ring * rows_l, rows_l), pl.ds(missing, span - missing)],
                f_here.at[(lag * rings + ring) * chans + chan],
            )
            for ring in range(rings)
            for chan in range(chans)
        ]

    @pl.when(step == 0)
    def _():
        g_copies = []
        for piece in range(pieces_n):
            if len(grad_refs) == 1:
                source, target = grad_refs[0].at[piece], cells_ref.at[piece]
            else:
                source, target = grad_refs[piece], cells_ref.at[lax.rem(ring_ref[0] + pieces_n - piece, pieces_n)]
            g_copies.append(pltpu.make_async_copy(source, target, g_here.at[piece]))
        for copy in g_copies + feature_copies(0) + feature_copies(1) + feature_copies(2):
            copy.start()
        for lag in range(first + 1, 3):
            for chan in range(chans):
                missing = (lag - first) * width_n
                feature_ref[lag, chan, :, 0:missing] = jnp.zeros((rows_n, missing, width_c), BF16)
        same = lax.broadcasted_iota(jnp.int32, (group, group), 0) == lax.broadcasted_iota(jnp.int32, (group, group), 1)
        identity = jnp.where(same, 1.0, 0.0).astype(BF16)
        source = lax.broadcasted_iota(jnp.int32, (width_n, 2 * width_n), 0)
        target = lax.broadcasted_iota(jnp.int32, (width_n, 2 * width_n), 1)
        moved = (source == target + 1) & (target < width_n) | (source == target - width_n - 1)
        shifts = jnp.where(moved, 1.0, 0.0).astype(BF16)
        edge = jnp.zeros((3 * group, span), BF16)
        sides[:, 0:span] = edge
        sides[:, (rows_n + 1) * span :] = edge
        for copy in g_copies:
            copy.wait()
        for frame in range(frames_n):
            joined = [cells_ref[piece, frame, row] for row in range(rows_n) for piece in range(pieces_n)]
            turned = lax.dot_general(
                identity,
                jnp.concatenate(joined, axis=0),
                (((1,), (1,)), ((), ())),
                preferred_element_type=F32,
            ).astype(BF16)
            for row in range(rows_n):
                start = (row + 1) * span + frame * width_n
                cells = turned[:, row * width_n : (row + 1) * width_n]
                both = jnp.dot(cells, shifts, preferred_element_type=F32).astype(BF16)
                sides[0:group, start : start + width_n] = both[:, :width_n]
                sides[group : 2 * group, start : start + width_n] = cells
                sides[2 * group : 3 * group, start : start + width_n] = both[:, width_n:]

    for lag in range(3):

        @pl.when(step == 3 * lag)
        def _():
            for copy in feature_copies(lag):
                copy.wait()

    start = pl.multiple_of((2 - step % 3) * span, 128)
    for chan in range(chans):
        lanes = slice(chan * width_c, (chan + 1) * width_c)
        total = jnp.dot(
            sides[:, pl.ds(start, rows_n * span)],
            feature_ref[step // 3, chan].reshape(rows_n * span, width_c),
            preferred_element_type=F32,
        ).reshape(3, group, width_c)
        if has_sum:
            total = total + sum_ref[:, :, lanes].astype(F32)
        out_ref[:, :, lanes] = total.astype(out_ref.dtype)


def kernel_gradient(first, grads, parts, ring_pos, known):
    held = grads[0].shape if len(grads) == 1 else (len(grads),) + grads[0].shape
    pieces_n, frames_n, rows_n, own, group = held
    rings, chans, rows_l, _, width_c = parts.shape
    channels = chans * width_c
    width_n = pieces_n * own
    far = pl.BlockSpec(memory_space=pltpu.HBM)
    out_spec = pl.BlockSpec((3, group, channels), lambda step: (step, 0, 0))
    has_sum = known is not None
    return pl.pallas_call(
        functools.partial(tap_kernel, first, has_sum),
        grid=(9,),
        in_specs=[pl.BlockSpec(memory_space=pltpu.SMEM), far] + [out_spec] * has_sum + [far] * len(grads),
        out_specs=out_spec,
        out_shape=jax.ShapeDtypeStruct((27, group, channels), BF16),
        scratch_shapes=[
            pltpu.VMEM(held, BF16),
            pltpu.VMEM((3 * group, (rows_n + 2) * frames_n * width_n), BF16),
            pltpu.VMEM((3, chans, rows_n, frames_n * width_n, width_c), BF16),
            pltpu.SemaphoreType.DMA((pieces_n,)),
            pltpu.SemaphoreType.DMA((3 * rings * chans,)),
        ],
        compiler_params=pltpu.CompilerParams(vmem_limit_bytes=58 * 2**20),
        cost_estimate=pl.CostEstimate(
            flops=54 * group * channels * rows_n * frames_n * width_n,
            bytes_accessed=6 * 27 * group * channels,
            transcendentals=0,
        ),
    )(*([ring_pos.reshape(1), parts] + [known] * has_sum + grads))


def body(upstream, acts, weights):
    group, frames_all, rows_l, width_n = upstream.shape
    sections, rings, chans = lax.axis_size("section"), lax.axis_size("frame"), lax.axis_size("chan")
    section_pos, ring_pos, chan_pos = lax.axis_index("section"), lax.axis_index("frame"), lax.axis_index("chan")
    rows_n = rows_l * rings
    own = width_n // rings
    halo = sections
    window = own + 2 * halo
    blocks_n = frames_all // BLOCK_FRAMES
    assert blocks_n == sections
    half = frames_all // 2
    ticks = blocks_n + sections - 1
    kernels = weights[0]

    def to_columns(cells):
        wide = jnp.pad(cells, [(0, 0)] * (cells.ndim - 2) + [(halo, halo), (0, 0)])
        pieces = jnp.stack([wide[..., own * i : own * i + window, :] for i in range(rings)])
        pieces = lax.all_to_all(pieces, "frame", 0, 0)
        pieces = jnp.moveaxis(pieces, 0, -4)
        return pieces.reshape(cells.shape[:-3] + (rows_n, window, group))

    mine = lax.dynamic_slice_in_dim(acts[0], chan_pos * group, group, 0)
    top = frames_all - BLOCK_FRAMES
    relayed = lax.dynamic_slice_in_dim(upstream, (blocks_n - 1 - section_pos) * BLOCK_FRAMES, BLOCK_FRAMES, 1)
    pair = to_columns(jnp.stack([relayed, mine[:, top:]]).transpose(0, 2, 3, 4, 1))
    relayed = pair[0]
    rest = to_columns(mine[:, :top].transpose(1, 2, 3, 0))
    stored = [pair[1]]
    for order in range(1, blocks_n):
        first = top - order * BLOCK_FRAMES
        stored.append(rest[first : first + BLOCK_FRAMES])

    shared = group % 128 == 0
    values = (mine if shared else acts[0]).astype(F32)
    feature_part = (values * jax.nn.sigmoid(values)).astype(BF16).transpose(2, 1, 3, 0)
    feature_part = feature_part.reshape(rows_l, frames_all * width_n, -1)

    column = ring_pos * own - halo + jnp.arange(window)
    inside = jnp.logical_and(column >= 0, column < width_n)[None, None, :, None]
    later = jnp.zeros((BLOCK_FRAMES, rows_n, window, group), BF16)
    current = jnp.where(section_pos == 0, relayed, later)
    held, gathered, results = [], [], []
    for tick in range(ticks):
        if tick == 1:
            feature_part, current, stored[-1] = lax.optimization_barrier((feature_part, current, stored[-1]))
            feature_all = lax.all_gather(feature_part, ("frame", "chan") if shared else "frame")
            feature_all = feature_all.reshape(rings, chans if shared else 1, *feature_part.shape)
        if tick == ticks - 2:
            current, feature_all = lax.optimization_barrier((current, feature_all))
        held.append(current[:, :, halo : halo + own])
        if tick in (ticks - 1 - blocks_n // 2, ticks - 1):
            begin = len(gathered) * (blocks_n // 2)
            taken = jnp.stack(held[begin:])
            taken = lax.dynamic_slice_in_dim(taken, section_pos, blocks_n // 2, 0)[::-1]
            taken, current = lax.optimization_barrier((taken, current))
            taken = taken.reshape(half, rows_n, own, group)
            if begin and rings <= 4:
                pairs = [[(i, (i + step) % rings) for i in range(rings)] for step in range(1, rings)]
                gathered.append([taken] + [lax.ppermute(taken, "frame", pair) for pair in pairs])
            else:
                gathered.append([lax.all_gather(taken, "frame")])
        partial = back_block(current, later, kernels)
        if tick == ticks - 1:
            partial, gathered[0] = lax.optimization_barrier((partial, gathered[0]))
        summed = lax.dynamic_slice_in_dim(partial, chan_pos * group, group, 1).astype(F32)
        for step in range(1, chans):
            there = lax.rem(chan_pos + step, chans)
            piece = lax.dynamic_slice_in_dim(partial, there * group, group, 1)
            arrived = lax.ppermute(piece, "chan", [(i, (i + step) % chans) for i in range(chans)])
            summed = summed + arrived.astype(F32)
        known = jnp.stack(stored[: tick + 1])
        place = jnp.clip(tick - section_pos, 0, known.shape[0] - 1)
        slot = lax.dynamic_index_in_dim(known, place, 0, keepdims=False).astype(F32)
        logistic = jax.nn.sigmoid(slot)
        slope = logistic * (1.0 + slot * (1.0 - logistic))
        updated = current.astype(F32) + slope * summed.reshape(current.shape)
        updated = jnp.where(inside, updated, 0.0).astype(BF16)
        results.append(updated[:, :, halo : halo + own])
        later = current
        if tick + 1 < ticks:
            pairs = [(i, i + 1) for i in range(sections - 1) if i <= tick < i + blocks_n]
            if tick + 1 < sections:
                updated = jnp.where(section_pos == tick + 1, relayed, updated)
                pairs.append((tick + 1, 0))
            current = lax.ppermute(updated, "section", pairs)

    if own % 16 and rings > 4:
        gathered = [
            [block.transpose(1, 2, 0, 3, 4).reshape(1, half, rows_n, width_n, group)] for (block,) in gathered
        ]
    kernel_sum = kernel_gradient(half, gathered[0], feature_all, ring_pos, None)

    outs = lax.dynamic_slice_in_dim(jnp.stack(results), section_pos, blocks_n, 0)[::-1]
    outs = outs.reshape(frames_all, rings, rows_l, own, group).transpose(1, 0, 2, 3, 4)
    outs, gathered[1], kernel_sum = lax.optimization_barrier((outs, gathered[1], kernel_sum))
    outs = lax.all_to_all(outs, "frame", 0, 0)
    kernel_total = kernel_gradient(0, gathered[1], feature_all, ring_pos, kernel_sum)
    outs, kernel_total = lax.optimization_barrier((outs, kernel_total))
    outs = outs.transpose(4, 1, 2, 0, 3).reshape(group, frames_all, rows_l, width_n)
    return (outs[None], kernel_total[None])


def solution(mesh):
    placed = (
        P("chan", None, "frame", None),
        P("section", None, None, "frame", None),
        P("section", None, "chan", None),
    )
    return jax.shard_map(
        body,
        mesh=mesh,
        in_specs=placed,
        out_specs=(P("section", "chan", None, "frame", None), P("section", None, "chan", None)),
        check_vma=False,
    )
```

```python
import functools

import jax
import jax.numpy as jnp
from jax import lax
from jax.experimental import pallas as pl
from jax.experimental.pallas import tpu as pltpu
from jax.sharding import PartitionSpec as P

BLOCK_FRAMES = 2
F32 = jnp.float32
BF16 = jnp.bfloat16


def back_kernel(cur_ref, later_ref, w_ref, out_ref, spread, acc):
    frames_n, rows_n, width_n, group = cur_ref.shape
    empty = jnp.zeros((width_n, 3 * group), F32)
    for frame in range(2 * frames_n):
        spread[frame, 0] = empty
        spread[frame, rows_n + 1] = empty
        for row in range(rows_n):
            source = cur_ref[frame, row] if frame < frames_n else later_ref[frame - frames_n, row]
            cells = source.astype(F32)
            spread[frame, row + 1, :, 0:group] = pltpu.roll(cells, width_n - 1, 0)
            spread[frame, row + 1, :, group : 2 * group] = cells
            spread[frame, row + 1, :, 2 * group : 3 * group] = pltpu.roll(cells, 1, 0)
    for step in range(9):
        lag, offset = step // 3, 2 - step % 3
        taken = spread[lag : lag + frames_n, offset : offset + rows_n]
        taken = taken.reshape(frames_n * rows_n * width_n, 3 * group).astype(BF16)
        part = jnp.dot(
            taken, w_ref[3 * step : 3 * step + 3].reshape(3 * group, -1), preferred_element_type=F32
        )
        if step == 0:
            acc[...] = part
        elif step < 8:
            acc[...] += part
        else:
            out_ref[...] = (acc[...] + part).astype(BF16)


def back_block(current, later, kernels):
    frames_n, rows_n, width_n, group = current.shape
    channels = kernels.shape[2]
    cells = frames_n * rows_n * width_n
    held = pl.BlockSpec(memory_space=pltpu.VMEM)
    return pl.pallas_call(
        back_kernel,
        in_specs=[held, held, held],
        out_specs=held,
        out_shape=jax.ShapeDtypeStruct((cells, channels), BF16),
        scratch_shapes=[
            pltpu.VMEM((2 * frames_n, rows_n + 2, width_n, 3 * group), F32),
            pltpu.VMEM((cells, channels), F32),
        ],
        compiler_params=pltpu.CompilerParams(vmem_limit_bytes=24 * 2**20),
        cost_estimate=pl.CostEstimate(
            flops=54 * group * channels * cells, bytes_accessed=54 * group * channels, transcendentals=0
        ),
    )(current, later, kernels)


def tap_kernel(first, f_first, has_sum, *refs):
    ring_ref, parts_ref, *refs = refs
    sum_ref = refs.pop(0) if has_sum else None
    out_ref, cells_ref, sides, feature_ref, total, g_here, f_here = refs[-7:]
    grad_refs = refs[:-7]
    step = pl.program_id(0)
    pieces_n, frames_n, rows_n, own, group = cells_ref.shape
    rings, chans, rows_l, _, width_c = parts_ref.shape
    width_n = pieces_n * own
    held_n = feature_ref.shape[2] // width_n

    @pl.when(step == 0)
    def _():
        g_copies, f_copies = [], []
        for piece in range(pieces_n):
            if len(grad_refs) == 1:
                source, target = grad_refs[0].at[piece], cells_ref.at[piece]
            else:
                source, target = grad_refs[piece], cells_ref.at[lax.rem(ring_ref[0] + pieces_n - piece, pieces_n)]
            g_copies.append(pltpu.make_async_copy(source, target, g_here.at[piece]))
        for ring in range(rings):
            for chan in range(chans):
                f_copies.append(
                    pltpu.make_async_copy(
                        parts_ref.at[ring, chan, :, pl.ds(f_first * width_n, held_n * width_n)],
                        feature_ref.at[chan, pl.ds(ring * rows_l, rows_l)],
                        f_here.at[ring * chans + chan],
                    )
                )
        for copy in g_copies + f_copies:
            copy.start()
        same = lax.broadcasted_iota(jnp.int32, (group, group), 0) == lax.broadcasted_iota(jnp.int32, (group, group), 1)
        identity = jnp.where(same, 1.0, 0.0).astype(BF16)
        source = lax.broadcasted_iota(jnp.int32, (width_n, 2 * width_n), 0)
        target = lax.broadcasted_iota(jnp.int32, (width_n, 2 * width_n), 1)
        moved = (source == target + 1) & (target < width_n) | (source == target - width_n - 1)
        shifts = jnp.where(moved, 1.0, 0.0).astype(BF16)
        edge = jnp.zeros((3 * group, frames_n * width_n), BF16)
        sides[:, 0 : frames_n * width_n] = edge
        sides[:, (rows_n + 1) * frames_n * width_n :] = edge
        for copy in g_copies:
            copy.wait()
        for frame in range(frames_n):
            joined = [cells_ref[piece, frame, row] for row in range(rows_n) for piece in range(pieces_n)]
            turned = lax.dot_general(
                identity,
                jnp.concatenate(joined, axis=0),
                (((1,), (1,)), ((), ())),
                preferred_element_type=F32,
            ).astype(BF16)
            for row in range(rows_n):
                start = ((row + 1) * frames_n + frame) * width_n
                cells = turned[:, row * width_n : (row + 1) * width_n]
                both = jnp.dot(cells, shifts, preferred_element_type=F32).astype(BF16)
                sides[0:group, start : start + width_n] = both[:, :width_n]
                sides[group : 2 * group, start : start + width_n] = cells
                sides[2 * group : 3 * group, start : start + width_n] = both[:, width_n:]
        for copy in f_copies:
            copy.wait()

    offset = 2 - step % 3
    for lag in range(3):

        @pl.when(step // 3 == lag)
        def _():
            skipped = max(0, lag - first)
            span = (frames_n - skipped) * width_n
            low = (first + skipped - lag - f_first) * width_n
            starts = [((row + offset) * frames_n + skipped) * width_n for row in range(rows_n)]
            lefts = [sides[:, pl.ds(pl.multiple_of(start, 128), span)] for start in starts] if has_sum else None
            for chan in range(chans):
                lanes = slice(chan * width_c, (chan + 1) * width_c)
                if has_sum:
                    rights = [feature_ref[chan, row, low : low + span] for row in range(rows_n)]
                    whole = jnp.dot(
                        jnp.concatenate(lefts, axis=1), jnp.concatenate(rights, axis=0), preferred_element_type=F32
                    ).reshape(3, group, width_c)
                    whole = whole + sum_ref[:, :, lanes].astype(F32)
                    out_ref[:, :, lanes] = whole.astype(out_ref.dtype)
                    continue
                for row in range(rows_n):
                    part = jnp.dot(
                        sides[:, pl.ds(pl.multiple_of(starts[row], 128), span)],
                        feature_ref[chan, row, low : low + span],
                        preferred_element_type=F32,
                    )
                    if row == 0:
                        total[...] = part
                    elif row < rows_n - 1:
                        total[...] += part
                    else:
                        whole = (total[...] + part).reshape(3, group, width_c)
                        out_ref[:, :, lanes] = whole.astype(out_ref.dtype)


def kernel_gradient(first, grads, parts, ring_pos, known):
    held = grads[0].shape if len(grads) == 1 else (len(grads),) + grads[0].shape
    pieces_n, frames_n, rows_n, own, group = held
    rings, chans, rows_l, _, width_c = parts.shape
    channels = chans * width_c
    width_n = pieces_n * own
    f_first = max(0, first - 2)
    held_n = first + frames_n - f_first
    far = pl.BlockSpec(memory_space=pltpu.HBM)
    out_spec = pl.BlockSpec((3, group, channels), lambda step: (step, 0, 0))
    has_sum = known is not None
    return pl.pallas_call(
        functools.partial(tap_kernel, first, f_first, has_sum),
        grid=(9,),
        in_specs=[pl.BlockSpec(memory_space=pltpu.SMEM), far] + [out_spec] * has_sum + [far] * len(grads),
        out_specs=out_spec,
        out_shape=jax.ShapeDtypeStruct((27, group, channels), BF16),
        scratch_shapes=[
            pltpu.VMEM(held, BF16),
            pltpu.VMEM((3 * group, (rows_n + 2) * frames_n * width_n), BF16),
            pltpu.VMEM((chans, rows_n, held_n * width_n, width_c), BF16),
            pltpu.VMEM((3 * group, width_c), F32),
            pltpu.SemaphoreType.DMA((pieces_n,)),
            pltpu.SemaphoreType.DMA((rings * chans,)),
        ],
        compiler_params=pltpu.CompilerParams(vmem_limit_bytes=58 * 2**20),
        cost_estimate=pl.CostEstimate(
            flops=54 * group * channels * rows_n * frames_n * width_n,
            bytes_accessed=6 * 27 * group * channels,
            transcendentals=0,
        ),
    )(*([ring_pos.reshape(1), parts] + [known] * has_sum + grads))


def body(upstream, acts, weights):
    group, frames_all, rows_l, width_n = upstream.shape
    sections, rings, chans = lax.axis_size("section"), lax.axis_size("frame"), lax.axis_size("chan")
    section_pos, ring_pos, chan_pos = lax.axis_index("section"), lax.axis_index("frame"), lax.axis_index("chan")
    rows_n = rows_l * rings
    own = width_n // rings
    halo = sections
    window = own + 2 * halo
    blocks_n = frames_all // BLOCK_FRAMES
    assert blocks_n == sections
    half = frames_all // 2
    ticks = blocks_n + sections - 1
    kernels = weights[0]

    def to_columns(cells):
        wide = jnp.pad(cells, [(0, 0)] * (cells.ndim - 2) + [(halo, halo), (0, 0)])
        pieces = jnp.stack([wide[..., own * i : own * i + window, :] for i in range(rings)])
        pieces = lax.all_to_all(pieces, "frame", 0, 0)
        pieces = jnp.moveaxis(pieces, 0, -4)
        return pieces.reshape(cells.shape[:-3] + (rows_n, window, group))

    mine = lax.dynamic_slice_in_dim(acts[0], chan_pos * group, group, 0)
    top = frames_all - BLOCK_FRAMES
    relayed = lax.dynamic_slice_in_dim(upstream, (blocks_n - 1 - section_pos) * BLOCK_FRAMES, BLOCK_FRAMES, 1)
    pair = to_columns(jnp.stack([relayed, mine[:, top:]]).transpose(0, 2, 3, 4, 1))
    relayed = pair[0]
    rest = to_columns(mine[:, :top].transpose(1, 2, 3, 0))
    stored = [pair[1]]
    for order in range(1, blocks_n):
        first = top - order * BLOCK_FRAMES
        stored.append(rest[first : first + BLOCK_FRAMES])

    shared = group % 128 == 0
    values = (mine if shared else acts[0]).astype(F32)
    feature_part = (values * jax.nn.sigmoid(values)).astype(BF16).transpose(2, 1, 3, 0)
    feature_part = feature_part.reshape(rows_l, frames_all * width_n, -1)

    column = ring_pos * own - halo + jnp.arange(window)
    inside = jnp.logical_and(column >= 0, column < width_n)[None, None, :, None]
    later = jnp.zeros((BLOCK_FRAMES, rows_n, window, group), BF16)
    current = jnp.where(section_pos == 0, relayed, later)
    held, gathered, results = [], [], []
    for tick in range(ticks):
        if tick == 1:
            feature_part, current, stored[-1] = lax.optimization_barrier((feature_part, current, stored[-1]))
            feature_all = lax.all_gather(feature_part, ("frame", "chan") if shared else "frame")
            feature_all = feature_all.reshape(rings, chans if shared else 1, *feature_part.shape)
        if tick == ticks - 2:
            current, feature_all = lax.optimization_barrier((current, feature_all))
        held.append(current[:, :, halo : halo + own])
        if tick in (ticks - 1 - blocks_n // 2, ticks - 1):
            begin = len(gathered) * (blocks_n // 2)
            taken = jnp.stack(held[begin:])
            taken = lax.dynamic_slice_in_dim(taken, section_pos, blocks_n // 2, 0)[::-1]
            taken, current = lax.optimization_barrier((taken, current))
            taken = taken.reshape(half, rows_n, own, group)
            if not begin:
                gathered.append([lax.all_gather(taken, "frame")])
        partial = back_block(current, later, kernels)
        if tick == ticks - 1:
            partial, gathered[0], taken = lax.optimization_barrier((partial, gathered[0], taken))
            if rings <= 4:
                pairs = [[(i, (i + step) % rings) for i in range(rings)] for step in range(1, rings)]
                gathered.append([taken] + [lax.ppermute(taken, "frame", pair) for pair in pairs])
            else:
                gathered.append([lax.all_gather(taken, "frame")])
        summed = lax.dynamic_slice_in_dim(partial, chan_pos * group, group, 1).astype(F32)
        for step in range(1, chans):
            there = lax.rem(chan_pos + step, chans)
            piece = lax.dynamic_slice_in_dim(partial, there * group, group, 1)
            arrived = lax.ppermute(piece, "chan", [(i, (i + step) % chans) for i in range(chans)])
            summed = summed + arrived.astype(F32)
        known = jnp.stack(stored[: tick + 1])
        place = jnp.clip(tick - section_pos, 0, known.shape[0] - 1)
        slot = lax.dynamic_index_in_dim(known, place, 0, keepdims=False).astype(F32)
        logistic = jax.nn.sigmoid(slot)
        slope = logistic * (1.0 + slot * (1.0 - logistic))
        updated = current.astype(F32) + slope * summed.reshape(current.shape)
        updated = jnp.where(inside, updated, 0.0).astype(BF16)
        results.append(updated[:, :, halo : halo + own])
        later = current
        if tick + 1 < ticks:
            pairs = [(i, i + 1) for i in range(sections - 1) if i <= tick < i + blocks_n]
            if tick + 1 < sections:
                updated = jnp.where(section_pos == tick + 1, relayed, updated)
                pairs.append((tick + 1, 0))
            current = lax.ppermute(updated, "section", pairs)

    if own % 16 and rings > 4:
        gathered = [
            [block.transpose(1, 2, 0, 3, 4).reshape(1, half, rows_n, width_n, group)] for (block,) in gathered
        ]
    kernel_sum = kernel_gradient(half, gathered[0], feature_all, ring_pos, None)

    outs = lax.dynamic_slice_in_dim(jnp.stack(results), section_pos, blocks_n, 0)[::-1]
    outs = outs.reshape(frames_all, rings, rows_l, own, group).transpose(1, 0, 2, 3, 4)
    outs, gathered[1], kernel_sum = lax.optimization_barrier((outs, gathered[1], kernel_sum))
    outs = lax.all_to_all(outs, "frame", 0, 0)
    kernel_total = kernel_gradient(0, gathered[1], feature_all, ring_pos, kernel_sum)
    outs, kernel_total = lax.optimization_barrier((outs, kernel_total))
    outs = outs.transpose(4, 1, 2, 0, 3).reshape(group, frames_all, rows_l, width_n)
    return (outs[None], kernel_total[None])


def solution(mesh):
    placed = (
        P("chan", None, "frame", None),
        P("section", None, None, "frame", None),
        P("section", None, "chan", None),
    )
    return jax.shard_map(
        body,
        mesh=mesh,
        in_specs=placed,
        out_specs=(P("section", "chan", None, "frame", None), P("section", None, "chan", None)),
        check_vma=False,
    )
```

```python
import functools

import jax
import jax.numpy as jnp
from jax import lax
from jax.experimental import pallas as pl
from jax.experimental.pallas import tpu as pltpu
from jax.sharding import PartitionSpec as P

BLOCK_FRAMES = 2
F32 = jnp.float32
BF16 = jnp.bfloat16


def back_kernel(cur_ref, later_ref, w_ref, out_ref, spread, acc):
    frames_n, rows_n, width_n, group = cur_ref.shape
    empty = jnp.zeros((width_n, 3 * group), F32)
    for frame in range(2 * frames_n):
        spread[frame, 0] = empty
        spread[frame, rows_n + 1] = empty
        for row in range(rows_n):
            source = cur_ref[frame, row] if frame < frames_n else later_ref[frame - frames_n, row]
            cells = source.astype(F32)
            spread[frame, row + 1, :, 0:group] = pltpu.roll(cells, width_n - 1, 0)
            spread[frame, row + 1, :, group : 2 * group] = cells
            spread[frame, row + 1, :, 2 * group : 3 * group] = pltpu.roll(cells, 1, 0)
    for step in range(9):
        lag, offset = step // 3, 2 - step % 3
        taken = spread[lag : lag + frames_n, offset : offset + rows_n]
        taken = taken.reshape(frames_n * rows_n * width_n, 3 * group).astype(BF16)
        part = jnp.dot(
            taken, w_ref[3 * step : 3 * step + 3].reshape(3 * group, -1), preferred_element_type=F32
        )
        if step == 0:
            acc[...] = part
        elif step < 8:
            acc[...] += part
        else:
            out_ref[...] = (acc[...] + part).astype(BF16)


def back_block(current, later, kernels):
    frames_n, rows_n, width_n, group = current.shape
    channels = kernels.shape[2]
    cells = frames_n * rows_n * width_n
    held = pl.BlockSpec(memory_space=pltpu.VMEM)
    return pl.pallas_call(
        back_kernel,
        in_specs=[held, held, held],
        out_specs=held,
        out_shape=jax.ShapeDtypeStruct((cells, channels), BF16),
        scratch_shapes=[
            pltpu.VMEM((2 * frames_n, rows_n + 2, width_n, 3 * group), F32),
            pltpu.VMEM((cells, channels), F32),
        ],
        compiler_params=pltpu.CompilerParams(vmem_limit_bytes=24 * 2**20),
        cost_estimate=pl.CostEstimate(
            flops=54 * group * channels * cells, bytes_accessed=54 * group * channels, transcendentals=0
        ),
    )(current, later, kernels)


def tap_kernel(first, f_first, has_sum, *refs):
    ring_ref, parts_ref, *refs = refs
    sum_ref = refs.pop(0) if has_sum else None
    out_ref, cells_ref, sides, feature_ref, total, g_here, f_here = refs[-7:]
    grad_refs = refs[:-7]
    step = pl.program_id(0)
    pieces_n, frames_n, rows_n, own, group = cells_ref.shape
    rings, chans, rows_l, _, width_c = parts_ref.shape
    width_n = pieces_n * own
    held_n = feature_ref.shape[2] // width_n

    @pl.when(step == 0)
    def _():
        g_copies, f_copies = [], []
        for piece in range(pieces_n):
            if len(grad_refs) == 1:
                source, target = grad_refs[0].at[piece], cells_ref.at[piece]
            else:
                source, target = grad_refs[piece], cells_ref.at[lax.rem(ring_ref[0] + pieces_n - piece, pieces_n)]
            g_copies.append(pltpu.make_async_copy(source, target, g_here.at[piece]))
        for ring in range(rings):
            for chan in range(chans):
                f_copies.append(
                    pltpu.make_async_copy(
                        parts_ref.at[ring, chan, :, pl.ds(f_first * width_n, held_n * width_n)],
                        feature_ref.at[chan, pl.ds(ring * rows_l, rows_l)],
                        f_here.at[ring * chans + chan],
                    )
                )
        for copy in g_copies + f_copies:
            copy.start()
        same = lax.broadcasted_iota(jnp.int32, (group, group), 0) == lax.broadcasted_iota(jnp.int32, (group, group), 1)
        identity = jnp.where(same, 1.0, 0.0).astype(BF16)
        source = lax.broadcasted_iota(jnp.int32, (width_n, 2 * width_n), 0)
        target = lax.broadcasted_iota(jnp.int32, (width_n, 2 * width_n), 1)
        moved = (source == target + 1) & (target < width_n) | (source == target - width_n - 1)
        shifts = jnp.where(moved, 1.0, 0.0).astype(BF16)
        edge = jnp.zeros((3 * group, frames_n * width_n), BF16)
        sides[:, 0 : frames_n * width_n] = edge
        sides[:, (rows_n + 1) * frames_n * width_n :] = edge
        for copy in g_copies:
            copy.wait()
        for frame in range(frames_n):
            held = frames_n - (frame // BLOCK_FRAMES + 1) * BLOCK_FRAMES + frame % BLOCK_FRAMES
            joined = [cells_ref[piece, held, row] for row in range(rows_n) for piece in range(pieces_n)]
            turned = lax.dot_general(
                identity,
                jnp.concatenate(joined, axis=0),
                (((1,), (1,)), ((), ())),
                preferred_element_type=F32,
            ).astype(BF16)
            for row in range(rows_n):
                start = ((row + 1) * frames_n + frame) * width_n
                cells = turned[:, row * width_n : (row + 1) * width_n]
                both = jnp.dot(cells, shifts, preferred_element_type=F32).astype(BF16)
                sides[0:group, start : start + width_n] = both[:, :width_n]
                sides[group : 2 * group, start : start + width_n] = cells
                sides[2 * group : 3 * group, start : start + width_n] = both[:, width_n:]
        for copy in f_copies:
            copy.wait()

    offset = 2 - step % 3
    for lag in range(3):

        @pl.when(step // 3 == lag)
        def _():
            skipped = max(0, lag - first)
            span = (frames_n - skipped) * width_n
            low = (first + skipped - lag - f_first) * width_n
            starts = [((row + offset) * frames_n + skipped) * width_n for row in range(rows_n)]
            lefts = [sides[:, pl.ds(pl.multiple_of(start, 128), span)] for start in starts] if has_sum else None
            for chan in range(chans):
                lanes = slice(chan * width_c, (chan + 1) * width_c)
                if has_sum:
                    rights = [feature_ref[chan, row, low : low + span] for row in range(rows_n)]
                    whole = jnp.dot(
                        jnp.concatenate(lefts, axis=1), jnp.concatenate(rights, axis=0), preferred_element_type=F32
                    ).reshape(3, group, width_c)
                    whole = whole + sum_ref[:, :, lanes].astype(F32)
                    out_ref[:, :, lanes] = whole.astype(out_ref.dtype)
                    continue
                for row in range(rows_n):
                    part = jnp.dot(
                        sides[:, pl.ds(pl.multiple_of(starts[row], 128), span)],
                        feature_ref[chan, row, low : low + span],
                        preferred_element_type=F32,
                    )
                    if row == 0:
                        total[...] = part
                    elif row < rows_n - 1:
                        total[...] += part
                    else:
                        whole = (total[...] + part).reshape(3, group, width_c)
                        out_ref[:, :, lanes] = whole.astype(out_ref.dtype)


def kernel_gradient(first, grads, parts, ring_pos, known):
    held = grads[0].shape if len(grads) == 1 else (len(grads),) + grads[0].shape
    pieces_n, frames_n, rows_n, own, group = held
    rings, chans, rows_l, _, width_c = parts.shape
    channels = chans * width_c
    width_n = pieces_n * own
    f_first = max(0, first - 2)
    held_n = first + frames_n - f_first
    far = pl.BlockSpec(memory_space=pltpu.HBM)
    out_spec = pl.BlockSpec((3, group, channels), lambda step: (step, 0, 0))
    has_sum = known is not None
    return pl.pallas_call(
        functools.partial(tap_kernel, first, f_first, has_sum),
        grid=(9,),
        in_specs=[pl.BlockSpec(memory_space=pltpu.SMEM), far] + [out_spec] * has_sum + [far] * len(grads),
        out_specs=out_spec,
        out_shape=jax.ShapeDtypeStruct((27, group, channels), BF16),
        scratch_shapes=[
            pltpu.VMEM(held, BF16),
            pltpu.VMEM((3 * group, (rows_n + 2) * frames_n * width_n), BF16),
            pltpu.VMEM((chans, rows_n, held_n * width_n, width_c), BF16),
            pltpu.VMEM((3 * group, width_c), F32),
            pltpu.SemaphoreType.DMA((pieces_n,)),
            pltpu.SemaphoreType.DMA((rings * chans,)),
        ],
        compiler_params=pltpu.CompilerParams(vmem_limit_bytes=58 * 2**20),
        cost_estimate=pl.CostEstimate(
            flops=54 * group * channels * rows_n * frames_n * width_n,
            bytes_accessed=6 * 27 * group * channels,
            transcendentals=0,
        ),
    )(*([ring_pos.reshape(1), parts] + [known] * has_sum + grads))


def body(upstream, acts, weights):
    group, frames_all, rows_l, width_n = upstream.shape
    sections, rings, chans = lax.axis_size("section"), lax.axis_size("frame"), lax.axis_size("chan")
    section_pos, ring_pos, chan_pos = lax.axis_index("section"), lax.axis_index("frame"), lax.axis_index("chan")
    rows_n = rows_l * rings
    own = width_n // rings
    halo = sections
    window = own + 2 * halo
    blocks_n = frames_all // BLOCK_FRAMES
    assert blocks_n == sections
    half = frames_all // 2
    ticks = blocks_n + sections - 1
    kernels = weights[0]

    def to_columns(cells):
        wide = jnp.pad(cells, [(0, 0)] * (cells.ndim - 2) + [(halo, halo), (0, 0)])
        pieces = jnp.stack([wide[..., own * i : own * i + window, :] for i in range(rings)])
        pieces = lax.all_to_all(pieces, "frame", 0, 0)
        pieces = jnp.moveaxis(pieces, 0, -4)
        return pieces.reshape(cells.shape[:-3] + (rows_n, window, group))

    mine = lax.dynamic_slice_in_dim(acts[0], chan_pos * group, group, 0)
    top = frames_all - BLOCK_FRAMES
    relayed = lax.dynamic_slice_in_dim(upstream, (blocks_n - 1 - section_pos) * BLOCK_FRAMES, BLOCK_FRAMES, 1)
    pair = to_columns(jnp.stack([relayed, mine[:, top:]]).transpose(0, 2, 3, 4, 1))
    relayed = pair[0]
    rest = to_columns(mine[:, :top].transpose(1, 2, 3, 0))
    stored = [pair[1]]
    for order in range(1, blocks_n):
        first = top - order * BLOCK_FRAMES
        stored.append(rest[first : first + BLOCK_FRAMES])

    shared = group % 128 == 0
    values = (mine if shared else acts[0]).astype(F32)
    feature_part = (values * jax.nn.sigmoid(values)).astype(BF16).transpose(2, 1, 3, 0)
    feature_part = feature_part.reshape(rows_l, frames_all * width_n, -1)

    column = ring_pos * own - halo + jnp.arange(window)
    inside = jnp.logical_and(column >= 0, column < width_n)[None, None, :, None]
    later = jnp.zeros((BLOCK_FRAMES, rows_n, window, group), BF16)
    current = jnp.where(section_pos == 0, relayed, later)
    held, gathered, results = [], [], []
    for tick in range(ticks):
        if tick == 1:
            feature_part, current, stored[-1] = lax.optimization_barrier((feature_part, current, stored[-1]))
            feature_all = lax.all_gather(feature_part, ("frame", "chan") if shared else "frame")
            feature_all = feature_all.reshape(rings, chans if shared else 1, *feature_part.shape)
        if tick == ticks - 2:
            current, feature_all = lax.optimization_barrier((current, feature_all))
        held.append(current[:, :, halo : halo + own])
        if tick in (ticks - 1 - blocks_n // 2, ticks - 1):
            begin = len(gathered) * (blocks_n // 2)
            taken = jnp.stack(held[begin:])
            taken = lax.dynamic_slice_in_dim(taken, section_pos, blocks_n // 2, 0)
            taken, current = lax.optimization_barrier((taken, current))
            taken = taken.reshape(half, rows_n, own, group)
            if not begin:
                gathered.append([lax.all_gather(taken, "frame")])
        partial = back_block(current, later, kernels)
        if tick == ticks - 1:
            partial, gathered[0], taken = lax.optimization_barrier((partial, gathered[0], taken))
            if rings <= 4:
                pairs = [[(i, (i + step) % rings) for i in range(rings)] for step in range(1, rings)]
                gathered.append([taken] + [lax.ppermute(taken, "frame", pair) for pair in pairs])
            else:
                gathered.append([lax.all_gather(taken, "frame")])
        summed = lax.dynamic_slice_in_dim(partial, chan_pos * group, group, 1).astype(F32)
        for step in range(1, chans):
            there = lax.rem(chan_pos + step, chans)
            piece = lax.dynamic_slice_in_dim(partial, there * group, group, 1)
            arrived = lax.ppermute(piece, "chan", [(i, (i + step) % chans) for i in range(chans)])
            summed = summed + arrived.astype(F32)
        known = jnp.stack(stored[: tick + 1])
        place = jnp.clip(tick - section_pos, 0, known.shape[0] - 1)
        slot = lax.dynamic_index_in_dim(known, place, 0, keepdims=False).astype(F32)
        logistic = jax.nn.sigmoid(slot)
        slope = logistic * (1.0 + slot * (1.0 - logistic))
        updated = current.astype(F32) + slope * summed.reshape(current.shape)
        updated = jnp.where(inside, updated, 0.0).astype(BF16)
        results.append(updated[:, :, halo : halo + own])
        later = current
        if tick + 1 < ticks:
            pairs = [(i, i + 1) for i in range(sections - 1) if i <= tick < i + blocks_n]
            if tick + 1 < sections:
                updated = jnp.where(section_pos == tick + 1, relayed, updated)
                pairs.append((tick + 1, 0))
            current = lax.ppermute(updated, "section", pairs)

    if own % 16 and rings > 4:
        gathered = [
            [block.transpose(1, 2, 0, 3, 4).reshape(1, half, rows_n, width_n, group)] for (block,) in gathered
        ]
    kernel_sum = kernel_gradient(half, gathered[0], feature_all, ring_pos, None)

    outs = lax.dynamic_slice_in_dim(jnp.stack(results), section_pos, blocks_n, 0)[::-1]
    outs = outs.reshape(frames_all, rings, rows_l, own, group).transpose(1, 0, 2, 3, 4)
    outs, gathered[1], kernel_sum = lax.optimization_barrier((outs, gathered[1], kernel_sum))
    outs = lax.all_to_all(outs, "frame", 0, 0)
    kernel_total = kernel_gradient(0, gathered[1], feature_all, ring_pos, kernel_sum)
    outs, kernel_total = lax.optimization_barrier((outs, kernel_total))
    outs = outs.transpose(4, 1, 2, 0, 3).reshape(group, frames_all, rows_l, width_n)
    return (outs[None], kernel_total[None])


def solution(mesh):
    placed = (
        P("chan", None, "frame", None),
        P("section", None, None, "frame", None),
        P("section", None, "chan", None),
    )
    return jax.shard_map(
        body,
        mesh=mesh,
        in_specs=placed,
        out_specs=(P("section", "chan", None, "frame", None), P("section", None, "chan", None)),
        check_vma=False,
    )
```

```python
import functools

import jax
import jax.numpy as jnp
from jax import lax
from jax.experimental import pallas as pl
from jax.experimental.pallas import tpu as pltpu
from jax.sharding import PartitionSpec as P

BLOCK_FRAMES = 2
F32 = jnp.float32
BF16 = jnp.bfloat16


def back_kernel(cur_ref, later_ref, w_ref, out_ref, spread, acc):
    frames_n, rows_n, width_n, group = cur_ref.shape
    empty = jnp.zeros((width_n, 3 * group), F32)
    for frame in range(2 * frames_n):
        spread[frame, 0] = empty
        spread[frame, rows_n + 1] = empty
        for row in range(rows_n):
            source = cur_ref[frame, row] if frame < frames_n else later_ref[frame - frames_n, row]
            cells = source.astype(F32)
            spread[frame, row + 1, :, 0:group] = pltpu.roll(cells, width_n - 1, 0)
            spread[frame, row + 1, :, group : 2 * group] = cells
            spread[frame, row + 1, :, 2 * group : 3 * group] = pltpu.roll(cells, 1, 0)
    for step in range(9):
        lag, offset = step // 3, 2 - step % 3
        taken = spread[lag : lag + frames_n, offset : offset + rows_n]
        taken = taken.reshape(frames_n * rows_n * width_n, 3 * group).astype(BF16)
        part = jnp.dot(
            taken, w_ref[3 * step : 3 * step + 3].reshape(3 * group, -1), preferred_element_type=F32
        )
        if step == 0:
            acc[...] = part
        elif step < 8:
            acc[...] += part
        else:
            out_ref[...] = (acc[...] + part).astype(BF16)


def back_block(current, later, kernels):
    frames_n, rows_n, width_n, group = current.shape
    channels = kernels.shape[2]
    cells = frames_n * rows_n * width_n
    held = pl.BlockSpec(memory_space=pltpu.VMEM)
    return pl.pallas_call(
        back_kernel,
        in_specs=[held, held, held],
        out_specs=held,
        out_shape=jax.ShapeDtypeStruct((cells, channels), BF16),
        scratch_shapes=[
            pltpu.VMEM((2 * frames_n, rows_n + 2, width_n, 3 * group), F32),
            pltpu.VMEM((cells, channels), F32),
        ],
        compiler_params=pltpu.CompilerParams(vmem_limit_bytes=24 * 2**20),
        cost_estimate=pl.CostEstimate(
            flops=54 * group * channels * cells, bytes_accessed=54 * group * channels, transcendentals=0
        ),
    )(current, later, kernels)


def tap_kernel(first, f_first, has_sum, *refs):
    ring_ref, parts_ref, *refs = refs
    sum_ref = refs.pop(0) if has_sum else None
    out_ref, cells_ref, sides, feature_ref, total, g_here, f_here = refs[-7:]
    grad_refs = refs[:-7]
    step = pl.program_id(0)
    pieces_n, frames_n, rows_n, own, group = cells_ref.shape
    rings, chans, rows_l, _, width_c = parts_ref.shape
    width_n = pieces_n * own
    held_n = feature_ref.shape[2] // width_n

    @pl.when(step == 0)
    def _():
        g_copies, f_copies = [], []
        for piece in range(pieces_n):
            if len(grad_refs) == 1:
                source, target = grad_refs[0].at[piece], cells_ref.at[piece]
            else:
                source, target = grad_refs[piece], cells_ref.at[lax.rem(ring_ref[0] + pieces_n - piece, pieces_n)]
            g_copies.append(pltpu.make_async_copy(source, target, g_here.at[piece]))
        for ring in range(rings):
            for chan in range(chans):
                f_copies.append(
                    pltpu.make_async_copy(
                        parts_ref.at[ring, chan, :, pl.ds(f_first * width_n, held_n * width_n)],
                        feature_ref.at[chan, pl.ds(ring * rows_l, rows_l)],
                        f_here.at[ring * chans + chan],
                    )
                )
        for copy in g_copies:
            copy.start()
        for copy in f_copies:
            copy.start(priority=1)
        same = lax.broadcasted_iota(jnp.int32, (group, group), 0) == lax.broadcasted_iota(jnp.int32, (group, group), 1)
        identity = jnp.where(same, 1.0, 0.0).astype(BF16)
        source = lax.broadcasted_iota(jnp.int32, (width_n, 2 * width_n), 0)
        target = lax.broadcasted_iota(jnp.int32, (width_n, 2 * width_n), 1)
        moved = (source == target + 1) & (target < width_n) | (source == target - width_n - 1)
        shifts = jnp.where(moved, 1.0, 0.0).astype(BF16)
        edge = jnp.zeros((3 * group, frames_n * width_n), BF16)
        sides[:, 0 : frames_n * width_n] = edge
        sides[:, (rows_n + 1) * frames_n * width_n :] = edge
        for copy in g_copies:
            copy.wait()
        for frame in range(frames_n):
            held = frames_n - (frame // BLOCK_FRAMES + 1) * BLOCK_FRAMES + frame % BLOCK_FRAMES
            joined = [cells_ref[piece, held, row] for row in range(rows_n) for piece in range(pieces_n)]
            turned = lax.dot_general(
                identity,
                jnp.concatenate(joined, axis=0),
                (((1,), (1,)), ((), ())),
                preferred_element_type=F32,
            ).astype(BF16)
            for row in range(rows_n):
                start = ((row + 1) * frames_n + frame) * width_n
                cells = turned[:, row * width_n : (row + 1) * width_n]
                both = jnp.dot(cells, shifts, preferred_element_type=F32).astype(BF16)
                sides[0:group, start : start + width_n] = both[:, :width_n]
                sides[group : 2 * group, start : start + width_n] = cells
                sides[2 * group : 3 * group, start : start + width_n] = both[:, width_n:]
        for copy in f_copies:
            copy.wait()

    offset = 2 - step % 3
    for lag in range(3):

        @pl.when(step // 3 == lag)
        def _():
            skipped = max(0, lag - first)
            span = (frames_n - skipped) * width_n
            low = (first + skipped - lag - f_first) * width_n
            starts = [((row + offset) * frames_n + skipped) * width_n for row in range(rows_n)]
            lefts = [sides[:, pl.ds(pl.multiple_of(start, 128), span)] for start in starts] if has_sum else None
            for chan in range(chans):
                lanes = slice(chan * width_c, (chan + 1) * width_c)
                if has_sum:
                    rights = [feature_ref[chan, row, low : low + span] for row in range(rows_n)]
                    whole = jnp.dot(
                        jnp.concatenate(lefts, axis=1), jnp.concatenate(rights, axis=0), preferred_element_type=F32
                    ).reshape(3, group, width_c)
                    whole = whole + sum_ref[:, :, lanes].astype(F32)
                    out_ref[:, :, lanes] = whole.astype(out_ref.dtype)
                    continue
                for row in range(rows_n):
                    part = jnp.dot(
                        sides[:, pl.ds(pl.multiple_of(starts[row], 128), span)],
                        feature_ref[chan, row, low : low + span],
                        preferred_element_type=F32,
                    )
                    if row == 0:
                        total[...] = part
                    elif row < rows_n - 1:
                        total[...] += part
                    else:
                        whole = (total[...] + part).reshape(3, group, width_c)
                        out_ref[:, :, lanes] = whole.astype(out_ref.dtype)


def kernel_gradient(first, grads, parts, ring_pos, known):
    held = grads[0].shape if len(grads) == 1 else (len(grads),) + grads[0].shape
    pieces_n, frames_n, rows_n, own, group = held
    rings, chans, rows_l, _, width_c = parts.shape
    channels = chans * width_c
    width_n = pieces_n * own
    f_first = max(0, first - 2)
    held_n = first + frames_n - f_first
    far = pl.BlockSpec(memory_space=pltpu.HBM)
    out_spec = pl.BlockSpec((3, group, channels), lambda step: (step, 0, 0))
    has_sum = known is not None
    return pl.pallas_call(
        functools.partial(tap_kernel, first, f_first, has_sum),
        grid=(9,),
        in_specs=[pl.BlockSpec(memory_space=pltpu.SMEM), far] + [out_spec] * has_sum + [far] * len(grads),
        out_specs=out_spec,
        out_shape=jax.ShapeDtypeStruct((27, group, channels), BF16),
        scratch_shapes=[
            pltpu.VMEM(held, BF16),
            pltpu.VMEM((3 * group, (rows_n + 2) * frames_n * width_n), BF16),
            pltpu.VMEM((chans, rows_n, held_n * width_n, width_c), BF16),
            pltpu.VMEM((3 * group, width_c), F32),
            pltpu.SemaphoreType.DMA((pieces_n,)),
            pltpu.SemaphoreType.DMA((rings * chans,)),
        ],
        compiler_params=pltpu.CompilerParams(vmem_limit_bytes=58 * 2**20),
        cost_estimate=pl.CostEstimate(
            flops=54 * group * channels * rows_n * frames_n * width_n,
            bytes_accessed=6 * 27 * group * channels,
            transcendentals=0,
        ),
    )(*([ring_pos.reshape(1), parts] + [known] * has_sum + grads))


def body(upstream, acts, weights):
    group, frames_all, rows_l, width_n = upstream.shape
    sections, rings, chans = lax.axis_size("section"), lax.axis_size("frame"), lax.axis_size("chan")
    section_pos, ring_pos, chan_pos = lax.axis_index("section"), lax.axis_index("frame"), lax.axis_index("chan")
    rows_n = rows_l * rings
    own = width_n // rings
    halo = sections
    window = own + 2 * halo
    blocks_n = frames_all // BLOCK_FRAMES
    assert blocks_n == sections
    half = frames_all // 2
    ticks = blocks_n + sections - 1
    kernels = weights[0]

    def to_columns(cells):
        wide = jnp.pad(cells, [(0, 0)] * (cells.ndim - 2) + [(halo, halo), (0, 0)])
        pieces = jnp.stack([wide[..., own * i : own * i + window, :] for i in range(rings)])
        pieces = lax.all_to_all(pieces, "frame", 0, 0)
        pieces = jnp.moveaxis(pieces, 0, -4)
        return pieces.reshape(cells.shape[:-3] + (rows_n, window, group))

    mine = lax.dynamic_slice_in_dim(acts[0], chan_pos * group, group, 0)
    top = frames_all - BLOCK_FRAMES
    relayed = lax.dynamic_slice_in_dim(upstream, (blocks_n - 1 - section_pos) * BLOCK_FRAMES, BLOCK_FRAMES, 1)
    pair = to_columns(jnp.stack([relayed, mine[:, top:]]).transpose(0, 2, 3, 4, 1))
    relayed = pair[0]
    rest = to_columns(mine[:, :top].transpose(1, 2, 3, 0))
    stored = [pair[1]]
    for order in range(1, blocks_n):
        first = top - order * BLOCK_FRAMES
        stored.append(rest[first : first + BLOCK_FRAMES])

    shared = group % 128 == 0
    values = (mine if shared else acts[0]).astype(F32)
    feature_part = (values * jax.nn.sigmoid(values)).astype(BF16).transpose(2, 1, 3, 0)
    feature_part = feature_part.reshape(rows_l, frames_all * width_n, -1)

    column = ring_pos * own - halo + jnp.arange(window)
    inside = jnp.logical_and(column >= 0, column < width_n)[None, None, :, None]
    later = jnp.zeros((BLOCK_FRAMES, rows_n, window, group), BF16)
    current = jnp.where(section_pos == 0, relayed, later)
    held, gathered, results = [], [], []
    for tick in range(ticks):
        if tick == 1:
            feature_part, current, stored[-1] = lax.optimization_barrier((feature_part, current, stored[-1]))
            feature_all = lax.all_gather(feature_part, ("frame", "chan") if shared else "frame")
            feature_all = feature_all.reshape(rings, chans if shared else 1, *feature_part.shape)
        if tick == ticks - 2:
            current, feature_all = lax.optimization_barrier((current, feature_all))
        held.append(current[:, :, halo : halo + own])
        if tick in (ticks - 1 - blocks_n // 2, ticks - 1):
            begin = len(gathered) * (blocks_n // 2)
            taken = jnp.stack(held[begin:])
            taken = lax.dynamic_slice_in_dim(taken, section_pos, blocks_n // 2, 0)
            taken, current = lax.optimization_barrier((taken, current))
            taken = taken.reshape(half, rows_n, own, group)
            if not begin:
                gathered.append([lax.all_gather(taken, "frame")])
        partial = back_block(current, later, kernels)
        if tick == ticks - 1:
            partial, gathered[0], taken = lax.optimization_barrier((partial, gathered[0], taken))
            if rings <= 4:
                pairs = [[(i, (i + step) % rings) for i in range(rings)] for step in range(1, rings)]
                gathered.append([taken] + [lax.ppermute(taken, "frame", pair) for pair in pairs])
            else:
                gathered.append([lax.all_gather(taken, "frame")])
        summed = lax.dynamic_slice_in_dim(partial, chan_pos * group, group, 1).astype(F32)
        for step in range(1, chans):
            there = lax.rem(chan_pos + step, chans)
            piece = lax.dynamic_slice_in_dim(partial, there * group, group, 1)
            arrived = lax.ppermute(piece, "chan", [(i, (i + step) % chans) for i in range(chans)])
            summed = summed + arrived.astype(F32)
        known = jnp.stack(stored[: tick + 1])
        place = jnp.clip(tick - section_pos, 0, known.shape[0] - 1)
        slot = lax.dynamic_index_in_dim(known, place, 0, keepdims=False).astype(F32)
        logistic = jax.nn.sigmoid(slot)
        slope = logistic * (1.0 + slot * (1.0 - logistic))
        updated = current.astype(F32) + slope * summed.reshape(current.shape)
        updated = jnp.where(inside, updated, 0.0).astype(BF16)
        results.append(updated[:, :, halo : halo + own])
        later = current
        if tick + 1 < ticks:
            pairs = [(i, i + 1) for i in range(sections - 1) if i <= tick < i + blocks_n]
            if tick + 1 < sections:
                updated = jnp.where(section_pos == tick + 1, relayed, updated)
                pairs.append((tick + 1, 0))
            current = lax.ppermute(updated, "section", pairs)

    if own % 16 and rings > 4:
        gathered = [
            [block.transpose(1, 2, 0, 3, 4).reshape(1, half, rows_n, width_n, group)] for (block,) in gathered
        ]
    kernel_sum = kernel_gradient(half, gathered[0], feature_all, ring_pos, None)

    outs = lax.dynamic_slice_in_dim(jnp.stack(results), section_pos, blocks_n, 0)[::-1]
    outs = outs.reshape(frames_all, rings, rows_l, own, group).transpose(1, 0, 2, 3, 4)
    outs, gathered[1], kernel_sum = lax.optimization_barrier((outs, gathered[1], kernel_sum))
    outs = lax.all_to_all(outs, "frame", 0, 0)
    kernel_total = kernel_gradient(0, gathered[1], feature_all, ring_pos, kernel_sum)
    outs, kernel_total = lax.optimization_barrier((outs, kernel_total))
    outs = outs.transpose(4, 1, 2, 0, 3).reshape(group, frames_all, rows_l, width_n)
    return (outs[None], kernel_total[None])


def solution(mesh):
    placed = (
        P("chan", None, "frame", None),
        P("section", None, None, "frame", None),
        P("section", None, "chan", None),
    )
    return jax.shard_map(
        body,
        mesh=mesh,
        in_specs=placed,
        out_specs=(P("section", "chan", None, "frame", None), P("section", None, "chan", None)),
        check_vma=False,
    )
```

```python
import functools

import jax
import jax.numpy as jnp
from jax import lax
from jax.experimental import pallas as pl
from jax.experimental.pallas import tpu as pltpu
from jax.sharding import PartitionSpec as P

BLOCK_FRAMES = 2
F32 = jnp.float32
BF16 = jnp.bfloat16


def back_kernel(cur_ref, later_ref, w_ref, out_ref, spread, acc):
    frames_n, rows_n, width_n, group = cur_ref.shape
    empty = jnp.zeros((width_n, 3 * group), F32)
    for frame in range(2 * frames_n):
        spread[frame, 0] = empty
        spread[frame, rows_n + 1] = empty
        for row in range(rows_n):
            source = cur_ref[frame, row] if frame < frames_n else later_ref[frame - frames_n, row]
            cells = source.astype(F32)
            spread[frame, row + 1, :, 0:group] = pltpu.roll(cells, width_n - 1, 0)
            spread[frame, row + 1, :, group : 2 * group] = cells
            spread[frame, row + 1, :, 2 * group : 3 * group] = pltpu.roll(cells, 1, 0)
    for step in range(9):
        lag, offset = step // 3, 2 - step % 3
        taken = spread[lag : lag + frames_n, offset : offset + rows_n]
        taken = taken.reshape(frames_n * rows_n * width_n, 3 * group).astype(BF16)
        part = jnp.dot(
            taken, w_ref[3 * step : 3 * step + 3].reshape(3 * group, -1), preferred_element_type=F32
        )
        if step == 0:
            acc[...] = part
        elif step < 8:
            acc[...] += part
        else:
            out_ref[...] = (acc[...] + part).astype(BF16)


def back_block(current, later, kernels):
    frames_n, rows_n, width_n, group = current.shape
    channels = kernels.shape[2]
    cells = frames_n * rows_n * width_n
    held = pl.BlockSpec(memory_space=pltpu.VMEM)
    return pl.pallas_call(
        back_kernel,
        in_specs=[held, held, held],
        out_specs=held,
        out_shape=jax.ShapeDtypeStruct((cells, channels), BF16),
        scratch_shapes=[
            pltpu.VMEM((2 * frames_n, rows_n + 2, width_n, 3 * group), F32),
            pltpu.VMEM((cells, channels), F32),
        ],
        compiler_params=pltpu.CompilerParams(vmem_limit_bytes=24 * 2**20),
        cost_estimate=pl.CostEstimate(
            flops=54 * group * channels * cells, bytes_accessed=54 * group * channels, transcendentals=0
        ),
    )(current, later, kernels)


def tap_kernel(first, f_first, has_sum, *refs):
    ring_ref, parts_ref, *refs = refs
    sum_ref = refs.pop(0) if has_sum else None
    out_ref, cells_ref, sides, feature_ref, total, g_here, f_here = refs[-7:]
    grad_refs = refs[:-7]
    step = pl.program_id(0)
    pieces_n, frames_n, rows_n, own, group = cells_ref.shape
    rings, chans, rows_l, _, width_c = parts_ref.shape
    width_n = pieces_n * own
    held_n = feature_ref.shape[2] // width_n

    @pl.when(step == 0)
    def _():
        g_copies, f_copies = [], []
        for piece in range(pieces_n):
            if len(grad_refs) == 1:
                source, target = grad_refs[0].at[piece], cells_ref.at[piece]
            else:
                source, target = grad_refs[piece], cells_ref.at[lax.rem(ring_ref[0] + pieces_n - piece, pieces_n)]
            g_copies.append(pltpu.make_async_copy(source, target, g_here.at[piece]))
        for ring in range(rings):
            for chan in range(chans):
                f_copies.append(
                    pltpu.make_async_copy(
                        parts_ref.at[ring, chan, :, pl.ds(f_first * width_n, held_n * width_n)],
                        feature_ref.at[chan, pl.ds(ring * rows_l, rows_l)],
                        f_here.at[ring * chans + chan],
                    )
                )
        for index, copy in enumerate(g_copies + f_copies):
            copy.start(priority=index % 2)
        same = lax.broadcasted_iota(jnp.int32, (group, group), 0) == lax.broadcasted_iota(jnp.int32, (group, group), 1)
        identity = jnp.where(same, 1.0, 0.0).astype(BF16)
        source = lax.broadcasted_iota(jnp.int32, (width_n, 2 * width_n), 0)
        target = lax.broadcasted_iota(jnp.int32, (width_n, 2 * width_n), 1)
        moved = (source == target + 1) & (target < width_n) | (source == target - width_n - 1)
        shifts = jnp.where(moved, 1.0, 0.0).astype(BF16)
        edge = jnp.zeros((3 * group, frames_n * width_n), BF16)
        sides[:, 0 : frames_n * width_n] = edge
        sides[:, (rows_n + 1) * frames_n * width_n :] = edge
        for copy in g_copies:
            copy.wait()
        for frame in range(frames_n):
            held = frames_n - (frame // BLOCK_FRAMES + 1) * BLOCK_FRAMES + frame % BLOCK_FRAMES
            joined = [cells_ref[piece, held, row] for row in range(rows_n) for piece in range(pieces_n)]
            turned = lax.dot_general(
                identity,
                jnp.concatenate(joined, axis=0),
                (((1,), (1,)), ((), ())),
                preferred_element_type=F32,
            ).astype(BF16)
            for row in range(rows_n):
                start = ((row + 1) * frames_n + frame) * width_n
                cells = turned[:, row * width_n : (row + 1) * width_n]
                both = jnp.dot(cells, shifts, preferred_element_type=F32).astype(BF16)
                sides[0:group, start : start + width_n] = both[:, :width_n]
                sides[group : 2 * group, start : start + width_n] = cells
                sides[2 * group : 3 * group, start : start + width_n] = both[:, width_n:]
        for copy in f_copies:
            copy.wait()

    offset = 2 - step % 3
    for lag in range(3):

        @pl.when(step // 3 == (2 - lag if has_sum else lag))
        def _():
            skipped = max(0, lag - first)
            span = (frames_n - skipped) * width_n
            low = (first + skipped - lag - f_first) * width_n
            starts = [((row + offset) * frames_n + skipped) * width_n for row in range(rows_n)]
            lefts = [sides[:, pl.ds(pl.multiple_of(start, 128), span)] for start in starts] if has_sum else None
            for chan in range(chans):
                lanes = slice(chan * width_c, (chan + 1) * width_c)
                if has_sum:
                    rights = [feature_ref[chan, row, low : low + span] for row in range(rows_n)]
                    whole = jnp.dot(
                        jnp.concatenate(lefts, axis=1), jnp.concatenate(rights, axis=0), preferred_element_type=F32
                    ).reshape(3, group, width_c)
                    whole = whole + sum_ref[:, :, lanes].astype(F32)
                    out_ref[:, :, lanes] = whole.astype(out_ref.dtype)
                    continue
                for row in range(rows_n):
                    part = jnp.dot(
                        sides[:, pl.ds(pl.multiple_of(starts[row], 128), span)],
                        feature_ref[chan, row, low : low + span],
                        preferred_element_type=F32,
                    )
                    if row == 0:
                        total[...] = part
                    elif row < rows_n - 1:
                        total[...] += part
                    else:
                        whole = (total[...] + part).reshape(3, group, width_c)
                        out_ref[:, :, lanes] = whole.astype(out_ref.dtype)


def kernel_gradient(first, grads, parts, ring_pos, known):
    held = grads[0].shape if len(grads) == 1 else (len(grads),) + grads[0].shape
    pieces_n, frames_n, rows_n, own, group = held
    rings, chans, rows_l, _, width_c = parts.shape
    channels = chans * width_c
    width_n = pieces_n * own
    f_first = max(0, first - 2)
    held_n = first + frames_n - f_first
    far = pl.BlockSpec(memory_space=pltpu.HBM)
    has_sum = known is not None
    out_spec = pl.BlockSpec(
        (3, group, channels), lambda step: ((2 - step // 3) * 3 + step % 3 if has_sum else step, 0, 0)
    )
    return pl.pallas_call(
        functools.partial(tap_kernel, first, f_first, has_sum),
        grid=(9,),
        in_specs=[pl.BlockSpec(memory_space=pltpu.SMEM), far] + [out_spec] * has_sum + [far] * len(grads),
        out_specs=out_spec,
        out_shape=jax.ShapeDtypeStruct((27, group, channels), BF16),
        scratch_shapes=[
            pltpu.VMEM(held, BF16),
            pltpu.VMEM((3 * group, (rows_n + 2) * frames_n * width_n), BF16),
            pltpu.VMEM((chans, rows_n, held_n * width_n, width_c), BF16),
            pltpu.VMEM((3 * group, width_c), F32),
            pltpu.SemaphoreType.DMA((pieces_n,)),
            pltpu.SemaphoreType.DMA((rings * chans,)),
        ],
        compiler_params=pltpu.CompilerParams(vmem_limit_bytes=58 * 2**20),
        cost_estimate=pl.CostEstimate(
            flops=54 * group * channels * rows_n * frames_n * width_n,
            bytes_accessed=6 * 27 * group * channels,
            transcendentals=0,
        ),
    )(*([ring_pos.reshape(1), parts] + [known] * has_sum + grads))


def body(upstream, acts, weights):
    group, frames_all, rows_l, width_n = upstream.shape
    sections, rings, chans = lax.axis_size("section"), lax.axis_size("frame"), lax.axis_size("chan")
    section_pos, ring_pos, chan_pos = lax.axis_index("section"), lax.axis_index("frame"), lax.axis_index("chan")
    rows_n = rows_l * rings
    own = width_n // rings
    halo = sections
    window = own + 2 * halo
    blocks_n = frames_all // BLOCK_FRAMES
    assert blocks_n == sections
    half = frames_all // 2
    ticks = blocks_n + sections - 1
    kernels = weights[0]

    def to_columns(cells):
        wide = jnp.pad(cells, [(0, 0)] * (cells.ndim - 2) + [(halo, halo), (0, 0)])
        pieces = jnp.stack([wide[..., own * i : own * i + window, :] for i in range(rings)])
        pieces = lax.all_to_all(pieces, "frame", 0, 0)
        pieces = jnp.moveaxis(pieces, 0, -4)
        return pieces.reshape(cells.shape[:-3] + (rows_n, window, group))

    mine = lax.dynamic_slice_in_dim(acts[0], chan_pos * group, group, 0)
    top = frames_all - BLOCK_FRAMES
    relayed = lax.dynamic_slice_in_dim(upstream, (blocks_n - 1 - section_pos) * BLOCK_FRAMES, BLOCK_FRAMES, 1)
    pair = to_columns(jnp.stack([relayed, mine[:, top:]]).transpose(0, 2, 3, 4, 1))
    relayed = pair[0]
    rest = to_columns(mine[:, :top].transpose(1, 2, 3, 0))
    stored = [pair[1]]
    for order in range(1, blocks_n):
        first = top - order * BLOCK_FRAMES
        stored.append(rest[first : first + BLOCK_FRAMES])

    shared = group % 128 == 0
    values = (mine if shared else acts[0]).astype(F32)
    feature_part = (values * jax.nn.sigmoid(values)).astype(BF16).transpose(2, 1, 3, 0)
    feature_part = feature_part.reshape(rows_l, frames_all * width_n, -1)

    column = ring_pos * own - halo + jnp.arange(window)
    inside = jnp.logical_and(column >= 0, column < width_n)[None, None, :, None]
    later = jnp.zeros((BLOCK_FRAMES, rows_n, window, group), BF16)
    current = jnp.where(section_pos == 0, relayed, later)
    held, gathered, results = [], [], []
    for tick in range(ticks):
        if tick == 1:
            feature_part, current, stored[-1] = lax.optimization_barrier((feature_part, current, stored[-1]))
            feature_all = lax.all_gather(feature_part, ("frame", "chan") if shared else "frame")
            feature_all = feature_all.reshape(rings, chans if shared else 1, *feature_part.shape)
        if tick == ticks - 2:
            current, feature_all = lax.optimization_barrier((current, feature_all))
        held.append(current[:, :, halo : halo + own])
        if tick in (ticks - 1 - blocks_n // 2, ticks - 1):
            begin = len(gathered) * (blocks_n // 2)
            taken = jnp.stack(held[begin:])
            taken = lax.dynamic_slice_in_dim(taken, section_pos, blocks_n // 2, 0)
            taken, current = lax.optimization_barrier((taken, current))
            taken = taken.reshape(half, rows_n, own, group)
            if not begin:
                gathered.append([lax.all_gather(taken, "frame")])
        partial = back_block(current, later, kernels)
        if tick == ticks - 1:
            partial, gathered[0], taken = lax.optimization_barrier((partial, gathered[0], taken))
            if rings <= 4:
                pairs = [[(i, (i + step) % rings) for i in range(rings)] for step in range(1, rings)]
                gathered.append([taken] + [lax.ppermute(taken, "frame", pair) for pair in pairs])
            else:
                gathered.append([lax.all_gather(taken, "frame")])
        summed = lax.dynamic_slice_in_dim(partial, chan_pos * group, group, 1).astype(F32)
        for step in range(1, chans):
            there = lax.rem(chan_pos + step, chans)
            piece = lax.dynamic_slice_in_dim(partial, there * group, group, 1)
            arrived = lax.ppermute(piece, "chan", [(i, (i + step) % chans) for i in range(chans)])
            summed = summed + arrived.astype(F32)
        known = jnp.stack(stored[: tick + 1])
        place = jnp.clip(tick - section_pos, 0, known.shape[0] - 1)
        slot = lax.dynamic_index_in_dim(known, place, 0, keepdims=False).astype(F32)
        logistic = jax.nn.sigmoid(slot)
        slope = logistic * (1.0 + slot * (1.0 - logistic))
        updated = current.astype(F32) + slope * summed.reshape(current.shape)
        updated = jnp.where(inside, updated, 0.0).astype(BF16)
        results.append(updated[:, :, halo : halo + own])
        later = current
        if tick + 1 < ticks:
            pairs = [(i, i + 1) for i in range(sections - 1) if i <= tick < i + blocks_n]
            if tick + 1 < sections:
                updated = jnp.where(section_pos == tick + 1, relayed, updated)
                pairs.append((tick + 1, 0))
            current = lax.ppermute(updated, "section", pairs)

    if own % 16 and rings > 4:
        gathered = [
            [block.transpose(1, 2, 0, 3, 4).reshape(1, half, rows_n, width_n, group)] for (block,) in gathered
        ]
    kernel_sum = kernel_gradient(half, gathered[0], feature_all, ring_pos, None)

    outs = lax.dynamic_slice_in_dim(jnp.stack(results), section_pos, blocks_n, 0)[::-1]
    outs = outs.reshape(frames_all, rings, rows_l, own, group).transpose(1, 0, 2, 3, 4)
    outs, gathered[1], kernel_sum = lax.optimization_barrier((outs, gathered[1], kernel_sum))
    outs = lax.all_to_all(outs, "frame", 0, 0)
    kernel_total = kernel_gradient(0, gathered[1], feature_all, ring_pos, kernel_sum)
    outs, kernel_total = lax.optimization_barrier((outs, kernel_total))
    outs = outs.transpose(4, 1, 2, 0, 3).reshape(group, frames_all, rows_l, width_n)
    return (outs[None], kernel_total[None])


def solution(mesh):
    placed = (
        P("chan", None, "frame", None),
        P("section", None, None, "frame", None),
        P("section", None, "chan", None),
    )
    return jax.shard_map(
        body,
        mesh=mesh,
        in_specs=placed,
        out_specs=(P("section", "chan", None, "frame", None), P("section", None, "chan", None)),
        check_vma=False,
    )
```

```python
import functools

import jax
import jax.numpy as jnp
from jax import lax
from jax.experimental import pallas as pl
from jax.experimental.pallas import tpu as pltpu
from jax.sharding import PartitionSpec as P

BLOCK_FRAMES = 2
F32 = jnp.float32
BF16 = jnp.bfloat16


def back_kernel(cur_ref, later_ref, w_ref, out_ref, spread, acc):
    frames_n, rows_n, width_n, group = cur_ref.shape
    empty = jnp.zeros((width_n, 3 * group), F32)
    for frame in range(2 * frames_n):
        spread[frame, 0] = empty
        spread[frame, rows_n + 1] = empty
        for row in range(rows_n):
            source = cur_ref[frame, row] if frame < frames_n else later_ref[frame - frames_n, row]
            cells = source.astype(F32)
            spread[frame, row + 1, :, 0:group] = pltpu.roll(cells, width_n - 1, 0)
            spread[frame, row + 1, :, group : 2 * group] = cells
            spread[frame, row + 1, :, 2 * group : 3 * group] = pltpu.roll(cells, 1, 0)
    for step in range(9):
        lag, offset = step // 3, 2 - step % 3
        taken = spread[lag : lag + frames_n, offset : offset + rows_n]
        taken = taken.reshape(frames_n * rows_n * width_n, 3 * group).astype(BF16)
        part = jnp.dot(
            taken, w_ref[3 * step : 3 * step + 3].reshape(3 * group, -1), preferred_element_type=F32
        )
        if step == 0:
            acc[...] = part
        elif step < 8:
            acc[...] += part
        else:
            out_ref[...] = (acc[...] + part).astype(BF16)


def back_block(current, later, kernels):
    frames_n, rows_n, width_n, group = current.shape
    channels = kernels.shape[2]
    cells = frames_n * rows_n * width_n
    held = pl.BlockSpec(memory_space=pltpu.VMEM)
    return pl.pallas_call(
        back_kernel,
        in_specs=[held, held, held],
        out_specs=held,
        out_shape=jax.ShapeDtypeStruct((cells, channels), BF16),
        scratch_shapes=[
            pltpu.VMEM((2 * frames_n, rows_n + 2, width_n, 3 * group), F32),
            pltpu.VMEM((cells, channels), F32),
        ],
        compiler_params=pltpu.CompilerParams(vmem_limit_bytes=24 * 2**20),
        cost_estimate=pl.CostEstimate(
            flops=54 * group * channels * cells, bytes_accessed=54 * group * channels, transcendentals=0
        ),
    )(current, later, kernels)


def tap_kernel(first, f_first, has_sum, *refs):
    ring_ref, parts_ref, *refs = refs
    sum_ref = refs.pop(0) if has_sum else None
    out_ref, cells_ref, sides, feature_ref, total, g_here, f_here = refs[-7:]
    grad_refs = refs[:-7]
    step = pl.program_id(0)
    pieces_n, frames_n, rows_n, own, group = cells_ref.shape
    rings, chans, rows_l, _, width_c = parts_ref.shape
    width_n = pieces_n * own
    held_n = feature_ref.shape[2] // width_n

    lags = (2, 1, 0) if has_sum else (0, 1, 2)

    def feature_copies(phase):
        needed = []
        for lag in lags[: phase + 1]:
            skipped = max(0, lag - first)
            low = first + skipped - lag - f_first
            needed.append(set(range(low, low + frames_n - skipped)))
        fresh = sorted(needed[-1].difference(*needed[:-1]))
        begin, cells = fresh[0] * width_n, len(fresh) * width_n
        return [
            pltpu.make_async_copy(
                parts_ref.at[ring, chan, :, pl.ds(f_first * width_n + begin, cells)],
                feature_ref.at[chan, pl.ds(ring * rows_l, rows_l), pl.ds(begin, cells)],
                f_here.at[(phase * rings + ring) * chans + chan],
            )
            for ring in range(rings)
            for chan in range(chans)
        ]

    @pl.when(step == 0)
    def _():
        g_copies = []
        for piece in range(pieces_n):
            if len(grad_refs) == 1:
                source, target = grad_refs[0].at[piece], cells_ref.at[piece]
            else:
                source, target = grad_refs[piece], cells_ref.at[lax.rem(ring_ref[0] + pieces_n - piece, pieces_n)]
            g_copies.append(pltpu.make_async_copy(source, target, g_here.at[piece]))
        for copy in g_copies:
            copy.start()
        for phase in range(3):
            for copy in feature_copies(phase):
                copy.start(priority=1)
        same = lax.broadcasted_iota(jnp.int32, (group, group), 0) == lax.broadcasted_iota(jnp.int32, (group, group), 1)
        identity = jnp.where(same, 1.0, 0.0).astype(BF16)
        source = lax.broadcasted_iota(jnp.int32, (width_n, 2 * width_n), 0)
        target = lax.broadcasted_iota(jnp.int32, (width_n, 2 * width_n), 1)
        moved = (source == target + 1) & (target < width_n) | (source == target - width_n - 1)
        shifts = jnp.where(moved, 1.0, 0.0).astype(BF16)
        edge = jnp.zeros((3 * group, frames_n * width_n), BF16)
        sides[:, 0 : frames_n * width_n] = edge
        sides[:, (rows_n + 1) * frames_n * width_n :] = edge
        for copy in g_copies:
            copy.wait()
        for frame in range(frames_n):
            held = frames_n - (frame // BLOCK_FRAMES + 1) * BLOCK_FRAMES + frame % BLOCK_FRAMES
            joined = [cells_ref[piece, held, row] for row in range(rows_n) for piece in range(pieces_n)]
            turned = lax.dot_general(
                identity,
                jnp.concatenate(joined, axis=0),
                (((1,), (1,)), ((), ())),
                preferred_element_type=F32,
            ).astype(BF16)
            for row in range(rows_n):
                start = ((row + 1) * frames_n + frame) * width_n
                cells = turned[:, row * width_n : (row + 1) * width_n]
                both = jnp.dot(cells, shifts, preferred_element_type=F32).astype(BF16)
                sides[0:group, start : start + width_n] = both[:, :width_n]
                sides[group : 2 * group, start : start + width_n] = cells
                sides[2 * group : 3 * group, start : start + width_n] = both[:, width_n:]

    for phase in range(3):

        @pl.when(step == 3 * phase)
        def _():
            for copy in feature_copies(phase):
                copy.wait()

    offset = 2 - step % 3
    for lag in range(3):

        @pl.when(step // 3 == lags.index(lag))
        def _():
            skipped = max(0, lag - first)
            span = (frames_n - skipped) * width_n
            low = (first + skipped - lag - f_first) * width_n
            starts = [((row + offset) * frames_n + skipped) * width_n for row in range(rows_n)]
            lefts = [sides[:, pl.ds(pl.multiple_of(start, 128), span)] for start in starts] if has_sum else None
            for chan in range(chans):
                lanes = slice(chan * width_c, (chan + 1) * width_c)
                if has_sum:
                    rights = [feature_ref[chan, row, low : low + span] for row in range(rows_n)]
                    whole = jnp.dot(
                        jnp.concatenate(lefts, axis=1), jnp.concatenate(rights, axis=0), preferred_element_type=F32
                    ).reshape(3, group, width_c)
                    whole = whole + sum_ref[:, :, lanes].astype(F32)
                    out_ref[:, :, lanes] = whole.astype(out_ref.dtype)
                    continue
                for row in range(rows_n):
                    part = jnp.dot(
                        sides[:, pl.ds(pl.multiple_of(starts[row], 128), span)],
                        feature_ref[chan, row, low : low + span],
                        preferred_element_type=F32,
                    )
                    if row == 0:
                        total[...] = part
                    elif row < rows_n - 1:
                        total[...] += part
                    else:
                        whole = (total[...] + part).reshape(3, group, width_c)
                        out_ref[:, :, lanes] = whole.astype(out_ref.dtype)


def kernel_gradient(first, grads, parts, ring_pos, known):
    held = grads[0].shape if len(grads) == 1 else (len(grads),) + grads[0].shape
    pieces_n, frames_n, rows_n, own, group = held
    rings, chans, rows_l, _, width_c = parts.shape
    channels = chans * width_c
    width_n = pieces_n * own
    f_first = max(0, first - 2)
    held_n = first + frames_n - f_first
    far = pl.BlockSpec(memory_space=pltpu.HBM)
    has_sum = known is not None
    out_spec = pl.BlockSpec(
        (3, group, channels), lambda step: ((2 - step // 3) * 3 + step % 3 if has_sum else step, 0, 0)
    )
    return pl.pallas_call(
        functools.partial(tap_kernel, first, f_first, has_sum),
        grid=(9,),
        in_specs=[pl.BlockSpec(memory_space=pltpu.SMEM), far] + [out_spec] * has_sum + [far] * len(grads),
        out_specs=out_spec,
        out_shape=jax.ShapeDtypeStruct((27, group, channels), BF16),
        scratch_shapes=[
            pltpu.VMEM(held, BF16),
            pltpu.VMEM((3 * group, (rows_n + 2) * frames_n * width_n), BF16),
            pltpu.VMEM((chans, rows_n, held_n * width_n, width_c), BF16),
            pltpu.VMEM((3 * group, width_c), F32),
            pltpu.SemaphoreType.DMA((pieces_n,)),
            pltpu.SemaphoreType.DMA((3 * rings * chans,)),
        ],
        compiler_params=pltpu.CompilerParams(vmem_limit_bytes=58 * 2**20),
        cost_estimate=pl.CostEstimate(
            flops=54 * group * channels * rows_n * frames_n * width_n,
            bytes_accessed=6 * 27 * group * channels,
            transcendentals=0,
        ),
    )(*([ring_pos.reshape(1), parts] + [known] * has_sum + grads))


def body(upstream, acts, weights):
    group, frames_all, rows_l, width_n = upstream.shape
    sections, rings, chans = lax.axis_size("section"), lax.axis_size("frame"), lax.axis_size("chan")
    section_pos, ring_pos, chan_pos = lax.axis_index("section"), lax.axis_index("frame"), lax.axis_index("chan")
    rows_n = rows_l * rings
    own = width_n // rings
    halo = sections
    window = own + 2 * halo
    blocks_n = frames_all // BLOCK_FRAMES
    assert blocks_n == sections
    half = frames_all // 2
    ticks = blocks_n + sections - 1
    kernels = weights[0]

    def to_columns(cells):
        wide = jnp.pad(cells, [(0, 0)] * (cells.ndim - 2) + [(halo, halo), (0, 0)])
        pieces = jnp.stack([wide[..., own * i : own * i + window, :] for i in range(rings)])
        pieces = lax.all_to_all(pieces, "frame", 0, 0)
        pieces = jnp.moveaxis(pieces, 0, -4)
        return pieces.reshape(cells.shape[:-3] + (rows_n, window, group))

    mine = lax.dynamic_slice_in_dim(acts[0], chan_pos * group, group, 0)
    top = frames_all - BLOCK_FRAMES
    relayed = lax.dynamic_slice_in_dim(upstream, (blocks_n - 1 - section_pos) * BLOCK_FRAMES, BLOCK_FRAMES, 1)
    pair = to_columns(jnp.stack([relayed, mine[:, top:]]).transpose(0, 2, 3, 4, 1))
    relayed = pair[0]
    rest = to_columns(mine[:, :top].transpose(1, 2, 3, 0))
    stored = [pair[1]]
    for order in range(1, blocks_n):
        first = top - order * BLOCK_FRAMES
        stored.append(rest[first : first + BLOCK_FRAMES])

    shared = group % 128 == 0
    values = (mine if shared else acts[0]).astype(F32)
    feature_part = (values * jax.nn.sigmoid(values)).astype(BF16).transpose(2, 1, 3, 0)
    feature_part = feature_part.reshape(rows_l, frames_all * width_n, -1)

    column = ring_pos * own - halo + jnp.arange(window)
    inside = jnp.logical_and(column >= 0, column < width_n)[None, None, :, None]
    later = jnp.zeros((BLOCK_FRAMES, rows_n, window, group), BF16)
    current = jnp.where(section_pos == 0, relayed, later)
    held, gathered, results = [], [], []
    for tick in range(ticks):
        if tick == 1:
            feature_part, current, stored[-1] = lax.optimization_barrier((feature_part, current, stored[-1]))
            feature_all = lax.all_gather(feature_part, ("frame", "chan") if shared else "frame")
            feature_all = feature_all.reshape(rings, chans if shared else 1, *feature_part.shape)
        if tick == ticks - 2:
            current, feature_all = lax.optimization_barrier((current, feature_all))
        held.append(current[:, :, halo : halo + own])
        if tick in (ticks - 1 - blocks_n // 2, ticks - 1):
            begin = len(gathered) * (blocks_n // 2)
            taken = jnp.stack(held[begin:])
            taken = lax.dynamic_slice_in_dim(taken, section_pos, blocks_n // 2, 0)
            taken, current = lax.optimization_barrier((taken, current))
            taken = taken.reshape(half, rows_n, own, group)
            if not begin:
                gathered.append([lax.all_gather(taken, "frame")])
        partial = back_block(current, later, kernels)
        if tick == ticks - 1:
            partial, gathered[0], taken = lax.optimization_barrier((partial, gathered[0], taken))
            if rings <= 4:
                pairs = [[(i, (i + step) % rings) for i in range(rings)] for step in range(1, rings)]
                gathered.append([taken] + [lax.ppermute(taken, "frame", pair) for pair in pairs])
            else:
                gathered.append([lax.all_gather(taken, "frame")])
        summed = lax.dynamic_slice_in_dim(partial, chan_pos * group, group, 1).astype(F32)
        for step in range(1, chans):
            there = lax.rem(chan_pos + step, chans)
            piece = lax.dynamic_slice_in_dim(partial, there * group, group, 1)
            arrived = lax.ppermute(piece, "chan", [(i, (i + step) % chans) for i in range(chans)])
            summed = summed + arrived.astype(F32)
        known = jnp.stack(stored[: tick + 1])
        place = jnp.clip(tick - section_pos, 0, known.shape[0] - 1)
        slot = lax.dynamic_index_in_dim(known, place, 0, keepdims=False).astype(F32)
        logistic = jax.nn.sigmoid(slot)
        slope = logistic * (1.0 + slot * (1.0 - logistic))
        updated = current.astype(F32) + slope * summed.reshape(current.shape)
        updated = jnp.where(inside, updated, 0.0).astype(BF16)
        results.append(updated[:, :, halo : halo + own])
        later = current
        if tick + 1 < ticks:
            pairs = [(i, i + 1) for i in range(sections - 1) if i <= tick < i + blocks_n]
            if tick + 1 < sections:
                updated = jnp.where(section_pos == tick + 1, relayed, updated)
                pairs.append((tick + 1, 0))
            current = lax.ppermute(updated, "section", pairs)

    if own % 16 and rings > 4:
        gathered = [
            [block.transpose(1, 2, 0, 3, 4).reshape(1, half, rows_n, width_n, group)] for (block,) in gathered
        ]
    kernel_sum = kernel_gradient(half, gathered[0], feature_all, ring_pos, None)

    outs = lax.dynamic_slice_in_dim(jnp.stack(results), section_pos, blocks_n, 0)[::-1]
    outs = outs.reshape(frames_all, rings, rows_l, own, group).transpose(1, 0, 2, 3, 4)
    outs, gathered[1], kernel_sum = lax.optimization_barrier((outs, gathered[1], kernel_sum))
    outs = lax.all_to_all(outs, "frame", 0, 0)
    kernel_total = kernel_gradient(0, gathered[1], feature_all, ring_pos, kernel_sum)
    outs, kernel_total = lax.optimization_barrier((outs, kernel_total))
    outs = outs.transpose(4, 1, 2, 0, 3).reshape(group, frames_all, rows_l, width_n)
    return (outs[None], kernel_total[None])


def solution(mesh):
    placed = (
        P("chan", None, "frame", None),
        P("section", None, None, "frame", None),
        P("section", None, "chan", None),
    )
    return jax.shard_map(
        body,
        mesh=mesh,
        in_specs=placed,
        out_specs=(P("section", "chan", None, "frame", None), P("section", None, "chan", None)),
        check_vma=False,
    )
```
